32 devices in a mesh: batch: 16 (over z, x, core), tp: 2 (over y).
Axes of the slice: x: 2, y: 2, z: 4, core: 2. Of those that a mesh axis runs over, the one named last changes fastest.
Arguments:
- inputs: bfloat16 [24576, 768], P(('batch', 'tp')), may hold values from -6 to 6
- cotangent: bfloat16 [24576, 768], P(('batch', 'tp')), may hold values from -6 to 6
- zinc_lengths: int32 [128], P(('batch', 'tp')), may hold values from 8 to 64, as said below
- pubchem_lengths: int32 [64], P(('batch', 'tp')), may hold values from 16 to 256, as said below
- feature_stack: float32 [8, 12, 32, 64], replicated, may hold values from -6 to 6
- train_step: int32 [1], replicated, may hold values from 0 to 999999
- redraw_interval: int32 [1], replicated, may hold values from 1 to 4999
- attn_gain: float32 [768], replicated, may hold values from 0.5 to 1.5
- attn_shift: float32 [768], replicated, may hold values from -1 to 1
- query_weight: bfloat16 [768, 768], replicated, may hold values from -0.21875 to 0.21875
- query_bias: float32 [768], replicated, may hold values from -1 to 1
- key_weight: bfloat16 [768, 768], replicated, may hold values from -0.21875 to 0.21875
- key_bias: float32 [768], replicated, may hold values from -1 to 1
- value_weight: bfloat16 [768, 768], replicated, may hold values from -0.21875 to 0.21875
- value_bias: float32 [768], replicated, may hold values from -1 to 1
- output_weight: bfloat16 [768, 768], replicated, may hold values from -0.625 to 0.625
- output_bias: float32 [768], replicated, may hold values from -1 to 1
- ffn_gain: float32 [768], replicated, may hold values from 0.5 to 1.5
- ffn_shift: float32 [768], replicated, may hold values from -1 to 1
- hidden_weight: bfloat16 [768, 3072], P(None, 'tp'), may hold values from -0.21875 to 0.21875
- hidden_bias: bfloat16 [3072], P('tp'), may hold values from -1 to 1
- return_weight: bfloat16 [3072, 768], P('tp'), may hold values from -0.109375 to 0.109375
- return_bias: float32 [768], replicated, may hold values from -1 to 1
Outputs:
- layer_out: bfloat16 [24576, 768], P(('batch', 'tp'))
- input_grad: bfloat16 [24576, 768], P(('batch', 'tp'))
- grad_attn_gain: float32 [768], replicated
- grad_attn_shift: float32 [768], replicated
- grad_query_weight: float32 [768, 768], replicated
- grad_query_bias: float32 [768], replicated
- grad_key_weight: float32 [768, 768], replicated
- grad_key_bias: float32 [768], replicated
- grad_value_weight: float32 [768, 768], replicated
- grad_value_bias: float32 [768], replicated
- grad_output_weight: float32 [768, 768], replicated
- grad_output_bias: float32 [768], replicated
- grad_ffn_gain: float32 [768], replicated
- grad_ffn_shift: float32 [768], replicated
- grad_hidden_weight: float32 [768, 3072], P(None, 'tp')
- grad_hidden_bias: float32 [3072], P('tp')
- grad_return_weight: float32 [3072, 768], P('tp')
- grad_return_bias: float32 [768], replicated
The draws below stay inside these ranges and needn't reach their ends.
Inputs may be any that keep to these rules, and one draw needn't show every extreme that they name: `zinc_lengths`: each ZINC molecule has between 8 and 64 live slots. `pubchem_lengths`: each PubChem molecule has between 16 and 256 live slots.
All inputs are finite; a program needn't handle non-finite values.
Results may differ from the reference program's by a relative error of at most 0.018.
Values may be sent and summed in bfloat16 or wider, within the bound.
No kernel may reach another device: no remote copies, remote signals or barrier semaphores. Data moves between devices by JAX's collectives and lax.ppermute only.
A program may use at most 256 MiB of HBM per device.

```python
import math
import jax
import jax.numpy as jnp
from jax import lax

D = 768
H = 12
M = 32
FF = 3072
HD = 64
STACK = 8
ZPAD = 64
PPAD = 256
ZM_DEV = 4
PM_DEV = 2
R_DEV = 768
ZMOLS = 128
PMOLS = 64
ROWS = 24576
DEVICES = 32


def draw_zinc_lengths(key, part):
    key = jax.random.fold_in(key, 11)
    raw = jax.random.randint(key, (ZMOLS,), ZPAD // 8, ZPAD + ZPAD // 4 + 1)
    return jnp.minimum(raw, ZPAD).astype(jnp.int32)


def draw_pubchem_lengths(key, part):
    key = jax.random.fold_in(key, 23)
    raw = jax.random.randint(key, (PMOLS,), PPAD // 16, PPAD + PPAD // 4 + 1)
    return jnp.minimum(raw, PPAD).astype(jnp.int32)


def block_levels(key, shape, shards, least, largest):
    def one(axis_at, shards_of):
        steps = jax.random.uniform(jax.random.fold_in(jax.random.fold_in(key, 6), axis_at), (shards_of,), jnp.float32, least / len(shards), largest / len(shards))
        return jnp.repeat(jnp.exp(steps), shape[axis_at] // shards_of).reshape((-1,) + (1,) * (len(shape) - axis_at - 1))

    factor_of = one(*shards[0])
    for cut in shards[1:]:
        factor_of = factor_of * one(*cut)
    return factor_of


def centred(own_key, dims, scale, limit, cuts=(), kind=jnp.bfloat16):
    level = block_levels(own_key, dims, cuts, -0.22, 0.18) if cuts else 1.0
    array = jax.random.normal(own_key, dims, jnp.float32) * scale * level
    return jnp.minimum(jnp.maximum(array, -limit), limit).astype(kind)


def setup_inputs(seed: int = 0) -> dict:
    key_list = jax.random.split(jax.random.key(seed), 24)
    return {
        "inputs": centred(key_list[0], (ROWS, D), 1.0, 6.0, ((0, 32),)),
        "cotangent": centred(key_list[1], (ROWS, D), 1.0, 6.0, ((0, 32),)),
        "zinc_lengths": draw_zinc_lengths(jax.random.fold_in(key_list[23], 71), 0),
        "pubchem_lengths": draw_pubchem_lengths(jax.random.fold_in(key_list[23], 71), 0),
        "feature_stack": centred(key_list[4], (STACK, H, M, HD), 1.0, 6.0, (), jnp.float32),
        "train_step": jax.random.randint(key_list[5], (1,), 0, 1000000).astype(jnp.int32),
        "redraw_interval": jax.random.randint(key_list[6], (1,), 1, 5000).astype(jnp.int32),
        "attn_gain": jnp.clip(1.0 + 0.1 * jax.random.normal(key_list[7], (D,), jnp.float32), 0.5, 1.5),
        "attn_shift": centred(key_list[8], (D,), 0.2, 1.0, (), jnp.float32),
        "query_weight": centred(key_list[9], (D, D), D ** -0.5, 0.21875),
        "query_bias": centred(key_list[10], (D,), 0.2, 1.0, (), jnp.float32),
        "key_weight": centred(key_list[11], (D, D), D ** -0.5, 0.21875),
        "key_bias": centred(key_list[12], (D,), 0.2, 1.0, (), jnp.float32),
        "value_weight": centred(key_list[13], (D, D), D ** -0.5, 0.21875),
        "value_bias": centred(key_list[14], (D,), 0.2, 1.0, (), jnp.float32),
        "output_weight": centred(key_list[15], (D, D), (D // 8) ** -0.5, 0.625),
        "output_bias": centred(key_list[16], (D,), 0.2, 1.0, (), jnp.float32),
        "ffn_gain": jnp.clip(1.0 + 0.1 * jax.random.normal(key_list[17], (D,), jnp.float32), 0.5, 1.5),
        "ffn_shift": centred(key_list[18], (D,), 0.2, 1.0, (), jnp.float32),
        "hidden_weight": centred(key_list[19], (D, FF), D ** -0.5, 0.21875, ((1, 2),)),
        "hidden_bias": centred(key_list[20], (FF,), 0.2, 1.0, ((0, 2),)),
        "return_weight": centred(key_list[21], (FF, D), FF ** -0.5, 0.109375, ((0, 2),)),
        "return_bias": centred(key_list[22], (D,), 0.2, 1.0, (), jnp.float32),
    }


highest_precision = lax.Precision.HIGHEST

@jax.custom_vjp
def low(v):
    return lax.optimization_barrier(v.astype(jnp.bfloat16)).astype(jnp.float32)

@jax.custom_vjp
def low_back(v):
    return v

def low_keep(v):
    return (low(v), None)

def low_pass(kept, grad):
    return (grad,)

def back_keep(v):
    return (v, None)

def back_low(kept, grad):
    return (low(grad),)
low.defvjp(low_keep, low_pass)
low_back.defvjp(back_keep, back_low)

def norm_rows(values, gain, shift):
    center = values - lax.optimization_barrier(jnp.mean(values, axis=-1, keepdims=True))
    spread = lax.optimization_barrier(jnp.mean(center * center, axis=-1, keepdims=True))
    return center * lax.rsqrt(spread + 1e-05) * gain + shift

def rotary_tables(length, width):
    half = width // 2
    place = jnp.arange(length, dtype=jnp.float32)
    rates = jnp.exp(jnp.arange(half, dtype=jnp.float32) * (-2.0 * math.log(10000.0) / width))
    angles = place[:, None] * rates[None, :]
    return (jnp.cos(angles)[:, None, :], jnp.sin(angles)[:, None, :])

def rotate(values, cosine, sine):
    half = values.shape[-1] // 2
    first = values[..., :half]
    second = values[..., half:]
    return jnp.concatenate([first * cosine - second * sine, second * cosine + first * sine], axis=-1)

def positive_features(values, feature_projection):
    scaled_rows = values * values.shape[-1] ** (-0.25)
    inner_product = jnp.einsum('ijrc,rnc->ijrn', scaled_rows, feature_projection, precision=highest_precision)
    energy = 0.5 * lax.optimization_barrier(jnp.sum(scaled_rows * scaled_rows, axis=-1, keepdims=True))
    return jnp.exp(inner_product - energy) * feature_projection.shape[1] ** (-0.5)

def molecule_attention(query, key, value, lengths, feature_projection):
    length = query.shape[1]
    cosine, sine = rotary_tables(length, query.shape[-1])
    query_maps = positive_features(rotate(query, cosine, sine), feature_projection)
    key_maps = positive_features(rotate(key, cosine, sine), feature_projection)
    live = (jnp.arange(length, dtype=jnp.int32)[None, :] < lengths[:, None]).astype(jnp.float32)
    key_maps = key_maps * live[:, :, None, None]
    state = jnp.einsum('gphm,gphd->ghmd', key_maps, value, precision=highest_precision)
    total = lax.optimization_barrier(jnp.sum(key_maps, axis=1))
    weighted = jnp.einsum('gphm,ghmd->gphd', query_maps, state, precision=highest_precision)
    normaliser = jnp.einsum('gphm,ghm->gph', query_maps, total, precision=highest_precision)
    return weighted / normaliser[..., None]

def attention_core(query, key, value, zinc_lengths, pubchem_lengths, feature_projection):
    heads = feature_projection.shape[0]
    width = query.shape[1] // heads
    zinc_rows = zinc_lengths.shape[0] * ZPAD
    all_rows = query.shape[0]
    zinc_part = molecule_attention(query[:zinc_rows].reshape(zinc_lengths.shape[0], ZPAD, heads, width), key[:zinc_rows].reshape(zinc_lengths.shape[0], ZPAD, heads, width), value[:zinc_rows].reshape(zinc_lengths.shape[0], ZPAD, heads, width), zinc_lengths, feature_projection)
    pubchem_part = molecule_attention(query[zinc_rows:].reshape(pubchem_lengths.shape[0], PPAD, heads, width), key[zinc_rows:].reshape(pubchem_lengths.shape[0], PPAD, heads, width), value[zinc_rows:].reshape(pubchem_lengths.shape[0], PPAD, heads, width), pubchem_lengths, feature_projection)
    return jnp.concatenate([zinc_part.reshape(zinc_rows, heads * width), pubchem_part.reshape(all_rows - zinc_rows, heads * width)], axis=0)

def product(left, right):
    return jnp.dot(left, right, precision=highest_precision)

def layer_block(params, block, zinc_lengths, pubchem_lengths, feature_projection):
    attn_gain, attn_shift, query_weight, query_bias, key_weight, key_bias, value_weight, value_bias, output_weight, output_bias, ffn_gain, ffn_shift, hidden_weight, hidden_bias, return_weight, return_bias = params
    normed_one = low(norm_rows(block, attn_gain, attn_shift))
    query = low_back(product(normed_one, query_weight) + query_bias)
    key = low_back(product(normed_one, key_weight) + key_bias)
    value = low_back(product(normed_one, value_weight) + value_bias)
    attended = low(attention_core(query, key, value, zinc_lengths, pubchem_lengths, feature_projection))
    branch = low_back(product(attended, output_weight) + output_bias)
    middle = block + branch
    normed_two = low(norm_rows(middle, ffn_gain, ffn_shift))
    hidden = low_back(product(normed_two, hidden_weight) + hidden_bias)
    active = low(jax.nn.gelu(hidden, approximate=False))
    returned = low_back(product(active, return_weight))
    return middle + returned + return_bias

def reference(inputs, cotangent, zinc_lengths, pubchem_lengths, feature_stack, train_step, redraw_interval, attn_gain, attn_shift, query_weight, query_bias, key_weight, key_bias, value_weight, value_bias, output_weight, output_bias, ffn_gain, ffn_shift, hidden_weight, hidden_bias, return_weight, return_bias):
    pick = (train_step[0] // redraw_interval[0] % STACK).astype(jnp.int32)
    feature_projection = lax.dynamic_index_in_dim(feature_stack.astype(jnp.float32), pick, 0, keepdims=False)
    params = tuple((weight.astype(jnp.float32) for weight in (attn_gain, attn_shift, query_weight, query_bias, key_weight, key_bias, value_weight, value_bias, output_weight, output_bias, ffn_gain, ffn_shift, hidden_weight, hidden_bias, return_weight, return_bias)))
    blocks = inputs.astype(jnp.float32).reshape(DEVICES, R_DEV, D)
    zinc_blocks = zinc_lengths.reshape(DEVICES, ZM_DEV)
    pubchem_blocks = pubchem_lengths.reshape(DEVICES, PM_DEV)

    def forward(weights, rows):

        def one_block(items):
            return jax.checkpoint(layer_block)(weights, items[0], items[1], items[2], feature_projection)
        return lax.map(one_block, (rows, zinc_blocks, pubchem_blocks))
    result, pullback = jax.vjp(forward, params, blocks)
    grads, rows_grad = pullback(cotangent.astype(jnp.float32).reshape(DEVICES, R_DEV, D))
    return (result.reshape(ROWS, D).astype(jnp.bfloat16), rows_grad.reshape(ROWS, D).astype(jnp.bfloat16), grads[0], grads[1], grads[2], grads[3], grads[4], grads[5], grads[6], grads[7], grads[8], grads[9], grads[10], grads[11], grads[12], grads[13], grads[14], grads[15])
```

```python
import math
import functools
import jax, jax.numpy as jnp, numpy as np
from jax import lax
from jax.experimental import pallas as pl
from jax.experimental.pallas import tpu as pltpu
from jax.sharding import PartitionSpec as P

ZPAD = 64
PPAD = 256
F32 = jnp.float32
BF = jnp.bfloat16
VM = pltpu.VMEM
GROUP = 4

def dot(a, b):
    return jnp.dot(a, b, preferred_element_type=F32)

def dot_t(a, b):
    return lax.dot_general(a, b, (((1,), (1,)), ((), ())), preferred_element_type=F32)

def dot_c(a, b):
    return lax.dot_general(a, b, (((0,), (0,)), ((), ())), preferred_element_type=F32)

def split(v):
    hi = v.astype(BF)
    return hi, (v - hi.astype(F32)).astype(BF)

def norm_parts(values):
    center = values - jnp.mean(values, axis=-1, keepdims=True)
    rate = lax.rsqrt(jnp.mean(center * center, axis=-1, keepdims=True) + 1e-05)
    return center * rate, rate

def row(ref):
    return ref[...].reshape(1, -1)

def block_mask(width):
    f = lax.broadcasted_iota(jnp.int32, (128, width), 0) // 32
    c = lax.broadcasted_iota(jnp.int32, (128, width), 1) % 256 // 64
    return f == c

def molecules(zm, pm):
    return [(i * ZPAD, ZPAD) for i in range(zm)] + [(zm * ZPAD + i * PPAD, PPAD) for i in range(pm)]

def attend_fwd_kernel(zm, pm, zlen, plen, x, gain, shift, wq, wk, wv, bq, bk, bv, wo, bo, gain2, shift2,
                      proj_hi, proj_lo, energy, cos, sin,
                      n1_o, n1t_o, xq_o, xk_o, v_o, fq_o, fk_o, state_o, att_o, attt_o, middle_o, n2_o, n2t_o):
    mols = molecules(zm, pm)
    rows = x.shape[0]
    blocks = []
    start = 0
    while start < rows:
        blocks.append([(i, r, n) for i, (r, n) in enumerate(mols) if start <= r < start + PPAD])
        start += PPAD
    normed, _ = norm_parts(x[...].astype(F32))
    n1_all = (normed * row(gain) + row(shift)).astype(BF)
    n1_o[...] = n1_all
    n1t_o[...] = n1_all.T
    groups = wq.shape[1] // 256
    keep = block_mask(512)
    ones = jnp.ones((PPAD, 256), BF)
    for b, mem in enumerate(blocks):
        rs = slice(b * PPAD, (b + 1) * PPAD)
        n1 = n1_o[rs, :]
        cosb = jnp.concatenate([cos[:n, :] for _, _, n in mem], axis=0)
        sinb = jnp.concatenate([sin[:n, :] for _, _, n in mem], axis=0)
        cosb = jnp.concatenate([cosb, cosb], axis=1)
        sinb = jnp.concatenate([sinb, sinb], axis=1)
        live = []
        for i, r, n in mem:
            limit = zlen[i] if i < zm else plen[i - zm]
            live.append((lax.broadcasted_iota(jnp.int32, (n, 128), 0) < limit).astype(F32))
        live = jnp.concatenate(live, axis=0)
        for g in range(groups):
            cs = slice(g * 256, (g + 1) * 256)
            fs = slice(g * 128, (g + 1) * 128)

            def features(w, bias, x_o):
                v = dot(n1, w[:, cs]) + row(bias)[:, cs]
                x_o[rs, cs] = v.astype(BF)
                ch, cl = split(v * cosb)
                sh, sl = split(v * sinb)
                eh, el = split(v * v)
                ph, plo = proj_hi[g], proj_lo[g]
                e = energy[...]
                inner = (dot_t(ch, ph[:, :256]) + dot_t(sh, ph[:, 256:]) + dot_t(cl, ph[:, :256]) + dot_t(sl, ph[:, 256:])
                         + dot_t(ch, plo[:, :256]) + dot_t(sh, plo[:, 256:]) - dot_t(eh, e) - dot_t(el, e))
                return jnp.exp(inner) * (32 ** -0.5)

            fq = features(wq, bq, xq_o).astype(BF)
            fk = (features(wk, bk, xk_o) * live).astype(BF)
            fq_o[rs, fs] = fq
            fk_o[rs, fs] = fk
            v = (dot(n1, wv[:, cs]) + row(bv)[:, cs]).astype(BF)
            v_o[rs, cs] = v
            for i, r, n in mem:
                off = r - b * PPAD
                ms = slice(off, off + n)
                vo = jnp.concatenate([v[ms], ones[:n]], axis=1)
                state = jnp.where(keep, dot_c(fk[ms], vo), 0.0).astype(BF)
                state_o[i, g] = state
                nd = dot(fq[ms], state)
                att = (nd[:, :256] / nd[:, 256:]).astype(BF)
                att_o[slice(r, r + n), cs] = att
        middle = x[rs, :].astype(F32) + (dot(att_o[rs, :], wo[...]) + row(bo))
        middle_o[rs, :] = middle
        normed, _ = norm_parts(middle)
        n2_o[rs, :] = (normed * row(gain2) + row(shift2)).astype(BF)
    attt_o[...] = att_o[...].T
    n2t_o[...] = n2_o[...].T

def rotary_const():
    place = np.arange(PPAD, dtype=np.float64)
    rates = np.exp(np.arange(32, dtype=np.float64) * (-2.0 * math.log(10000.0) / 64))
    ang = place[:, None] * rates[None, :]
    return (np.tile(np.cos(ang), (1, 4)).astype(np.float32), np.tile(np.sin(ang), (1, 4)).astype(np.float32))

def projection_blocks(fp):
    heads, m, hd = fp.shape
    s = hd ** -0.25
    turned = jnp.concatenate([fp[..., hd // 2:], -fp[..., :hd // 2]], axis=-1)
    eye = jnp.eye(GROUP, dtype=F32)
    def blocks(p):
        p = (p * s).reshape(heads // GROUP, GROUP, m, 1, hd) * eye[None, :, None, :, None]
        return p.reshape(heads // GROUP, GROUP * m, GROUP * hd)
    both = jnp.concatenate([blocks(fp), blocks(turned)], axis=-1)
    return split(both)

def energy_const():
    f = np.arange(128)[:, None] // 32
    c = np.arange(256)[None, :] // 64
    return ((f == c) / 16.0).astype(jnp.bfloat16)

def attend_fwd(x, zlen, plen, gain, shift, wq, bq, wk, bk, wv, bv, wo, bo, gain2, shift2, proj_hi, proj_lo, cos, sin):
    rows, d = x.shape
    zm, pm = zlen.shape[0], plen.shape[0]
    groups = d // 256
    S = jax.ShapeDtypeStruct
    vm = pl.BlockSpec(memory_space=VM)
    sm = pl.BlockSpec(memory_space=pltpu.SMEM)
    outs = (S((rows, d), BF), S((d, rows), BF), S((rows, d), BF), S((rows, d), BF), S((rows, d), BF),
            S((rows, d // 2), BF), S((rows, d // 2), BF), S((zm + pm, groups, 128, 512), BF),
            S((rows, d), BF), S((d, rows), BF), S((rows, d), F32), S((rows, d), BF), S((d, rows), BF))
    return pl.pallas_call(
        functools.partial(attend_fwd_kernel, zm, pm),
        out_shape=outs,
        in_specs=[sm, sm] + [vm] * 18,
        out_specs=(vm,) * len(outs),
        compiler_params=pltpu.CompilerParams(vmem_limit_bytes=40 * 2**20),
        cost_estimate=pl.CostEstimate(flops=2 * 768**3 * 5, bytes_accessed=12 * 2**20, transcendentals=10**6),
        name="attend_fwd",
    )(zlen, plen, x, gain, shift, wq, wk, wv, bq, bk, bv, wo, bo, gain2, shift2, proj_hi, proj_lo, energy_const(), cos, sin)

SQRT_HALF = math.sqrt(0.5)

def gelu_parts(h):
    bell = jnp.exp(h * h * -0.5)
    t = 1.0 / (1.0 + (0.3275911 * SQRT_HALF) * jnp.abs(h))
    poly = t * (0.127414796 + t * (-0.142248368 + t * (0.7107068705 + t * (-0.7265760135 + t * 0.5307027145))))
    tail = poly * bell
    phi = jnp.where(h >= 0, 1.0 - tail, tail)
    return h * phi, phi + h * bell * (1.0 / math.sqrt(2 * math.pi))

def store_relative(out, value, cs, code, pieces):
    step = value.shape[0] // pieces
    for p in range(pieces):
        off = pl.multiple_of(jnp.bitwise_xor(p, code) * step, 16)
        out[pl.ds(off, step), cs] = value[p * step:(p + 1) * step]

def ffn_kernel(pieces, count, at, meta, n2, n2t, cot, cott, hb, *refs):
    hws, rws, refs = refs[:count], refs[count:2 * count], refs[2 * count:]
    send_o, keep_o, act_o, gh_o, bias_o = refs[:5]
    left, right = refs[-2:]
    width = act_o.shape[1]
    tile = 256 if width % 256 == 0 else 128
    if count > 1:
        hw, rw = refs[5:7]
        quarter = meta[4]
        for src, dst in ((hws, hw), (rws, rw)):
            step = src[0].shape[0]
            for p in range(count):
                off = pl.multiple_of(jnp.bitwise_xor(p, quarter) * step, 16)
                dst[pl.ds(off, step), :] = src[p][...]
    else:
        hw, rw = hws[0], rws[0]
    left[0] = n2t[...]
    left[1] = cott[...]
    for c in range(0, width, tile):
        cs = slice(c, c + tile)
        ws = slice(at * width + c, at * width + c + tile)
        h = dot(n2[...], hw[:, ws]) + hb[...].reshape(1, -1)[:, cs].astype(F32)
        act, slope = gelu_parts(h)
        ga = dot_t(cot[...], rw[ws, :])
        gh = (ga * slope).astype(BF)
        act = act.astype(BF)
        act_o[:, cs] = act
        gh_o[:, cs] = gh
        right[0, :, cs] = gh
        right[1, :, cs] = act
        bias_o[:, cs] = jnp.sum(gh.astype(F32), axis=0, keepdims=True)
    me, code = meta[0], meta[1]
    for c in range(0, width, tile):
        cs = slice(c, c + tile)
        store_relative(send_o, dot(left[1 - me], right[1 - me, :, cs]).astype(BF), cs, code, pieces)
        store_relative(keep_o, dot(left[me], right[me, :, cs]).astype(BF), cs, code, pieces)

def ffn_chunk(meta, pieces, n2, n2t, cot, cott, hws, rws, hb, at):
    rows, d = n2.shape
    count = len(hws)
    width = hb.shape[0]
    S = jax.ShapeDtypeStruct
    vm = pl.BlockSpec(memory_space=VM)
    outs = (S((d, width), BF), S((d, width), BF), S((rows, width), BF), S((rows, width), BF), S((1, width), F32))
    if count > 1:
        outs += (S((d, width), BF), S((width, d), BF))
    return pl.pallas_call(
        functools.partial(ffn_kernel, pieces, count, at), out_shape=outs,
        in_specs=[pl.BlockSpec(memory_space=pltpu.SMEM)] + [vm] * (5 + 2 * count), out_specs=(vm,) * len(outs),
        scratch_shapes=[VM((2, d, rows), BF), VM((2, rows, width), BF)],
        compiler_params=pltpu.CompilerParams(vmem_limit_bytes=32 * 2**20),
        cost_estimate=pl.CostEstimate(flops=2 * rows * d * width * 4, bytes_accessed=6 * 2**20, transcendentals=10**6),
        name="ffn_chunk",
    )(meta, n2, n2t, cot, cott, hb, *hws, *rws)

def mid_kernel(k, *refs):
    ghs, hws = refs[:k], refs[k:2 * k]
    middle, cot, wo, gain2, gm_o, gb_o, gatt_o, vec_o = refs[2 * k:]
    rows = middle.shape[0]
    acc_g = acc_s = acc_b = acc_c = 0.0
    for r in range(0, rows, 256):
        rs = slice(r, r + 256)
        e = sum(dot_t(gh[rs, :], hw[...]) for gh, hw in zip(ghs, hws))
        n, rate = norm_parts(middle[rs, :])
        c = cot[rs, :].astype(F32)
        acc_g += jnp.sum(e * n, axis=0, keepdims=True)
        acc_s += jnp.sum(e, axis=0, keepdims=True)
        acc_c += jnp.sum(c, axis=0, keepdims=True)
        eg = e * row(gain2)
        gm = c + rate * (eg - jnp.mean(eg, axis=-1, keepdims=True) - n * jnp.mean(eg * n, axis=-1, keepdims=True))
        gm_o[rs, :] = gm
        gb = gm.astype(BF)
        gb_o[rs, :] = gb
        acc_b += jnp.sum(gb.astype(F32), axis=0, keepdims=True)
        gatt_o[rs, :] = dot_t(gb, wo[...])
    vec_o[...] = jnp.concatenate([acc_g, acc_s, acc_b, acc_c] + [jnp.zeros_like(acc_g)] * 4, axis=0)

def mid(ghs, hws, middle, cot, wo, gain2):
    rows, d = middle.shape
    k = len(ghs)
    S = jax.ShapeDtypeStruct
    vm = pl.BlockSpec(memory_space=VM)
    outs = (S((rows, d), F32), S((rows, d), BF), S((rows, d), F32), S((8, d), F32))
    return pl.pallas_call(
        functools.partial(mid_kernel, k), out_shape=outs,
        in_specs=[vm] * (2 * k + 4), out_specs=(vm,) * 4,
        compiler_params=pltpu.CompilerParams(vmem_limit_bytes=40 * 2**20),
        cost_estimate=pl.CostEstimate(flops=2 * rows * d * (sum(h.shape[1] for h in hws) + 2 * d), bytes_accessed=20 * 2**20, transcendentals=10**4),
        name="mid",
    )(*ghs, *hws, middle, cot, wo, gain2)

def attend_bwd_kernel(zm, pm, pieces, meta, zlen, plen, gatt, gb, xq, xk, v, fq, fk, state, n1t, attt, proj, energy, cos, sin,
                      gq_o, gk_o, gv_o, send_a, keep_a, send_b, keep_b, vec_o, left, right):
    mols = molecules(zm, pm)
    rows, d = gatt.shape
    s2 = 64 ** -0.5
    groups = d // 256
    keep = block_mask(512)
    zero = jnp.zeros((1, 256), F32)
    for g in range(groups):
        cs = slice(g * 256, (g + 1) * 256)
        fs = slice(g * 128, (g + 1) * 128)
        sums = [0.0, 0.0, 0.0]
        for b in range(0, rows, PPAD):
            mem = [(i, r, n) for i, (r, n) in enumerate(mols) if b <= r < b + PPAD]
            gfq, gfk = [], []
            for i, r, n in mem:
                ms = slice(r, r + n)
                st = state[i, g]
                q, k, val = fq[ms, fs], fk[ms, fs], v[ms, cs]
                nd = dot(q, st)
                rden = 1.0 / nd[:, 256:]
                u = gatt[ms, cs] * rden
                w = u * (nd[:, :256] * rden)
                uw = jnp.concatenate([u, -w], axis=1).astype(BF)
                gfq.append(dot_t(uw, st))
                gst = jnp.where(keep, dot_c(q, uw), 0.0).astype(BF)
                val1 = jnp.concatenate([val, jnp.ones((n, 256), BF)], axis=1)
                gv = dot(k, gst[:, :256]).astype(BF)
                gv_o[ms, cs] = gv
                gfk.append(dot_t(val1, gst))
            rs = slice(b, b + PPAD)
            cosb = jnp.concatenate([cos[:n, :] for _, _, n in mem], axis=0)
            sinb = jnp.concatenate([sin[:n, :] for _, _, n in mem], axis=0)
            cosb = jnp.concatenate([cosb, cosb], axis=1)
            sinb = jnp.concatenate([sinb, sinb], axis=1)
            for t, (gf, f, x, o) in enumerate(((gfq, fq, xq, gq_o), (gfk, fk, xk, gk_o))):
                gp = (jnp.concatenate(gf, axis=0) * f[rs, fs].astype(F32)).astype(BF)
                back = dot(gp, proj[g])
                tot = dot(gp, energy[...])
                grad = (cosb * back[:, :256] + sinb * back[:, 256:] - tot * x[rs, cs].astype(F32)).astype(BF)
                o[rs, cs] = grad
                sums[t] += jnp.sum(grad.astype(F32), axis=0, keepdims=True)
            sums[2] += jnp.sum(gv_o[rs, cs].astype(F32), axis=0, keepdims=True)
        vec_o[:, cs] = jnp.concatenate(sums + [zero] * 5, axis=0)
    left[0] = attt[...]
    left[1] = n1t[...]
    right[0] = gb[...]
    right[1] = gv_o[...]
    right[2] = gq_o[...]
    right[3] = gk_o[...]
    me = meta[0]
    half = d // 2
    for lane in range(2):
        code = meta[2 + lane]
        for c in range(0, half, 128):
            cs, to = slice(lane * half + c, lane * half + c + 128), slice(lane * half + c, lane * half + c + 128)
            store_relative(send_a, dot(left[1 - me], right[1 - me, :, cs]).astype(BF), to, code, pieces)
            store_relative(keep_a, dot(left[me], right[me, :, cs]).astype(BF), to, code, pieces)
            store_relative(send_b, dot(left[1], right[3 - me, :, cs]).astype(BF), to, code, pieces)
            store_relative(keep_b, dot(left[1], right[2 + me, :, cs]).astype(BF), to, code, pieces)

def attend_bwd(meta, n_pair, zlen, plen, gatt, gb, xq, xk, v, fq, fk, state, n1t, attt, proj, cos, sin):
    rows, d = gatt.shape
    zm, pm = zlen.shape[0], plen.shape[0]
    S = jax.ShapeDtypeStruct
    vm = pl.BlockSpec(memory_space=VM)
    sm = pl.BlockSpec(memory_space=pltpu.SMEM)
    outs = (S((rows, d), BF),) * 3 + (S((d, d), BF),) * 4 + (S((8, d), F32),)
    return pl.pallas_call(
        functools.partial(attend_bwd_kernel, zm, pm, 2 ** n_pair), out_shape=outs,
        in_specs=[sm] * 3 + [vm] * 14, out_specs=(vm,) * 8,
        scratch_shapes=[VM((2, d, rows), BF), VM((4, rows, d), BF)],
        compiler_params=pltpu.CompilerParams(vmem_limit_bytes=40 * 2**20),
        cost_estimate=pl.CostEstimate(flops=2 * d**3 * 6, bytes_accessed=12 * 2**20, transcendentals=10**6),
        name="attend_bwd",
    )(meta, zlen, plen, gatt, gb, xq, xk, v, fq, fk, state, n1t, attt, proj, back_energy_const(), cos, sin)

def back_energy_const():
    f = np.arange(128)[:, None] // 32
    c = np.arange(256)[None, :] // 64
    return ((f == c) * 64 ** -0.5).astype(jnp.bfloat16)

def input_kernel(gq, gk, gv, wq, wk, wv, x, gm, gain, out_o, vec_o):
    rows = x.shape[0]
    acc_g = acc_s = 0.0
    for r in range(0, rows, 256):
        rs = slice(r, r + 256)
        e = dot_t(gq[rs, :], wq[...]) + dot_t(gk[rs, :], wk[...]) + dot_t(gv[rs, :], wv[...])
        n, rate = norm_parts(x[rs, :].astype(F32))
        acc_g += jnp.sum(e * n, axis=0, keepdims=True)
        acc_s += jnp.sum(e, axis=0, keepdims=True)
        eg = e * row(gain)
        gx = rate * (eg - jnp.mean(eg, axis=-1, keepdims=True) - n * jnp.mean(eg * n, axis=-1, keepdims=True))
        out_o[rs, :] = (gm[rs, :] + gx).astype(BF)
    vec_o[...] = jnp.concatenate([acc_g, acc_s] + [jnp.zeros_like(acc_g)] * 6, axis=0)

def input_back(gq, gk, gv, wq, wk, wv, x, gm, gain):
    rows, d = x.shape
    S = jax.ShapeDtypeStruct
    vm = pl.BlockSpec(memory_space=VM)
    return pl.pallas_call(
        input_kernel, out_shape=(S((rows, d), BF), S((8, d), F32)),
        in_specs=[vm] * 9, out_specs=(vm,) * 2,
        compiler_params=pltpu.CompilerParams(vmem_limit_bytes=32 * 2**20),
        cost_estimate=pl.CostEstimate(flops=2 * d**3 * 3, bytes_accessed=12 * 2**20, transcendentals=10**4),
        name="input_back",
    )(gq, gk, gv, wq, wk, wv, x, gm, gain)

def layer_kernel(k, *refs):
    acts, rws = refs[:k], refs[k:2 * k]
    middle, bias, out_o = refs[2 * k:]
    rows = middle.shape[0]
    for r in range(0, rows, 256):
        rs = slice(r, r + 256)
        total = sum(dot(a[rs, :], w[...]) for a, w in zip(acts, rws))
        out_o[rs, :] = (middle[rs, :] + total + row(bias)).astype(BF)

def layer_end(acts, rws, middle, bias):
    rows, d = middle.shape
    k = len(acts)
    vm = pl.BlockSpec(memory_space=VM)
    return pl.pallas_call(
        functools.partial(layer_kernel, k), out_shape=jax.ShapeDtypeStruct((rows, d), BF),
        in_specs=[vm] * (2 * k + 2), out_specs=vm,
        compiler_params=pltpu.CompilerParams(vmem_limit_bytes=32 * 2**20),
        cost_estimate=pl.CostEstimate(flops=2 * rows * d * sum(w.shape[0] for w in rws), bytes_accessed=12 * 2**20, transcendentals=0),
        name="layer_end",
    )(*acts, *rws, middle, bias)


def flip(value, axis, bit, size):
    return lax.ppermute(value, axis, [(i, i ^ bit) for i in range(size)])

def bits_below(size):
    return [1 << i for i in range(size.bit_length() - 1)]

class Layout:
    def __init__(self, mesh):
        self.nb, self.nt = mesh.shape["batch"], mesh.shape["tp"]
        self.tp = [("tp", b) for b in bits_below(self.nt)]
        self.batch = [("batch", b) for b in bits_below(self.nb)[1:]]
        self.lane_bits = (self.tp + self.batch, self.batch[:1] + self.tp + self.batch[1:])

    def swap(self, value, level):
        axis, bit = level
        return flip(value, axis, bit, self.nb if axis == "batch" else self.nt)

    def core(self, value):
        return flip(value, "batch", 1, self.nb)

def code_of(levels, place):
    out = jnp.int32(0)
    for axis, bit in levels:
        out = out * 2 + (place[axis] // bit) % 2
    return out

def add(a, b):
    return (a.astype(F32) + b.astype(F32)).astype(BF)

def halve(lay, value, level):
    n = value.shape[0] // 2
    return add(value[:n], lay.swap(value[n:], level))

def scatter_width(levels, rows, least=48):
    n = 0
    while n < len(levels) and rows % 2 == 0 and rows // 2 >= least and (rows // 2) % 16 == 0:
        rows //= 2
        n += 1
    return n

def finish_ffn_kernel(pieces, meta, m0, m1, t0, t1, *rest):
    ghw_o, grw_o, mine, theirs = rest[-4:]
    code, core = meta[1], meta[0]
    half = pieces // 2
    step = m0.shape[0] // half
    for p in range(pieces):
        off = pl.multiple_of(jnp.bitwise_xor(p, code) * step, 16)
        src = slice((p % half) * step, (p % half + 1) * step)
        mine[pl.ds(off, step), :] = (m0 if p < half else m1)[src, :]
        theirs[pl.ds(off, step), :] = (t0 if p < half else t1)[src, :]
    first = (core == 0).astype(F32)
    a, b = mine[...].astype(F32), theirs[...].astype(F32)
    ghw_o[...] = jnp.where(core == 0, a, b)
    grw_o[...] = jnp.where(core == 0, b, a).T

def finish_ffn(meta, pieces, parts, k, shard, before):
    d, width = 2 * parts[0].shape[0], parts[0].shape[1]
    S = jax.ShapeDtypeStruct
    vm = pl.BlockSpec(memory_space=VM)
    sm = pl.BlockSpec(memory_space=pltpu.SMEM)
    extra = [] if before is None else list(before)
    return pl.pallas_call(
        functools.partial(finish_ffn_kernel, pieces), grid=(1,),
        out_shape=(S((d, shard), F32), S((shard, d), F32)),
        in_specs=[sm] + [vm] * 4 + [pl.BlockSpec(memory_space=pl.ANY)] * len(extra),
        out_specs=(pl.BlockSpec((d, width), lambda i: (0, k)), pl.BlockSpec((width, d), lambda i: (k, 0))),
        scratch_shapes=[VM((d, width), BF)] * 2,
        input_output_aliases={5: 0, 6: 1} if extra else {},
        compiler_params=pltpu.CompilerParams(vmem_limit_bytes=32 * 2**20),
        cost_estimate=pl.CostEstimate(flops=0, bytes_accessed=12 * d * width, transcendentals=0),
        name="finish_ffn",
    )(meta, *parts, *extra)

def finish_pair_kernel(pieces, cut, meta, *refs):
    parts, (first_o, second_o, mine, theirs) = refs[:-4], refs[-4:]
    half = pieces // 2
    for lane, cs in enumerate((slice(0, cut), slice(cut, None))):
        code = meta[2 + lane]
        m0, m1, t0, t1 = parts[4 * lane:4 * lane + 4]
        step = m0.shape[0] // half
        for p in range(pieces):
            off = pl.multiple_of(jnp.bitwise_xor(p, code) * step, 16)
            src = slice((p % half) * step, (p % half + 1) * step)
            mine[pl.ds(off, step), cs] = (m0 if p < half else m1)[src, :]
            theirs[pl.ds(off, step), cs] = (t0 if p < half else t1)[src, :]
    a, b = mine[...].astype(F32), theirs[...].astype(F32)
    first_o[...] = jnp.where(meta[0] == 0, a, b)
    second_o[...] = jnp.where(meta[0] == 0, b, a)

def finish_pair(meta, pieces, cut, parts, d):
    S = jax.ShapeDtypeStruct
    vm = pl.BlockSpec(memory_space=VM)
    sm = pl.BlockSpec(memory_space=pltpu.SMEM)
    whole = pl.BlockSpec((d, d), lambda i: (0, 0))
    return pl.pallas_call(
        functools.partial(finish_pair_kernel, pieces, cut), grid=(1,),
        out_shape=(S((d, d), F32),) * 2,
        in_specs=[sm] + [vm] * 8, out_specs=(whole, whole),
        scratch_shapes=[VM((d, d), BF)] * 2,
        compiler_params=pltpu.CompilerParams(vmem_limit_bytes=32 * 2**20),
        cost_estimate=pl.CostEstimate(flops=0, bytes_accessed=12 * d * d, transcendentals=0),
        name="finish_pair",
    )(meta, *parts)

def reduce_ffn(lay, keeps, recvs, cut):
    x = lay.batch[0]
    nt = len(keeps)
    d = keeps[0].shape[0]
    low, high = slice(0, d // 2), slice(d // 2, d)
    left = [add(a[:, :cut], b[:, :cut]) for a, b in zip(keeps, recvs)]
    right_send = jnp.concatenate([add(a[high, cut:], b[high, cut:]) for a, b in zip(keeps, recvs)], axis=0)
    right = jnp.concatenate([add(a[low, cut:], b[low, cut:]) for a, b in zip(keeps, recvs)], axis=0)
    right = add(right, lay.swap(right_send, x))
    right = [right[j * (d // 2):(j + 1) * (d // 2)] for j in range(nt)]
    for level in reversed(lay.tp):
        bit = level[1]
        left = [add(left[j], lay.swap(left[j | bit], level)) for j in range(bit)]
        right = [add(right[j], lay.swap(right[j | bit], level)) for j in range(bit)]
    left = halve(lay, left[0], x)
    held = jnp.concatenate([left, right[0]], axis=1)
    for level in lay.batch[1:]:
        held = halve(lay, held, level)
    for level in reversed(lay.batch[1:]):
        held = jnp.concatenate([held, lay.swap(held, level)], axis=0)
    other = lay.swap(held, x)
    return held, other, lay.core(held), lay.core(other)

def reduce_pair(lay, keep, recv, cut):
    d = keep.shape[0]
    lanes = []
    n = scatter_width(lay.lane_bits[0], d)
    join = 1 + len(lay.tp)
    for bits, cs in zip(lay.lane_bits, (slice(0, cut), slice(cut, None))):
        half = d // 2
        held = add(add(keep[:half, cs], recv[:half, cs]), lay.swap(add(keep[half:, cs], recv[half:, cs]), bits[0]))
        for level in bits[1:min(n, join)]:
            held = halve(lay, held, level)
        lanes.append(held)
    held = jnp.concatenate(lanes, axis=1)
    rest = lay.lane_bits[0][join:]
    back = min(n, join)
    for i, level in enumerate(rest):
        held = halve(lay, held, level) if join + i < n else add(held, lay.swap(held, level))
    assert n >= join or True
    for i, level in reversed(list(enumerate(rest))):
        if join + i < n:
            held = jnp.concatenate([held, lay.swap(held, level)], axis=0)
    out = []
    for bits, cs in zip(lay.lane_bits, (slice(0, cut), slice(cut, None))):
        part = held[:, cs]
        for level in reversed(bits[1:back]):
            part = jnp.concatenate([part, lay.swap(part, level)], axis=0)
        other = lay.swap(part, bits[0])
        out += [part, other, lay.core(part), lay.core(other)]
    return out

def on_device(
    lay,
    inputs,
    cotangent,
    zinc_lengths,
    pubchem_lengths,
    feature_stack,
    train_step,
    redraw_interval,
    attn_gain,
    attn_shift,
    query_weight,
    query_bias,
    key_weight,
    key_bias,
    value_weight,
    value_bias,
    output_weight,
    output_bias,
    ffn_gain,
    ffn_shift,
    hidden_weight,
    hidden_bias,
    return_weight,
    return_bias,
):
    nt = lay.nt
    d, shard = hidden_weight.shape
    width = min(768, shard)
    chunks = shard // width
    place = {"batch": lax.axis_index("batch"), "tp": lax.axis_index("tp")}
    core = place["batch"] % 2
    n_pair = scatter_width(lay.lane_bits[0], d)
    quarter = place["batch"] % 4
    meta = jnp.stack([
        core, code_of(lay.batch, place), code_of(lay.lane_bits[0][:n_pair], place),
        code_of(lay.lane_bits[1][:n_pair], place), quarter,
    ]).astype(jnp.int32)
    pick = train_step[0] // redraw_interval[0] % feature_stack.shape[0]
    fp = lax.dynamic_index_in_dim(feature_stack, pick, 0, keepdims=False)
    proj_hi, proj_lo = projection_blocks(fp)
    cos, sin = rotary_const()

    gathered = {}
    for k in range(chunks):
        hw = lax.dynamic_slice(hidden_weight, (quarter * (d // 4), k * width), (d // 4, width))
        rw = lax.dynamic_slice(return_weight, (k * width + quarter * (width // 4), 0), (width // 4, d))
        hb = hidden_bias[k * width:(k + 1) * width]
        pool = {0: (hw, rw, hb)}
        for level in lay.tp:
            for j in list(pool):
                pool[j | level[1]] = tuple(lay.swap(v, level) for v in pool[j])
        for j in range(1, nt):
            hw, rw, hb = pool[j]
            x = lay.batch[0]
            hw2, rw2 = lay.swap(hw, x), lay.swap(rw, x)
            gathered[j, k] = ([hw, lay.core(hw), hw2, lay.core(hw2)], [rw, lay.core(rw), rw2, lay.core(rw2)], hb)

    (n1, n1t, xq, xk, v, fq, fk, state, att, attt, middle, n2, n2t) = attend_fwd(
        inputs, zinc_lengths, pubchem_lengths, attn_gain, attn_shift, query_weight, query_bias, key_weight, key_bias,
        value_weight, value_bias, output_weight, output_bias, ffn_gain, ffn_shift, proj_hi, proj_lo, cos, sin)
    cott = cotangent.T
    acts, slopes, hws, rws, biases, ffn_parts = [], [], [], [], {}, []
    cut = (width // 256) * 128
    for k in range(chunks):
        keeps, recvs = {}, {}
        for j in list(range(1, nt)) + [0]:
            if j:
                hw4, rw4, hb = gathered[j, k]
                send, keep, act, gh, gb, hw, rw = ffn_chunk(meta, 2 ** len(lay.batch), n2, n2t, cotangent, cott, hw4, rw4, hb, 0)
            else:
                send, keep, act, gh, gb = ffn_chunk(meta, 2 ** len(lay.batch), n2, n2t, cotangent, cott, [hidden_weight], [return_weight],
                                                    hidden_bias[k * width:(k + 1) * width], k)
                hw, rw = hidden_weight[:, k * width:(k + 1) * width], return_weight[k * width:(k + 1) * width]
            acts.append(act)
            slopes.append(gh)
            hws.append(hw)
            rws.append(rw)
            biases[j, k] = gb[0]
            keeps[j], recvs[j] = keep, lay.core(send)
        ffn_parts.append(reduce_ffn(lay, [keeps[j] for j in range(nt)], [recvs[j] for j in range(nt)], cut))
    gm, gb, gatt, vec1 = mid(slopes, hws, middle, cotangent, output_weight, ffn_gain)
    gq, gk, gv, send_a, keep_a, send_b, keep_b, vec2 = attend_bwd(
        meta, n_pair, zinc_lengths, pubchem_lengths, gatt, gb, xq, xk, v, fq, fk, state, n1t, attt, proj_hi, cos, sin)
    pair_a = reduce_pair(lay, keep_a, lay.core(send_a), d // 2)
    pair_b = reduce_pair(lay, keep_b, lay.core(send_b), d // 2)
    input_grad, vec3 = input_back(gq, gk, gv, query_weight, key_weight, value_weight, inputs, gm, attn_gain)
    layer_out = layer_end(acts, rws, middle, return_bias)

    vectors = jnp.concatenate([vec1[:4], vec2[:3], vec3[:2]], axis=0).reshape(-1)
    hidden = {j: jnp.concatenate([biases[j, k] for k in range(chunks)]) for j in range(nt)}
    for level in reversed(lay.tp):
        bit = level[1]
        got = lay.swap(jnp.concatenate([vectors] + [hidden[j | bit] for j in range(bit)]), level)
        vectors = vectors + got[:vectors.shape[0]]
        hidden = {j: hidden[j] + got[vectors.shape[0] + j * shard:vectors.shape[0] + (j + 1) * shard] for j in range(bit)}
    small = jnp.concatenate([vectors, hidden[0]])
    for level in [("batch", 1)] + lay.batch:
        small = small + lay.swap(small, level)
    vecs = small[:9 * d].reshape(9, d)
    grad_hidden_bias = small[9 * d:]

    ffn_out = None
    for k in range(chunks):
        ffn_out = finish_ffn(meta, 2 ** len(lay.batch), ffn_parts[k], k, shard, ffn_out)
    gwo, gwv = finish_pair(meta, 2 ** n_pair, d // 2, pair_a, d)
    gwq, gwk = finish_pair(meta, 2 ** n_pair, d // 2, pair_b, d)
    return (layer_out, input_grad, vecs[7], vecs[8], gwq, vecs[4], gwk, vecs[5], gwv, vecs[6], gwo, vecs[2],
            vecs[0], vecs[1], ffn_out[0], grad_hidden_bias, ffn_out[1], vecs[3])

def solution(mesh):
    rows, whole, hidden = P(("batch", "tp"), None), P(), P(None, "tp")
    return jax.shard_map(
        functools.partial(on_device, Layout(mesh)),
        mesh=mesh,
        in_specs=(rows, rows, P(("batch", "tp")), P(("batch", "tp"))) + (whole,) * 15 + (hidden, P("tp"), P("tp", None), whole),
        out_specs=(rows, rows) + (whole,) * 12 + (hidden, P("tp"), P("tp", None), whole),
        check_vma=False,
    )
```

```python
import functools
import math

import jax
import jax.numpy as jnp
import numpy as np
from jax import lax
from jax.experimental import pallas as pl
from jax.experimental.pallas import tpu as pltpu
from jax.sharding import PartitionSpec as P

ZPAD = 64
PPAD = 256
F32 = jnp.float32
BF = jnp.bfloat16
VM = pltpu.VMEM
GROUP = 4
S = jax.ShapeDtypeStruct
TIMES = {"attend_fwd": 14, "ffn_chunk": 17, "layer_end": 9, "value_bwd": 24, "query_bwd": 20, "finish_ffn": 5, "finish_pair": 5}
MIB = 2**20
GRANT = 60


def dot(a, b):
    return jnp.dot(a, b, preferred_element_type=F32)


def dot_t(a, b):
    return lax.dot_general(a, b, (((1,), (1,)), ((), ())), preferred_element_type=F32)


def dot_c(a, b):
    return lax.dot_general(a, b, (((0,), (0,)), ((), ())), preferred_element_type=F32)


def split(v):
    hi = v.astype(BF)
    return hi, (v - hi.astype(F32)).astype(BF)


def norm_parts(values):
    center = values - jnp.mean(values, axis=-1, keepdims=True)
    rate = lax.rsqrt(jnp.mean(center * center, axis=-1, keepdims=True) + 1e-05)
    return center * rate, rate


def row(ref):
    return ref[...].reshape(1, -1)


def block_mask(width):
    f = lax.broadcasted_iota(jnp.int32, (128, width), 0) // 32
    c = lax.broadcasted_iota(jnp.int32, (128, width), 1) % 256 // 64
    return f == c


def molecules(zm, pm):
    return [(i * ZPAD, ZPAD) for i in range(zm)] + [(zm * ZPAD + i * PPAD, PPAD) for i in range(pm)]


def members(mols, b):
    return [(i, r, n) for i, (r, n) in enumerate(mols) if b * PPAD <= r < (b + 1) * PPAD]


class Mover:
    def __init__(self, sems):
        self.sems, self.n, self.out = sems, 0, []

    def load(self, src, dst):
        copy = pltpu.make_async_copy(src, dst, self.sems.at[self.n])
        self.n += 1
        copy.start()
        return copy

    def store(self, src, dst):
        self.out.append(self.load(src, dst))

    def finish(self):
        for copy in self.out:
            copy.wait()


def call(kernel, name, args, spaces, outs, scratch, copies, flops, moved, aliases=None, after=()):
    n, extra = len(args), len(after)

    def body(*refs):
        kernel(*refs[:n], *refs[n + extra:])

    spec = {
        "v": pl.BlockSpec(memory_space=VM),
        "h": pl.BlockSpec(memory_space=pltpu.HBM),
        "s": pl.BlockSpec(memory_space=pltpu.SMEM),
    }
    return pl.pallas_call(
        body,
        out_shape=tuple(o for _, o in outs),
        in_specs=[spec[s] for s in spaces] + [spec["h"]] * extra,
        out_specs=tuple(spec[s] for s, _ in outs),
        scratch_shapes=list(scratch) + [pltpu.SemaphoreType.DMA((copies,))],
        input_output_aliases=aliases or {},
        compiler_params=pltpu.CompilerParams(vmem_limit_bytes=GRANT * MIB),
        cost_estimate=pl.CostEstimate(flops=int(TIMES[name] * 1.15e9), bytes_accessed=moved, transcendentals=0),
        name=name,
    )(*args, *after)


VECS = ("gain", "shift", "bq", "bk", "bv", "bo", "gain2", "shift2", "br")


def attend_fwd_kernel(zm, pm, at, which, meta, cot_h, x_h, vec_h, wq_h, wk_h, wv_h, wo_h, proj_h, table_h, energy_h, *refs):
    (qkv_h, f_h, state_h, trans_h, middle_h, n2_h, left_h,
     cot, n2_o, left_o, x, vec, wq, wk, wv, wo, proj, table, energy, qkv, f_s, state_s, trans, middle_s, att_s, sems) = refs[-26:]
    move = Mover(sems)
    d = x.shape[1]
    every = slice(which[0] * PPAD, (which[-1] + 1) * PPAD)
    first = [move.load(x_h.at[every], x.at[every]), move.load(vec_h, vec), move.load(cot_h.at[every], cot.at[every])]
    later = [move.load(s, t) for s, t in ((wq_h, wq), (proj_h, proj), (table_h, table), (energy_h, energy), (wk_h, wk), (wv_h, wv))]
    last = move.load(wo_h, wo)
    mols = molecules(zm, pm)
    groups = d // 256
    keep = block_mask(512)
    ones = jnp.ones((PPAD, 256), BF)
    for c in first:
        c.wait()
    gain, shift, bq, bk, bv, bo, gain2, shift2 = (row(vec)[:, i * d:(i + 1) * d] for i in range(8))
    n1s = {}
    for b in which:
        rs = slice(b * PPAD, (b + 1) * PPAD)
        normed, _ = norm_parts(x[rs, :].astype(F32))
        n1s[b] = (normed * gain + shift).astype(BF)
        trans[1, :, rs] = n1s[b].T
        left_o[1, :, rs] = cot[rs, :].T
    for c in later:
        c.wait()
    for b in which:
        mem = members(mols, b)
        rs = slice(b * PPAD, (b + 1) * PPAD)
        n1 = n1s[b]
        cosb, sinb = (jnp.concatenate([table[t, :n, :] for _, _, n in mem], axis=0) for t in range(2))
        cosb = jnp.concatenate([cosb, cosb], axis=1)
        sinb = jnp.concatenate([sinb, sinb], axis=1)
        live = jnp.concatenate(
            [(lax.broadcasted_iota(jnp.int32, (n, 128), 0) < meta[at + i]).astype(F32) for i, r, n in mem], axis=0)
        for g in range(groups):
            cs = slice(g * 256, (g + 1) * 256)
            fs = slice(g * 128, (g + 1) * 128)

            def features(w, bias, slot):
                v = dot(n1, w[:, cs]) + bias[:, cs]
                qkv[slot, rs, cs] = v.astype(BF)
                ch, cl = split(v * cosb)
                sh, sl = split(v * sinb)
                eh, el = split(v * v)
                ph, plo = proj[0, g], proj[1, g]
                e = energy[...]
                inner = (dot_t(ch, ph[:, :256]) + dot_t(sh, ph[:, 256:]) + dot_t(cl, ph[:, :256]) + dot_t(sl, ph[:, 256:])
                         + dot_t(ch, plo[:, :256]) + dot_t(sh, plo[:, 256:]) - dot_t(eh, e) - dot_t(el, e))
                return jnp.exp(inner) * (32 ** -0.5)

            fq = features(wq, bq, 0).astype(BF)
            fk = (features(wk, bk, 1) * live).astype(BF)
            f_s[0, rs, fs] = fq
            f_s[1, rs, fs] = fk
            v = (dot(n1, wv[:, cs]) + bv[:, cs]).astype(BF)
            qkv[2, rs, cs] = v
            for i, r, n in mem:
                ms = slice(r - b * PPAD, r - b * PPAD + n)
                vo = jnp.concatenate([v[ms], ones[:n]], axis=1)
                state = jnp.where(keep, dot_c(fk[ms], vo), 0.0).astype(BF)
                state_s[i, g] = state
                nd = dot(fq[ms], state)
                att_s[r:r + n, cs] = (nd[:, :256] / nd[:, 256:]).astype(BF)
    inside = [i for b in which for i, _, _ in members(mols, b)]
    ms = slice(inside[0], inside[-1] + 1)
    for s, t in ((qkv.at[:, every], qkv_h.at[:, every]), (f_s.at[:, every], f_h.at[:, every]), (state_s.at[ms], state_h.at[ms])):
        move.store(s, t)
    last.wait()
    for b in which:
        rs = slice(b * PPAD, (b + 1) * PPAD)
        trans[0, :, rs] = att_s[rs, :].T
        middle = x[rs, :].astype(F32) + (dot(att_s[rs, :], wo[...]) + bo)
        middle_s[rs, :] = middle
        normed, _ = norm_parts(middle)
        n2 = (normed * gain2 + shift2).astype(BF)
        n2_o[rs, :] = n2
        left_o[0, :, rs] = n2.T
    move.store(n2_o.at[every], n2_h.at[every])
    move.store(left_o.at[:, :, every], left_h.at[:, :, every])
    move.store(middle_s.at[every], middle_h.at[every])
    move.store(trans.at[:, :, every], trans_h.at[:, :, every])
    move.finish()


def rotary_const():
    place = np.arange(PPAD, dtype=np.float64)
    rates = np.exp(np.arange(32, dtype=np.float64) * (-2.0 * math.log(10000.0) / 64))
    ang = place[:, None] * rates[None, :]
    return np.tile(np.stack([np.cos(ang), np.sin(ang)]), (1, 1, 4)).astype(np.float32)


def projection_blocks(fp):
    heads, m, hd = fp.shape
    turned = jnp.concatenate([fp[..., hd // 2:], -fp[..., :hd // 2]], axis=-1)
    eye = jnp.eye(GROUP, dtype=F32)

    def blocks(p):
        p = (p * hd ** -0.25).reshape(heads // GROUP, GROUP, m, 1, hd) * eye[None, :, None, :, None]
        return p.reshape(heads // GROUP, GROUP * m, GROUP * hd)

    return jnp.stack(split(jnp.concatenate([blocks(fp), blocks(turned)], axis=-1)))


def head_const(scale):
    f = np.arange(128)[:, None] // 32
    c = np.arange(256)[None, :] // 64
    return ((f == c) * scale).astype(jnp.bfloat16)


def attend_fwd(which, before, after, meta, at, zm, pm, cot, x, vec, wq, wk, wv, wo, proj, table):
    rows, d = x.shape
    groups = d // 256
    states = (zm + pm, groups, 128, 512)
    outs = [("h", S((3, rows, d), BF)), ("h", S((2, rows, d // 2), BF)), ("h", S(states, BF)), ("h", S((2, d, rows), BF)),
            ("h", S((rows, d), F32)), ("h", S((rows, d), BF)), ("h", S((2, d, rows), BF))]
    args = (meta, cot, x, vec, wq, wk, wv, wo, proj, table, head_const(1 / 16))
    scratch = ([VM((rows, d), BF)] * 2 + [VM((2, d, rows), BF), VM((rows, d), BF), VM(vec.shape, F32)] + [VM((d, d), BF)] * 4 + [VM(proj.shape, BF), VM(table.shape, F32), VM((128, 256), BF)]
               + [VM((3, rows, d), BF), VM((2, rows, d // 2), BF), VM(states, BF), VM((2, d, rows), BF), VM((rows, d), F32), VM((rows, d), BF)])
    return call(
        functools.partial(attend_fwd_kernel, zm, pm, at, which), "attend_fwd", args + tuple(before),
        "s" + "h" * (len(args) - 1 + len(before)), outs, scratch, 20,
        2 * 256 * d * d * 4 * len(which), 4 * MIB * len(which), {len(args) + i: i for i in range(len(before))}, after)


def gelu_parts(h):
    bell = jnp.exp(h * h * -0.5)
    t = 1.0 / (1.0 + (0.3275911 * math.sqrt(0.5)) * jnp.abs(h))
    poly = t * (0.127414796 + t * (-0.142248368 + t * (0.7107068705 + t * (-0.7265760135 + t * 0.5307027145))))
    tail = poly * bell
    phi = jnp.where(h >= 0, 1.0 - tail, tail)
    return h * phi, phi + h * bell * (1.0 / math.sqrt(2 * math.pi))


def place_pieces(code, src, dst):
    n, step = src.shape[0], src.shape[1]
    for p in range(n):
        off = pl.multiple_of(jnp.bitwise_xor(p, code) * step, 16)
        dst[pl.ds(off, step), :] = src[p]


def store_relative(out, value, cs, code, pieces):
    step = value.shape[0] // pieces
    for p in range(pieces):
        off = pl.multiple_of(jnp.bitwise_xor(p, code) * step, 16)
        out[pl.ds(off, step), cs] = value[p * step:(p + 1) * step]


def ffn_kernel(pieces, shards, k, per, chunks, meta, n2_h, left_h, cot_h, hb_h, hw_h, rw_h, *refs):
    parts = {j: refs[(j - 1) * per:j * per] for j in range(1, shards)}
    hbs = refs[(shards - 1) * per:(shards - 1) * (per + 1)]
    (send_h, keep_h, right_h, bias_o, hws_h, rws_h, n2, left, cot, hb, hw, rw, hw4, rw4, right, stage, sems) = refs[-17:]
    move = Mover(sems)
    d, width = hw.shape[1:]
    quarter = d // 4
    me, code = meta[0], meta[1]
    order = list(range(1, shards)) + [0]
    early, late = {}, {}
    for j in order:
        early[j] = [move.load(hbs[j - 1] if j else hb_h, hb.at[j])]
        if j == order[0]:
            early[j].append(move.load(n2_h, n2))
        late[j] = []
        if j == 0:
            early[j].append(move.load(hw_h.at[:, k * width:(k + 1) * width], hw.at[0]))
            late[j].append(move.load(rw_h.at[k * width:(k + 1) * width, :], rw.at[0]))
        elif per == 4:
            early[j] += [move.load(parts[j][p].at[:quarter], hw4.at[j - 1, p]) for p in range(4)]
            late[j] += [move.load(parts[j][p].at[quarter:], rw4.at[j - 1, p]) for p in range(4)]
        else:
            early[j] += [move.load(parts[j][p], hw4.at[j - 1, p]) for p in range(4)]
            late[j] += [move.load(parts[j][4 + p], rw4.at[j - 1, p]) for p in range(4)]
        if j == order[0]:
            late[j].append(move.load(cot_h, cot))
    last = move.load(left_h, left)
    step, half = d // pieces, pieces // 2
    tile = 256 if width % 256 == 0 else 128
    for j in order:
        for c in early[j] + late[j]:
            c.wait()
        if j:
            place_pieces(meta[4], hw4.at[j - 1], hw.at[j])
            place_pieces(meta[4], rw4.at[j - 1], rw.at[j])
        bias = hb[j].reshape(1, -1)[:, k * width:(k + 1) * width].astype(F32)
        for c in range(0, width, tile):
            cs = slice(c, c + tile)
            h = dot(n2[...], hw[j, :, cs]) + bias[:, cs]
            act, slope = gelu_parts(h)
            ga = dot_t(cot[...], rw[j, cs, :])
            gh = (ga * slope).astype(BF)
            right[0, j, :, cs] = gh
            right[1, j, :, cs] = act.astype(BF)
            bias_o[j:j + 1, cs] = jnp.sum(gh.astype(F32), axis=0, keepdims=True)
        move.store(right.at[:, j], right_h.at[:, j])
        move.store(hw.at[j], hws_h.at[j])
        move.store(rw.at[j], rws_h.at[j])
    last.wait()
    for kind, slot, out in ((1 - me, 0, send_h), (me, 1, keep_h)):
        for j in order:
            for c in range(0, width, tile):
                cs = slice(c, c + tile)
                value = dot(left[kind], right[kind, j, :, cs]).astype(BF)
                for p in range(pieces):
                    rel = jnp.bitwise_xor(p, code)
                    second = rel // half * (shards * half) + j * half + rel % half
                    off = pl.multiple_of(jnp.where(kind == 0, j * pieces + rel, second) * step, 16)
                    stage[slot, pl.ds(off, step), cs] = value[p * step:(p + 1) * step]
        move.store(stage.at[slot], out)
    move.finish()


def ffn_chunk(meta, pieces, shards, n2, left, cot, hb, hw, rw, parts, hbs, k, chunks, width, after=()):
    rows, d = n2.shape
    per = len(parts[0])
    big = S((shards * d, width), BF)
    outs = [("h", big), ("h", big), ("h", S((2, shards, rows, width), BF)), ("v", S((shards, width), F32)),
            ("h", S((shards, d, width), BF)), ("h", S((shards, width, d), BF))]
    scratch = [VM((rows, d), BF), VM((2, d, rows), BF), VM((rows, d), BF), VM((shards, 1) + hb.shape, BF), VM((shards, d, width), BF),
               VM((shards, width, d), BF), VM((shards - 1, 4, d // 4, width), BF), VM((shards - 1, 4, width // 4, d), BF),
               VM((2, shards, rows, width), BF), VM((2, shards * d, width), BF)]
    args = (meta, n2, left, cot, hb.reshape(1, -1), hw, rw) + tuple(p for part in parts for p in part) + tuple(b.reshape(1, -1) for b in hbs)
    return call(
        functools.partial(ffn_kernel, pieces, shards, k, per, chunks), "ffn_chunk", args,
        "s" + "h" * (len(args) - 1), outs, scratch, 10 + 13 * shards, 2 * rows * d * width * 4 * shards, 12 * MIB, None, after)


def products(move, pieces, codes, stage, outs):
    for slot, (left, right, out) in enumerate(outs):
        for c in range(0, out.shape[0], 256):
            cs = slice(c, c + 256)
            store_relative(stage.at[slot], dot(left[...], right[:, cs]).astype(BF), cs, codes[slot], pieces)
        move.store(stage.at[slot], out)


def value_bwd_kernel(zm, pm, pieces, chunks, meta, cot_h, middle_h, wo_h, vec_h, f_h, state_h, trans_h, *refs):
    rights_h, hws_h = refs[:chunks], refs[chunks:2 * chunks]
    (send_h, keep_h, gm_h, gv_h, uw_h, gst_h, vec_o,
     cot, middle, wo, vec, f, state, left, ghs, hws, e_s, gm_s, gatt, right, uw_o, gst_o, stage, sems) = refs[2 * chunks:]
    move = Mover(sems)
    rows, d = middle.shape
    shards = ghs.shape[1]
    loads = [[move.load(rights_h[k].at[0], ghs.at[k]), move.load(hws_h[k], hws.at[k])] for k in range(chunks)]
    norm = [move.load(middle_h, middle), move.load(vec_h, vec), move.load(cot_h, cot)]
    more = [move.load(wo_h, wo), move.load(f_h, f), move.load(state_h, state)]
    last = move.load(trans_h, left)
    mols = molecules(zm, pm)
    for load in loads:
        for c in load:
            c.wait()
    for c in range(0, d, 256):
        cs = slice(c, c + 256)
        e_s[:, cs] = sum(dot_t(ghs[k, j], hws[k, j, cs, :]) for k in range(chunks) for j in range(shards))
    for c in norm:
        c.wait()
    gain2 = row(vec)[:, 6 * d:7 * d]
    acc_g = acc_s = acc_b = acc_c = 0.0
    for r in range(0, rows, 256):
        rs = slice(r, r + 256)
        e = e_s[rs, :]
        n, rate = norm_parts(middle[rs, :])
        c = cot[rs, :].astype(F32)
        acc_g += jnp.sum(e * n, axis=0, keepdims=True)
        acc_s += jnp.sum(e, axis=0, keepdims=True)
        acc_c += jnp.sum(c, axis=0, keepdims=True)
        eg = e * gain2
        gm = c + rate * (eg - jnp.mean(eg, axis=-1, keepdims=True) - n * jnp.mean(eg * n, axis=-1, keepdims=True))
        gm_s[rs, :] = gm
        gb = gm.astype(BF)
        right[0, rs, :] = gb
        acc_b += jnp.sum(gb.astype(F32), axis=0, keepdims=True)
    move.store(gm_s, gm_h)
    vec_o[0:1, :] = acc_g
    vec_o[1:2, :] = acc_s
    vec_o[2:3, :] = acc_b
    vec_o[3:4, :] = acc_c
    for c in more:
        c.wait()
    for c in range(0, d, 256):
        cs = slice(c, c + 256)
        gatt[:, cs] = dot_t(right[0], wo[cs, :])
    keep = block_mask(512)
    for g in range(d // 256):
        cs = slice(g * 256, (g + 1) * 256)
        fs = slice(g * 128, (g + 1) * 128)
        total = 0.0
        for i, (r, n) in enumerate(mols):
            ms = slice(r, r + n)
            st = state[i, g]
            q = f[0, ms, fs]
            nd = dot(q, st)
            rden = 1.0 / nd[:, 256:]
            u = gatt[ms, cs] * rden
            uw = jnp.concatenate([u, -(u * (nd[:, :256] * rden))], axis=1).astype(BF)
            uw_o[ms, slice(g * 512, (g + 1) * 512)] = uw
            gst = jnp.where(keep, dot_c(q, uw), 0.0).astype(BF)
            gst_o[i, g] = gst
            gv = dot(f[1, ms, fs], gst[:, :256]).astype(BF)
            right[1, ms, cs] = gv
            total += jnp.sum(gv.astype(F32), axis=0, keepdims=True)
        vec_o[4:5, cs] = total
    move.store(right.at[1], gv_h)
    move.store(uw_o, uw_h)
    move.store(gst_o, gst_h)
    last.wait()
    me = meta[0]
    products(move, pieces, (meta[3], meta[2]), stage, ((left.at[1 - me], right.at[1 - me], send_h), (left.at[me], right.at[me], keep_h)))
    move.finish()


def value_bwd(meta, zm, pm, pieces, rights, hws, cot, middle, wo, vec, f, state, trans, after=()):
    rows, d = middle.shape
    k = len(rights)
    shards, width = rights[0].shape[1], rights[0].shape[3]
    outs = [("h", S((d, d), BF))] * 2 + [("h", S((rows, d), F32)), ("h", S((rows, d), BF)), ("h", S((rows, 2 * d), BF)),
                                         ("h", S(state.shape, BF)), ("v", S((5, d), F32))]
    scratch = [VM((rows, d), BF), VM((rows, d), F32), VM((d, d), BF), VM(vec.shape, F32), VM(f.shape, BF), VM(state.shape, BF),
               VM((2, d, rows), BF), VM((k, shards, rows, width), BF), VM((k, shards, d, width), BF), VM((rows, d), F32),
               VM((rows, d), F32), VM((rows, d), F32), VM((2, rows, d), BF), VM((rows, 2 * d), BF), VM(state.shape, BF), VM((2, d, d), BF)]
    args = (meta, cot, middle, wo, vec, f, state, trans, *rights, *hws)
    return call(functools.partial(value_bwd_kernel, zm, pm, pieces, k), "value_bwd", args, "s" + "h" * (len(args) - 1), outs, scratch,
                20 + 2 * k, 2 * rows * d * (k * shards * width + 4 * d), 12 * MIB, None, after)


def query_bwd_kernel(zm, pm, pieces, meta, uw_h, gst_h, qkv_h, f_h, state_h, trans_h, proj_h, energy_h, table_h,
                     gv_h, wq_h, wk_h, wv_h, x_h, gm_h, vec_h,
                     send_h, keep_h, out_h, vec_o, uw, gst, qkv, f, state, n1t, proj, energy, table,
                     gv, wq, wk, wv, x, gm, vec, gqk, e_s, out_s, stage, sems):
    move = Mover(sems)
    loads = [move.load(s, t) for s, t in (
        (uw_h, uw), (state_h, state), (f_h, f), (proj_h.at[0], proj), (energy_h, energy), (table_h, table), (qkv_h, qkv), (gst_h, gst))]
    later = [move.load(trans_h.at[1], n1t)]
    last = [move.load(s, t) for s, t in ((gv_h, gv), (wq_h, wq), (wk_h, wk), (wv_h, wv), (x_h, x), (gm_h, gm), (vec_h, vec))]
    mols = molecules(zm, pm)
    _, rows, d = qkv.shape
    for c in loads:
        c.wait()
    for g in range(d // 256):
        cs = slice(g * 256, (g + 1) * 256)
        fs = slice(g * 128, (g + 1) * 128)
        sums = [0.0, 0.0]
        for b in range(rows // PPAD):
            mem = members(mols, b)
            rs = slice(b * PPAD, (b + 1) * PPAD)
            gfq, gfk = [], []
            for i, r, n in mem:
                ms = slice(r, r + n)
                gfq.append(dot_t(uw[ms, slice(g * 512, (g + 1) * 512)], state[i, g]))
                gfk.append(dot_t(jnp.concatenate([qkv[2, ms, cs], jnp.ones((n, 256), BF)], axis=1), gst[i, g]))
            cosb, sinb = (jnp.concatenate([table[t, :n, :] for _, _, n in mem], axis=0) for t in range(2))
            cosb = jnp.concatenate([cosb, cosb], axis=1)
            sinb = jnp.concatenate([sinb, sinb], axis=1)
            for t, gf in enumerate((gfq, gfk)):
                gp = (jnp.concatenate(gf, axis=0) * f[t, rs, fs].astype(F32)).astype(BF)
                back = dot(gp, proj[g])
                tot = dot(gp, energy[...])
                grad = (cosb * back[:, :256] + sinb * back[:, 256:] - tot * qkv[t, rs, cs].astype(F32)).astype(BF)
                gqk[t, rs, cs] = grad
                sums[t] += jnp.sum(grad.astype(F32), axis=0, keepdims=True)
        for t in range(2):
            vec_o[t:t + 1, cs] = sums[t]
    for c in later:
        c.wait()
    me = meta[0]
    products(move, pieces, (meta[3], meta[2]), stage, ((n1t, gqk.at[1 - me], send_h), (n1t, gqk.at[me], keep_h)))
    for c in last:
        c.wait()
    for c in range(0, d, 256):
        cs = slice(c, c + 256)
        e_s[:, cs] = dot_t(gqk[0], wq[cs, :]) + dot_t(gqk[1], wk[cs, :]) + dot_t(gv[...], wv[cs, :])
    gain = row(vec)[:, :d]
    acc_g = acc_s = 0.0
    for r in range(0, rows, 256):
        rs = slice(r, r + 256)
        e = e_s[rs, :]
        n, rate = norm_parts(x[rs, :].astype(F32))
        acc_g += jnp.sum(e * n, axis=0, keepdims=True)
        acc_s += jnp.sum(e, axis=0, keepdims=True)
        eg = e * gain
        gx = rate * (eg - jnp.mean(eg, axis=-1, keepdims=True) - n * jnp.mean(eg * n, axis=-1, keepdims=True))
        out_s[rs, :] = (gm[rs, :] + gx).astype(BF)
    move.store(out_s, out_h)
    vec_o[2:3, :] = acc_g
    vec_o[3:4, :] = acc_s
    move.finish()


def query_bwd(meta, zm, pm, pieces, uw, gst, qkv, f, state, trans, proj, table, gv, wq, wk, wv, x, gm, vec, after=()):
    _, rows, d = qkv.shape
    outs = [("h", S((d, d), BF))] * 2 + [("h", S((rows, d), BF)), ("v", S((4, d), F32))]
    scratch = [VM(uw.shape, BF), VM(gst.shape, BF), VM(qkv.shape, BF), VM(f.shape, BF), VM(state.shape, BF), VM((d, rows), BF),
               VM(proj.shape[1:], BF), VM((128, 256), BF), VM(table.shape, F32), VM((rows, d), BF)] + [VM((d, d), BF)] * 3 + [
               VM((rows, d), BF), VM((rows, d), F32), VM(vec.shape, F32), VM((2, rows, d), BF), VM((rows, d), F32), VM((rows, d), BF),
               VM((2, d, d), BF)]
    args = (meta, uw, gst, qkv, f, state, trans, proj, head_const(64 ** -0.5), table, gv, wq, wk, wv, x, gm, vec)
    return call(functools.partial(query_bwd_kernel, zm, pm, pieces), "query_bwd", args, "s" + "h" * (len(args) - 1), outs, scratch,
                24, 2 * d**3 * 6, 12 * MIB, None, after)


def layer_kernel(chunks, middle_h, vec_h, *refs):
    rights_h, rws_h = refs[:chunks], refs[chunks:2 * chunks]
    out_h, acts, rws, middle, vec, out_s, sems = refs[2 * chunks:]
    move = Mover(sems)
    loads = []
    for k in range(chunks):
        loads += [move.load(rights_h[k].at[1], acts.at[k]), move.load(rws_h[k], rws.at[k])]
    loads += [move.load(middle_h, middle), move.load(vec_h, vec)]
    for c in loads:
        c.wait()
    d = middle.shape[1]
    for c in range(0, d, 256):
        cs = slice(c, c + 256)
        total = sum(dot(acts[k, j], rws[k, j, :, cs]) for k in range(chunks) for j in range(acts.shape[1]))
        out_s[:, cs] = (middle[:, cs] + total + row(vec)[:, 8 * d + c:8 * d + c + 256]).astype(BF)
    move.store(out_s, out_h)
    move.finish()


def layer_end(rights, rws, middle, vec, after=()):
    rows, d = middle.shape
    k = len(rights)
    shards, width = rights[0].shape[1], rights[0].shape[3]
    scratch = [VM((k, shards, rows, width), BF), VM((k, shards, width, d), BF), VM((rows, d), F32), VM(vec.shape, F32), VM((rows, d), BF)]
    args = (middle, vec, *rights, *rws)
    return call(functools.partial(layer_kernel, k), "layer_end", args, "h" * len(args),
                [("h", S((rows, d), BF))], scratch, 4 + 2 * k, 2 * rows * d * k * shards * width, 12 * MIB, None, after)[0]


def placed(ref, p, code, pieces):
    step = ref.shape[0] // pieces
    return ref[pl.ds(pl.multiple_of(jnp.bitwise_xor(p, code) * step, 16), step), :]


def finish_ffn_kernel(pieces, k, meta, m0, m1, t0, t1, *refs):
    ghw_h, grw_h, both, whole, wide, tall, sems = refs[-7:]
    move = Mover(sems)
    me, code = meta[0], meta[1]
    d, width = wide.shape
    half = d // 2
    for c in [move.load(m0, both.at[me, :half]), move.load(m1, both.at[me, half:]),
              move.load(t0, both.at[1 - me, :half]), move.load(t1, both.at[1 - me, half:])]:
        c.wait()
    step = d // pieces
    for p in range(pieces):
        whole[p * step:(p + 1) * step, :] = placed(both.at[1], p, code, pieces)
    for c in range(0, width, 128):
        cs = slice(c, c + 128)
        tall[cs, :] = whole[:, cs].T.astype(F32)
    move.store(tall, grw_h.at[k * width:(k + 1) * width])
    for p in range(pieces):
        wide[p * step:(p + 1) * step, :] = placed(both.at[0], p, code, pieces).astype(F32)
    move.store(wide, ghw_h.at[:, k * width:(k + 1) * width])
    move.finish()


def finish_ffn(meta, pieces, parts, k, shard, before):
    d, width = 2 * parts[0].shape[0], parts[0].shape[1]
    args = (meta, *parts)
    return call(functools.partial(finish_ffn_kernel, pieces, k), "finish_ffn", args + tuple(before), "s" + "h" * (4 + len(before)),
                [("h", S((d, shard), F32)), ("h", S((shard, d), F32))],
                [VM((2, d, width), BF), VM((d, width), BF), VM((d, width), F32), VM((width, d), F32)],
                8, 0, 4 * MIB, {len(args) + i: i for i in range(len(before))})


def finish_pair_kernel(pieces, meta, m0, m1, t0, t1, first_h, second_h, both, wide, sems):
    move = Mover(sems)
    me = meta[0]
    d = wide.shape[1]
    half = d // 2
    for c in [move.load(m0, both.at[me, :half]), move.load(m1, both.at[me, half:]),
              move.load(t0, both.at[1 - me, :half]), move.load(t1, both.at[1 - me, half:])]:
        c.wait()
    step = d // pieces
    for t, out in enumerate((first_h, second_h)):
        code = jnp.where(me == t, meta[2], meta[3])
        for p in range(pieces):
            wide[t, p * step:(p + 1) * step, :] = placed(both.at[t], p, code, pieces).astype(F32)
        move.store(wide.at[t], out)
    move.finish()


def finish_pair(meta, pieces, parts, d):
    return call(functools.partial(finish_pair_kernel, pieces), "finish_pair", (meta, *parts), "shhhh",
                [("h", S((d, d), F32))] * 2, [VM((2, d, d), BF), VM((2, d, d), F32)], 8, 0, 4 * MIB)


def bits_below(size):
    return [1 << i for i in range(size.bit_length() - 1)]


class Layout:
    def __init__(self, mesh):
        self.nb, self.nt = mesh.shape["batch"], mesh.shape["tp"]
        self.tp = [("tp", b) for b in reversed(bits_below(self.nt))]
        self.batch = [("batch", b) for b in bits_below(self.nb)[1:]]
        self.lanes = (self.tp + self.batch, self.batch[:1] + self.tp + self.batch[1:])

    def partner(self, device, level):
        b, t = divmod(device, self.nt)
        axis, bit = level
        return (b ^ bit) * self.nt + t if axis == "batch" else b * self.nt + (t ^ bit)

    def swap(self, value, level):
        pairs = []
        for device in range(self.nb * self.nt):
            core = device // self.nt % 2
            pairs.append((device, self.partner(device, self.lanes[core][level] if isinstance(level, int) else level)))
        return lax.ppermute(value, ("batch", "tp"), pairs)


CORE = ("batch", 1)


def code_of(levels, place):
    out = jnp.int32(0)
    for axis, bit in levels:
        out = out * 2 + (place[axis] // bit) % 2
    return out


def add(a, b):
    return (a.astype(F32) + b.astype(F32)).astype(BF)


def scatter_levels(levels, rows, least=48):
    n = 0
    while n < len(levels) and rows % 32 == 0 and rows // 2 >= least:
        rows //= 2
        n += 1
    return n


class Chain:
    def __init__(self, lay, steps):
        self.lay, self.steps, self.result = lay, steps, None
        self.go(next(steps))

    def go(self, requests):
        self.sent = [v for v, _ in requests]
        self.here = [self.lay.swap(v, level) for v, level in requests]

    def step(self):
        try:
            self.go(self.steps.send(self.here))
        except StopIteration as end:
            self.result, self.sent, self.here = end.value, [], []
        return self


def fence(arrays, *chains):
    arrays, held = lax.optimization_barrier((arrays, [c.here for c in chains]))
    for chain, here in zip(chains, held):
        chain.here = here
        chain.step()
    return arrays


def sent(*chains):
    return tuple(v for c in chains for v in c.sent)


def halving(a, b, levels):
    for level in levels:
        n = a.shape[0] // 2
        kept = add(a[:n], b[:n])
        (b,) = yield [(add(a[n:], b[n:]), level)]
        a = kept
    return a, b


def doubling(held, levels):
    for level in levels:
        (got,) = yield [(held, level)]
        held = jnp.concatenate([held, got], axis=0)
    return held


def spread(held, level):
    other, mine = yield [(held, level), (held, CORE)]
    (rest,) = yield [(other, CORE)]
    return held, other, mine, rest


def reduce_ffn(lay, send, keep):
    (recv,) = yield [(send, CORE)]
    a, b = yield from halving(keep, recv, range(len(lay.lanes[0])))
    held = yield from doubling(add(a, b), reversed(lay.batch[1:]))
    return (yield from spread(held, lay.batch[0]))


def reduce_pair(lay, n, send, keep):
    (recv,) = yield [(send, CORE)]
    a, b = yield from halving(keep, recv, range(n))
    held = add(a, b)
    for level in range(n, len(lay.lanes[0])):
        (got,) = yield [(held, level)]
        held = add(held, got)
    held = yield from doubling(held, reversed(range(1, n)))
    return (yield from spread(held, 0))


def reduce_small(lay, vectors, hidden):
    n, shard = vectors.shape[0], hidden[0].shape[0]
    for level in lay.tp:
        bit = level[1]
        (got,) = yield [(jnp.concatenate([vectors] + [hidden[j + bit] for j in range(bit)]), level)]
        vectors = vectors + got[:n]
        hidden = [hidden[j] + got[n + j * shard:n + (j + 1) * shard] for j in range(bit)]
    held = jnp.concatenate([vectors, hidden[0]])
    for level in [CORE] + lay.batch:
        (got,) = yield [(held, level)]
        held = held + got
    return held


def on_device(
    lay,
    inputs,
    cotangent,
    zinc_lengths,
    pubchem_lengths,
    feature_stack,
    train_step,
    redraw_interval,
    attn_gain,
    attn_shift,
    query_weight,
    query_bias,
    key_weight,
    key_bias,
    value_weight,
    value_bias,
    output_weight,
    output_bias,
    ffn_gain,
    ffn_shift,
    hidden_weight,
    hidden_bias,
    return_weight,
    return_bias,
):
    nt = lay.nt
    d, shard = hidden_weight.shape
    rows = inputs.shape[0]
    width = min(768, shard)
    chunks = shard // width
    zm, pm = zinc_lengths.shape[0], pubchem_lengths.shape[0]
    place = {"batch": lax.axis_index("batch"), "tp": lax.axis_index("tp")}
    core, quarter = place["batch"] % 2, place["batch"] % 4
    x = lay.batch[0]

    pools = []
    for k in range(chunks):
        hw = lax.dynamic_slice(hidden_weight, (quarter * (d // 4), k * width), (d // 4, width))
        rw = lax.dynamic_slice(return_weight, (k * width + quarter * (width // 4), 0), (width // 4, d))
        pool = {0: [jnp.concatenate([hw, rw], axis=0)] if width == d else [hw, rw]}
        for level in lay.tp:
            for j in list(pool):
                pool[j | level[1]] = [lay.swap(v, level) for v in pool[j]]
        pools.append(pool)
    biases = {0: hidden_bias}
    for level in lay.tp:
        for j in list(biases):
            biases[j | level[1]] = lay.swap(biases[j], level)
    others = range(1, nt)

    n_pair = scatter_levels(lay.lanes[0], d)
    codes = [code_of(lane[:n_pair], place) for lane in lay.lanes]
    meta = jnp.concatenate([jnp.stack([
        core, code_of(lay.batch, place), jnp.where(core == 0, codes[0], codes[1]), jnp.where(core == 0, codes[1], codes[0]), quarter,
    ]).astype(jnp.int32), zinc_lengths, pubchem_lengths])
    vec = jnp.concatenate([attn_gain, attn_shift, query_bias, key_bias, value_bias, output_bias, ffn_gain, ffn_shift, return_bias])
    pick = train_step[0] // redraw_interval[0] % feature_stack.shape[0]
    proj = projection_blocks(lax.dynamic_index_in_dim(feature_stack, pick, 0, keepdims=False))
    table = rotary_const()

    attend = (meta, 5, zm, pm, cotangent, inputs, vec, query_weight, key_weight, value_weight, output_weight, proj, table)
    early = attend_fwd((0,), (), (), *attend)
    per = len(pools[0][0])
    here = [[v for j in others for v in pool[j]] for pool in pools]
    near, far, last = [None] * chunks, [None] * chunks, [None] * chunks

    def over(k):
        far[k] = [lay.swap(v, x) for v in here[k]]
        near[k] = [lay.swap(v, CORE) for v in here[k]]

    here[0], early = lax.optimization_barrier((here[0], early))
    over(0)
    late = attend_fwd(tuple(range(1, rows // PPAD)), early, (), *attend)
    here[1:], far[0], near[0], (qkv, f, state, trans, middle, n2, left) = lax.optimization_barrier((here[1:], far[0], near[0], late))

    chains, rights, hws, rws, hidden = [], [], [], [], []
    for k in range(chunks):
        last[k] = [lay.swap(v, CORE) for v in far[k]]
        if k + 1 < chunks:
            over(k + 1)
        if chains:
            last[k] = fence(last[k], chains[-1])
        parts = [[v[k][i] for i in range((j - 1) * per, j * per) for v in (here, near, far, last)] for j in others]
        out = ffn_chunk(
            meta, 2 ** len(lay.batch), nt, n2, left, cotangent, hidden_bias, hidden_weight, return_weight, parts,
            [biases[j] for j in others], k, chunks, width, sent(*chains))
        if k + 1 < chunks:
            out, far[k + 1], near[k + 1] = lax.optimization_barrier((out, far[k + 1], near[k + 1]))
        send, keep, right, bias, hw, rw = fence(out, *chains)
        chains.append(Chain(lay, reduce_ffn(lay, send, keep)))
        rights.append(right)
        hws.append(hw)
        rws.append(rw)
        hidden.append(bias)
    layer_out = layer_end(rights, rws, middle, vec, sent(*chains))
    layer_out, cotangent = fence((layer_out, cotangent), *chains)
    out = value_bwd(
        meta, zm, pm, 2 ** n_pair, rights, hws, cotangent, middle, output_weight, vec, f, state, trans, sent(*chains))
    send_a, keep_a, gm, gv, uw, gst, vec1 = fence(out, *chains)
    pair_a = Chain(lay, reduce_pair(lay, n_pair, send_a, keep_a))
    out = query_bwd(
        meta, zm, pm, 2 ** n_pair, uw, gst, qkv, f, state, trans, proj, table, gv, query_weight, key_weight, value_weight,
        inputs, gm, vec, sent(*chains))
    send_b, keep_b, input_grad, vec2 = fence(out, pair_a, *chains)
    pair_b = Chain(lay, reduce_pair(lay, n_pair, send_b, keep_b))
    vectors = jnp.concatenate([vec1, vec2], axis=0).reshape(-1)
    small = Chain(lay, reduce_small(lay, vectors, [jnp.concatenate([hidden[k][j] for k in range(chunks)]) for j in range(nt)]))

    every = [pair_b, small, pair_a] + chains
    while any(c.result is None for c in every):
        fence((), *(c for c in every if c.result is None))
    vecs = small.result[:9 * d].reshape(9, d)
    ffn_out = ()
    for k in range(chunks):
        ffn_out = finish_ffn(meta, 2 ** len(lay.batch), chains[k].result, k, shard, ffn_out)
    gwo, gwv = finish_pair(meta, 2 ** n_pair, pair_a.result, d)
    gwq, gwk = finish_pair(meta, 2 ** n_pair, pair_b.result, d)
    return (layer_out, input_grad, vecs[7], vecs[8], gwq, vecs[5], gwk, vecs[6], gwv, vecs[4], gwo, vecs[2],
            vecs[0], vecs[1], ffn_out[0], small.result[9 * d:], ffn_out[1], vecs[3])


def solution(mesh):
    rows, whole, hidden = P(("batch", "tp"), None), P(), P(None, "tp")
    return jax.shard_map(
        functools.partial(on_device, Layout(mesh)),
        mesh=mesh,
        in_specs=(rows, rows, P(("batch", "tp")), P(("batch", "tp"))) + (whole,) * 15 + (hidden, P("tp"), P("tp", None), whole),
        out_specs=(rows, rows) + (whole,) * 12 + (hidden, P("tp"), P("tp", None), whole),
        check_vma=False,
    )
```

```python
import functools
import math

import jax
import jax.numpy as jnp
import numpy as np
from jax import lax
from jax.experimental import pallas as pl
from jax.experimental.pallas import tpu as pltpu
from jax.sharding import PartitionSpec as P

ZPAD = 64
PPAD = 256
F32 = jnp.float32
BF = jnp.bfloat16
VM = pltpu.VMEM
GROUP = 4
S = jax.ShapeDtypeStruct
TIMES = {"attend_fwd": 24, "ffn_chunk": 17, "layer_end": 9, "mid": 13, "value_bwd": 13, "query_bwd": 13, "input_back": 10, "finish_ffn": 5, "finish_pair": 5}
MIB = 2**20
GRANT = 60


def dot(a, b):
    return jnp.dot(a, b, preferred_element_type=F32)


def dot_t(a, b):
    return lax.dot_general(a, b, (((1,), (1,)), ((), ())), preferred_element_type=F32)


def dot_c(a, b):
    return lax.dot_general(a, b, (((0,), (0,)), ((), ())), preferred_element_type=F32)


def split(v):
    hi = v.astype(BF)
    return hi, (v - hi.astype(F32)).astype(BF)


def norm_parts(values):
    center = values - jnp.mean(values, axis=-1, keepdims=True)
    rate = lax.rsqrt(jnp.mean(center * center, axis=-1, keepdims=True) + 1e-05)
    return center * rate, rate


def row(ref):
    return ref[...].reshape(1, -1)


def block_mask(width):
    f = lax.broadcasted_iota(jnp.int32, (128, width), 0) // 32
    c = lax.broadcasted_iota(jnp.int32, (128, width), 1) % 256 // 64
    return f == c


def molecules(zm, pm):
    return [(i * ZPAD, ZPAD) for i in range(zm)] + [(zm * ZPAD + i * PPAD, PPAD) for i in range(pm)]


def members(mols, b):
    return [(i, r, n) for i, (r, n) in enumerate(mols) if b * PPAD <= r < (b + 1) * PPAD]


class Mover:
    def __init__(self, sems):
        self.sems, self.n, self.out = sems, 0, []

    def load(self, src, dst):
        copy = pltpu.make_async_copy(src, dst, self.sems.at[self.n])
        self.n += 1
        copy.start()
        return copy

    def store(self, src, dst):
        self.out.append(self.load(src, dst))

    def finish(self):
        for copy in self.out:
            copy.wait()


def call(kernel, name, args, spaces, outs, scratch, copies, flops, moved, aliases=None, after=()):
    n, extra = len(args), len(after)

    def body(*refs):
        kernel(*refs[:n], *refs[n + extra:])

    spec = {
        "v": pl.BlockSpec(memory_space=VM),
        "h": pl.BlockSpec(memory_space=pltpu.HBM),
        "s": pl.BlockSpec(memory_space=pltpu.SMEM),
    }
    return pl.pallas_call(
        body,
        out_shape=tuple(o for _, o in outs),
        in_specs=[spec[s] for s in spaces] + [spec["h"]] * extra,
        out_specs=tuple(spec[s] for s, _ in outs),
        scratch_shapes=list(scratch) + [pltpu.SemaphoreType.DMA((copies,))],
        input_output_aliases=aliases or {},
        compiler_params=pltpu.CompilerParams(vmem_limit_bytes=GRANT * MIB),
        cost_estimate=pl.CostEstimate(flops=int(TIMES[name] * 1.15e9), bytes_accessed=moved, transcendentals=0),
        name=name,
    )(*args, *after)


def place_heads(scaled):
    two = jnp.concatenate([scaled, scaled], axis=1)
    return jnp.where(block_mask(256), jnp.concatenate([two, two], axis=1), 0.0)


def attend_fwd_kernel(zm, pm, meta, zlen, plen, cot_h, x_h, gain_h, shift_h, bq_h, bk_h, bv_h, bo_h, gain2_h, shift2_h,
                      wq_h, wk_h, wv_h, wo_h, stack_h, table_h, energy_h,
                      qkv_h, f_h, state_h, trans_h, middle_h, n2_h, left_h, proj_h,
                      cot, n2_s, left, x, vec, wq, wk, wv, wo, fp, proj, table, energy, qkv, f_s, state_s, trans, middle_s, att_s, sems):
    move = Mover(sems)
    rows, d = x.shape
    first = [move.load(x_h, x), move.load(gain_h, vec.at[0]), move.load(shift_h, vec.at[1]), move.load(stack_h.at[meta[5]], fp),
             move.load(cot_h, cot)]
    later = [move.load(s, t) for s, t in ((wq_h, wq), (bq_h, vec.at[2]), (table_h, table), (energy_h, energy), (wk_h, wk),
                                          (bk_h, vec.at[3]), (wv_h, wv), (bv_h, vec.at[4]))]
    last = [move.load(s, t) for s, t in ((wo_h, wo), (bo_h, vec.at[5]), (gain2_h, vec.at[6]), (shift2_h, vec.at[7]))]
    mols = molecules(zm, pm)
    groups = d // 256
    blocks = range(rows // PPAD)
    keep = block_mask(512)
    ones = jnp.ones((PPAD, 256), BF)

    def vector(i):
        return vec[i].reshape(1, -1)

    for c in first:
        c.wait()
    for g in range(groups):
        p = fp[g * GROUP:(g + 1) * GROUP].reshape(GROUP * 32, 64) * 64 ** -0.25
        turned = jnp.concatenate([p[:, 32:], -p[:, :32]], axis=1)
        hi, lo = split(jnp.concatenate([place_heads(p), place_heads(turned)], axis=1))
        proj[0, g] = hi
        proj[1, g] = lo
    n1s = {}
    for b in blocks:
        rs = slice(b * PPAD, (b + 1) * PPAD)
        normed, _ = norm_parts(x[rs, :].astype(F32))
        n1s[b] = (normed * vector(0) + vector(1)).astype(BF)
        trans[1, :, rs] = n1s[b].T
        left[1, :, rs] = cot[rs, :].T
    for c in later:
        c.wait()
    move.store(proj.at[0], proj_h)
    move.store(trans.at[1], trans_h.at[1])
    move.store(left.at[1], left_h.at[1])
    for b in blocks:
        mem = members(mols, b)
        rs = slice(b * PPAD, (b + 1) * PPAD)
        n1 = n1s[b]
        cosb, sinb = (jnp.concatenate([table[t, :n, :] for _, _, n in mem], axis=0) for t in range(2))
        cosb = jnp.concatenate([cosb, cosb], axis=1)
        sinb = jnp.concatenate([sinb, sinb], axis=1)
        live = jnp.concatenate(
            [(lax.broadcasted_iota(jnp.int32, (n, 128), 0) < (zlen[i] if i < zm else plen[i - zm])).astype(F32) for i, r, n in mem], axis=0)
        for g in range(groups):
            cs = slice(g * 256, (g + 1) * 256)
            fs = slice(g * 128, (g + 1) * 128)

            def features(w, bias, slot):
                v = dot(n1, w[:, cs]) + vector(bias)[:, cs]
                qkv[slot, rs, cs] = v.astype(BF)
                ch, cl = split(v * cosb)
                sh, sl = split(v * sinb)
                eh, el = split(v * v)
                ph, plo = proj[0, g], proj[1, g]
                e = energy[...]
                inner = (dot_t(ch, ph[:, :256]) + dot_t(sh, ph[:, 256:]) + dot_t(cl, ph[:, :256]) + dot_t(sl, ph[:, 256:])
                         + dot_t(ch, plo[:, :256]) + dot_t(sh, plo[:, 256:]) - dot_t(eh, e) - dot_t(el, e))
                return jnp.exp(inner) * (32 ** -0.5)

            fq = features(wq, 2, 0).astype(BF)
            fk = (features(wk, 3, 1) * live).astype(BF)
            f_s[0, rs, fs] = fq
            f_s[1, rs, fs] = fk
            v = (dot(n1, wv[:, cs]) + vector(4)[:, cs]).astype(BF)
            qkv[2, rs, cs] = v
            for i, r, n in mem:
                ms = slice(r - b * PPAD, r - b * PPAD + n)
                vo = jnp.concatenate([v[ms], ones[:n]], axis=1)
                state = jnp.where(keep, dot_c(fk[ms], vo), 0.0).astype(BF)
                state_s[i, g] = state
                nd = dot(fq[ms], state)
                att_s[r:r + n, cs] = (nd[:, :256] / nd[:, 256:]).astype(BF)
    for s, t in ((qkv, qkv_h), (f_s, f_h), (state_s, state_h)):
        move.store(s, t)
    for c in last:
        c.wait()
    for b in blocks:
        rs = slice(b * PPAD, (b + 1) * PPAD)
        trans[0, :, rs] = att_s[rs, :].T
        middle = x[rs, :].astype(F32) + (dot(att_s[rs, :], wo[...]) + vector(5))
        middle_s[rs, :] = middle
        normed, _ = norm_parts(middle)
        n2 = (normed * vector(6) + vector(7)).astype(BF)
        n2_s[rs, :] = n2
        left[0, :, rs] = n2.T
    move.store(middle_s, middle_h)
    move.store(n2_s, n2_h)
    move.store(trans.at[0], trans_h.at[0])
    move.store(left.at[0], left_h.at[0])
    move.finish()


def rotary_const():
    place = np.arange(PPAD, dtype=np.float64)
    rates = np.exp(np.arange(32, dtype=np.float64) * (-2.0 * math.log(10000.0) / 64))
    ang = place[:, None] * rates[None, :]
    return np.tile(np.stack([np.cos(ang), np.sin(ang)]), (1, 1, 4)).astype(np.float32)


def head_const(scale):
    f = np.arange(128)[:, None] // 32
    c = np.arange(256)[None, :] // 64
    return ((f == c) * scale).astype(jnp.bfloat16)


def attend_fwd(meta, zlen, plen, cot, x, vectors, wq, wk, wv, wo, stack, table):
    rows, d = x.shape
    zm, pm = zlen.shape[0], plen.shape[0]
    groups = d // 256
    states = (zm + pm, groups, 128, 512)
    outs = [S((3, rows, d), BF), S((2, rows, d // 2), BF), S(states, BF), S((2, d, rows), BF),
            S((rows, d), F32), S((rows, d), BF), S((2, d, rows), BF), S((groups, 128, 512), BF)]
    args = (meta, zlen, plen, cot, x, *vectors, wq, wk, wv, wo, stack, table, head_const(1 / 16))
    scratch = ([VM((rows, d), BF)] * 2 + [VM((2, d, rows), BF), VM((rows, d), BF), VM((8, d), F32)] + [VM((d, d), BF)] * 4
               + [VM(stack.shape[1:], F32), VM((2, groups, 128, 512), BF), VM(table.shape, F32), VM((128, 256), BF)]
               + [VM((3, rows, d), BF), VM((2, rows, d // 2), BF), VM(states, BF), VM((2, d, rows), BF), VM((rows, d), F32), VM((rows, d), BF)])
    return call(
        functools.partial(attend_fwd_kernel, zm, pm), "attend_fwd", args, "sss" + "h" * (len(args) - 3),
        [("h", o) for o in outs], scratch, 32, 2 * rows * d * d * 4, 16 * MIB)


def gelu_parts(h):
    bell = jnp.exp(h * h * -0.5)
    t = 1.0 / (1.0 + (0.3275911 * math.sqrt(0.5)) * jnp.abs(h))
    poly = t * (0.127414796 + t * (-0.142248368 + t * (0.7107068705 + t * (-0.7265760135 + t * 0.5307027145))))
    tail = poly * bell
    phi = jnp.where(h >= 0, 1.0 - tail, tail)
    return h * phi, phi + h * bell * (1.0 / math.sqrt(2 * math.pi))


def place_pieces(code, src, dst):
    n, step = src.shape[0], src.shape[1]
    for p in range(n):
        off = pl.multiple_of(jnp.bitwise_xor(p, code) * step, 16)
        dst[pl.ds(off, step), :] = src[p]


def ffn_kernel(pieces, shards, k, per, meta, n2_h, left_h, cot_h, hb_h, hw_h, rw_h, *refs):
    parts = {j: refs[(j - 1) * per:j * per] for j in range(1, shards)}
    hbs = refs[(shards - 1) * per:(shards - 1) * (per + 1)]
    (gone_h, stay_h, keep_h, right_h, bias_o, hws_h, rws_h, n2, left, cot, hb, hw, rw, hw2, rw2, right, stage, sems) = refs[-18:]
    move = Mover(sems)
    d, width = hw.shape[1:]
    half_d = d // 2
    me, code = meta[0], meta[1]
    order = list(range(1, shards)) + [0]
    early, late = {}, {}
    for j in order:
        early[j] = [move.load(hbs[j - 1] if j else hb_h, hb.at[j])]
        if j == order[0]:
            early[j].append(move.load(n2_h, n2))
        late[j] = []
        if j == 0:
            early[j].append(move.load(hw_h.at[:, k * width:(k + 1) * width], hw.at[0]))
            late[j].append(move.load(rw_h.at[k * width:(k + 1) * width, :], rw.at[0]))
        elif per == 2:
            early[j] += [move.load(parts[j][p].at[:half_d], hw2.at[j - 1, p]) for p in range(2)]
            late[j] += [move.load(parts[j][p].at[half_d:], rw2.at[j - 1, p]) for p in range(2)]
        else:
            early[j] += [move.load(parts[j][p], hw2.at[j - 1, p]) for p in range(2)]
            late[j] += [move.load(parts[j][2 + p], rw2.at[j - 1, p]) for p in range(2)]
        if j == order[0]:
            late[j].append(move.load(cot_h, cot))
    last = move.load(left_h, left)
    step, half = d // pieces, pieces // 2
    tile = 256 if width % 256 == 0 else 128
    for j in order:
        for c in early[j] + late[j]:
            c.wait()
        if j:
            place_pieces(me, hw2.at[j - 1], hw.at[j])
            place_pieces(me, rw2.at[j - 1], rw.at[j])
        bias = hb[j].reshape(1, -1)[:, k * width:(k + 1) * width].astype(F32)
        for c in range(0, width, tile):
            cs = slice(c, c + tile)
            h = dot(n2[...], hw[j, :, cs]) + bias[:, cs]
            act, slope = gelu_parts(h)
            ga = dot_t(cot[...], rw[j, cs, :])
            gh = (ga * slope).astype(BF)
            right[0, j, :, cs] = gh
            right[1, j, :, cs] = act.astype(BF)
            bias_o[j:j + 1, cs] = jnp.sum(gh.astype(F32), axis=0, keepdims=True)
        move.store(right.at[:, j], right_h.at[:, j])
        move.store(hw.at[j], hws_h.at[j])
        move.store(rw.at[j], rws_h.at[j])
    last.wait()
    for kind, slot in ((1 - me, 0), (me, 1)):
        for j in order:
            for c in range(0, width, tile):
                cs = slice(c, c + tile)
                value = dot(left[kind], right[kind, j, :, cs]).astype(BF)
                for p in range(pieces):
                    rel = jnp.bitwise_xor(p, code)
                    second = rel // half * (shards * half) + j * half + rel % half
                    off = pl.multiple_of(jnp.where(kind == 0, j * pieces + rel, second) * step, 16)
                    stage[slot, pl.ds(off, step), cs] = value[p * step:(p + 1) * step]
        if slot:
            move.store(stage.at[1], keep_h)
        else:
            cut = shards * d // 2
            move.store(stage.at[0, cut:], gone_h)
            move.store(stage.at[0, :cut], stay_h)
    move.finish()


def ffn_chunk(meta, pieces, shards, n2, left, cot, hb, hw, rw, parts, hbs, k, width, after=()):
    rows, d = n2.shape
    per = len(parts[0])
    part = S((shards * d // 2, width), BF)
    outs = [("h", part), ("h", part), ("h", S((shards * d, width), BF)), ("h", S((2, shards, rows, width), BF)), ("v", S((shards, width), F32)),
            ("h", S((shards, d, width), BF)), ("h", S((shards, width, d), BF))]
    scratch = [VM((rows, d), BF), VM((2, d, rows), BF), VM((rows, d), BF), VM((shards, 1) + hb.shape, BF), VM((shards, d, width), BF),
               VM((shards, width, d), BF), VM((shards - 1, 2, d // 2, width), BF), VM((shards - 1, 2, width // 2, d), BF),
               VM((2, shards, rows, width), BF), VM((2, shards * d, width), BF)]
    args = (meta, n2, left, cot, hb.reshape(1, -1), hw, rw) + tuple(p for part in parts for p in part) + tuple(b.reshape(1, -1) for b in hbs)
    return call(
        functools.partial(ffn_kernel, pieces, shards, k, per), "ffn_chunk", args,
        "s" + "h" * (len(args) - 1), outs, scratch, 10 + 13 * shards, 2 * rows * d * width * 4 * shards, 12 * MIB, None, after)


def products(move, pieces, codes, stage, outs):
    for slot, (left, right, out) in enumerate(outs):
        d = out.shape[0]
        step = d // pieces
        for c in range(0, d, 256):
            cs = slice(c, c + 256)
            value = dot(left[...], right[:, cs]).astype(BF)
            for p in range(pieces):
                off = pl.multiple_of(jnp.bitwise_xor(p, codes[slot]) * step, 16)
                stage[slot, pl.ds(off, step), cs] = value[p * step:(p + 1) * step]
        move.store(stage.at[slot], out)


def mid_kernel(chunks, cot_h, middle_h, wo_h, vec_h, *refs):
    rights_h, hws_h = refs[:chunks], refs[chunks:2 * chunks]
    gm_h, gb_h, gatt_h, vec_o, cot, middle, wo, vec, ghs, hws, e_s, gm_s, gb_s, gatt, sems = refs[2 * chunks:]
    move = Mover(sems)
    rows, d = middle.shape
    shards = ghs.shape[1]
    loads = [[(move.load(rights_h[k].at[0, j], ghs.at[k, j]), move.load(hws_h[k].at[j], hws.at[k, j])) for j in range(shards)]
             for k in range(chunks)]
    norm = [move.load(middle_h, middle), move.load(vec_h, vec), move.load(cot_h, cot)]
    last = move.load(wo_h, wo)
    for k in range(chunks):
        for j in range(shards):
            for c in loads[k][j]:
                c.wait()
            for c in range(0, d, 256):
                cs = slice(c, c + 256)
                part = dot_t(ghs[k, j], hws[k, j, cs, :])
                e_s[:, cs] = e_s[:, cs] + part if k or j else part
    for c in norm:
        c.wait()
    gain2 = row(vec)
    acc_g = acc_s = acc_b = acc_c = 0.0
    for r in range(0, rows, 256):
        rs = slice(r, r + 256)
        e = e_s[rs, :]
        n, rate = norm_parts(middle[rs, :])
        c = cot[rs, :].astype(F32)
        acc_g += jnp.sum(e * n, axis=0, keepdims=True)
        acc_s += jnp.sum(e, axis=0, keepdims=True)
        acc_c += jnp.sum(c, axis=0, keepdims=True)
        eg = e * gain2
        gm = c + rate * (eg - jnp.mean(eg, axis=-1, keepdims=True) - n * jnp.mean(eg * n, axis=-1, keepdims=True))
        gm_s[rs, :] = gm
        gb = gm.astype(BF)
        gb_s[rs, :] = gb
        acc_b += jnp.sum(gb.astype(F32), axis=0, keepdims=True)
    for i, acc in enumerate((acc_g, acc_s, acc_b, acc_c)):
        vec_o[i:i + 1, :] = acc
    move.store(gm_s, gm_h)
    move.store(gb_s, gb_h)
    last.wait()
    for c in range(0, d, 256):
        cs = slice(c, c + 256)
        gatt[:, cs] = dot_t(gb_s[...], wo[cs, :])
    move.store(gatt, gatt_h)
    move.finish()


def mid(rights, hws, cot, middle, wo, gain2, after=()):
    rows, d = middle.shape
    k = len(rights)
    shards, width = rights[0].shape[1], rights[0].shape[3]
    outs = [("h", S((rows, d), F32)), ("h", S((rows, d), BF)), ("h", S((rows, d), F32)), ("v", S((4, d), F32))]
    scratch = [VM((rows, d), BF), VM((rows, d), F32), VM((d, d), BF), VM(gain2.shape, F32), VM((k, shards, rows, width), BF),
               VM((k, shards, d, width), BF), VM((rows, d), F32), VM((rows, d), F32), VM((rows, d), BF), VM((rows, d), F32)]
    args = (cot, middle, wo, gain2, *rights, *hws)
    return call(functools.partial(mid_kernel, k), "mid", args, "h" * len(args), outs, scratch,
                10 + 2 * k * shards, 2 * rows * d * (k * shards * width + d), 12 * MIB, None, after)


def value_bwd_kernel(zm, pm, pieces, meta, gatt_h, gb_h, f_h, state_h, trans_h,
                     send_h, keep_h, gv_h, uw_h, gst_h, vec_o, gatt, uw_o, gst_o, f, state, left, right, stage, sems):
    move = Mover(sems)
    mols = molecules(zm, pm)
    rows, d = gatt.shape
    groups = d // 256
    loads = []
    for g in range(groups):
        cs, fs = slice(g * 256, (g + 1) * 256), slice(g * 128, (g + 1) * 128)
        loads.append([move.load(f_h.at[:, :, fs], f.at[:, :, fs]), move.load(state_h.at[:, g], state.at[:, g]),
                      move.load(gatt_h.at[:, cs], gatt.at[:, cs])])
    last = [move.load(trans_h, left), move.load(gb_h, right.at[0])]
    keep = block_mask(512)
    for g in range(groups):
        for c in loads[g]:
            c.wait()
        cs = slice(g * 256, (g + 1) * 256)
        fs = slice(g * 128, (g + 1) * 128)
        total = 0.0
        for i, (r, n) in enumerate(mols):
            ms = slice(r, r + n)
            st = state[i, g]
            q = f[0, ms, fs]
            nd = dot(q, st)
            rden = 1.0 / nd[:, 256:]
            u = gatt[ms, cs] * rden
            uw = jnp.concatenate([u, -(u * (nd[:, :256] * rden))], axis=1).astype(BF)
            uw_o[ms, slice(g * 512, (g + 1) * 512)] = uw
            gst = jnp.where(keep, dot_c(q, uw), 0.0).astype(BF)
            gst_o[i, g] = gst
            gv = dot(f[1, ms, fs], gst[:, :256]).astype(BF)
            right[1, ms, cs] = gv
            total += jnp.sum(gv.astype(F32), axis=0, keepdims=True)
        vec_o[0:1, cs] = total
    move.store(right.at[1], gv_h)
    move.store(uw_o, uw_h)
    move.store(gst_o, gst_h)
    for c in last:
        c.wait()
    me = meta[0]
    products(move, pieces, (meta[3], meta[2]), stage, ((left.at[1 - me], right.at[1 - me], send_h), (left.at[me], right.at[me], keep_h)))
    move.finish()


def value_bwd(meta, zm, pm, pieces, gatt, gb, f, state, trans, after=()):
    rows, d = gatt.shape
    outs = [("h", S((d, d), BF))] * 2 + [("h", S((rows, d), BF)), ("h", S((rows, 2 * d), BF)), ("h", S(state.shape, BF)), ("v", S((1, d), F32))]
    scratch = [VM((rows, d), F32), VM((rows, 2 * d), BF), VM(state.shape, BF), VM(f.shape, BF), VM(state.shape, BF), VM((2, d, rows), BF),
               VM((2, rows, d), BF), VM((2, d, d), BF)]
    args = (meta, gatt, gb, f, state, trans)
    return call(functools.partial(value_bwd_kernel, zm, pm, pieces), "value_bwd", args, "shhhhh", outs, scratch,
                10 + 3 * d // 256, 2 * d**3 * 3, 8 * MIB, None, after)


def query_bwd_kernel(zm, pm, pieces, meta, uw_h, gst_h, qkv_h, f_h, state_h, trans_h, proj_h, energy_h, table_h,
                     send_h, keep_h, gqk_h, vec_o, uw, gst, qkv, f, state, n1t, proj, energy, table, gqk, stage, sems):
    move = Mover(sems)
    mols = molecules(zm, pm)
    _, rows, d = qkv.shape
    loads = [[move.load(s, t) for s, t in ((proj_h, proj), (energy_h, energy), (table_h, table))]]
    for g in range(d // 256):
        cs, fs, us = slice(g * 256, (g + 1) * 256), slice(g * 128, (g + 1) * 128), slice(g * 512, (g + 1) * 512)
        if g:
            loads.append([])
        loads[g] += [move.load(uw_h.at[:, us], uw.at[:, us]), move.load(state_h.at[:, g], state.at[:, g]),
                     move.load(f_h.at[:, :, fs], f.at[:, :, fs]), move.load(gst_h.at[:, g], gst.at[:, g]),
                     move.load(qkv_h.at[:, :, cs], qkv.at[:, :, cs])]
    later = [move.load(trans_h.at[1], n1t)]
    for g in range(d // 256):
        for c in loads[g]:
            c.wait()
        cs = slice(g * 256, (g + 1) * 256)
        fs = slice(g * 128, (g + 1) * 128)
        sums = [0.0, 0.0]
        for b in range(rows // PPAD):
            mem = members(mols, b)
            rs = slice(b * PPAD, (b + 1) * PPAD)
            gfq, gfk = [], []
            for i, r, n in mem:
                ms = slice(r, r + n)
                gfq.append(dot_t(uw[ms, slice(g * 512, (g + 1) * 512)], state[i, g]))
                gfk.append(dot_t(jnp.concatenate([qkv[2, ms, cs], jnp.ones((n, 256), BF)], axis=1), gst[i, g]))
            cosb, sinb = (jnp.concatenate([table[t, :n, :] for _, _, n in mem], axis=0) for t in range(2))
            cosb = jnp.concatenate([cosb, cosb], axis=1)
            sinb = jnp.concatenate([sinb, sinb], axis=1)
            for t, gf in enumerate((gfq, gfk)):
                gp = (jnp.concatenate(gf, axis=0) * f[t, rs, fs].astype(F32)).astype(BF)
                back = dot(gp, proj[g])
                tot = dot(gp, energy[...])
                grad = (cosb * back[:, :256] + sinb * back[:, 256:] - tot * qkv[t, rs, cs].astype(F32)).astype(BF)
                gqk[t, rs, cs] = grad
                sums[t] += jnp.sum(grad.astype(F32), axis=0, keepdims=True)
        for t in range(2):
            vec_o[t:t + 1, cs] = sums[t]
    for c in later:
        c.wait()
    me = meta[0]
    products(move, pieces, (meta[3], meta[2]), stage, ((n1t, gqk.at[1 - me], send_h), (n1t, gqk.at[me], keep_h)))
    move.store(gqk, gqk_h)
    move.finish()


def query_bwd(meta, zm, pm, pieces, uw, gst, qkv, f, state, trans, proj, table, after=()):
    _, rows, d = qkv.shape
    outs = [("h", S((d, d), BF))] * 2 + [("h", S((2, rows, d), BF)), ("v", S((2, d), F32))]
    scratch = [VM(uw.shape, BF), VM(gst.shape, BF), VM(qkv.shape, BF), VM(f.shape, BF), VM(state.shape, BF), VM((d, rows), BF),
               VM(proj.shape, BF), VM((128, 256), BF), VM(table.shape, F32), VM((2, rows, d), BF), VM((2, d, d), BF)]
    args = (meta, uw, gst, qkv, f, state, trans, proj, head_const(64 ** -0.5), table)
    return call(functools.partial(query_bwd_kernel, zm, pm, pieces), "query_bwd", args, "s" + "h" * (len(args) - 1), outs, scratch,
                8 + 5 * d // 256, 2 * d**3 * 6, 12 * MIB, None, after)


def input_kernel(gqk_h, gv_h, wq_h, wk_h, wv_h, x_h, gm_h, gain_h, out_h, vec_o, gqk, gv, wq, wk, wv, x, gm, vec, e_s, out_s, sems):
    move = Mover(sems)
    rows, d = x.shape
    loads = [(move.load(gqk_h.at[0], gqk.at[0]), move.load(wq_h, wq)), (move.load(gqk_h.at[1], gqk.at[1]), move.load(wk_h, wk)),
             (move.load(gv_h, gv), move.load(wv_h, wv))]
    last = [move.load(s, t) for s, t in ((x_h, x), (gm_h, gm), (gain_h, vec))]
    for (left, right), load in zip(((gqk.at[0], wq), (gqk.at[1], wk), (gv, wv)), loads):
        for c in load:
            c.wait()
        for c in range(0, d, 256):
            cs = slice(c, c + 256)
            part = dot_t(left[...], right[cs, :])
            e_s[:, cs] = part if right is wq else e_s[:, cs] + part
    for c in last:
        c.wait()
    gain = row(vec)
    acc_g = acc_s = 0.0
    for r in range(0, rows, 256):
        rs = slice(r, r + 256)
        e = e_s[rs, :]
        n, rate = norm_parts(x[rs, :].astype(F32))
        acc_g += jnp.sum(e * n, axis=0, keepdims=True)
        acc_s += jnp.sum(e, axis=0, keepdims=True)
        eg = e * gain
        gx = rate * (eg - jnp.mean(eg, axis=-1, keepdims=True) - n * jnp.mean(eg * n, axis=-1, keepdims=True))
        out_s[rs, :] = (gm[rs, :] + gx).astype(BF)
    move.store(out_s, out_h)
    vec_o[0:1, :] = acc_g
    vec_o[1:2, :] = acc_s
    move.finish()


def input_back(gqk, gv, wq, wk, wv, x, gm, gain, after=()):
    rows, d = x.shape
    scratch = [VM(gqk.shape, BF), VM(gv.shape, BF)] + [VM((d, d), BF)] * 3 + [
        VM((rows, d), BF), VM((rows, d), F32), VM(gain.shape, F32), VM((rows, d), F32), VM((rows, d), BF)]
    args = (gqk, gv, wq, wk, wv, x, gm, gain)
    return call(input_kernel, "input_back", args, "h" * len(args), [("h", S((rows, d), BF)), ("v", S((2, d), F32))], scratch,
                16, 2 * d**3 * 3, 8 * MIB, None, after)


def layer_kernel(chunks, middle_h, vec_h, *refs):
    rights_h, rws_h = refs[:chunks], refs[chunks:2 * chunks]
    out_h, acts, rws, middle, vec, out_s, sems = refs[2 * chunks:]
    move = Mover(sems)
    base = [move.load(middle_h, middle), move.load(vec_h, vec)]
    loads = [[move.load(rights_h[k].at[1], acts.at[k]), move.load(rws_h[k], rws.at[k])] for k in range(chunks)]
    d = middle.shape[1]
    for c in base:
        c.wait()
    for k, load in enumerate(loads):
        for c in load:
            c.wait()
        for c in range(0, d, 256):
            cs = slice(c, c + 256)
            total = middle[:, cs] + sum(dot(acts[k, j], rws[k, j, :, cs]) for j in range(acts.shape[1]))
            if k + 1 < chunks:
                middle[:, cs] = total
            else:
                out_s[:, cs] = (total + row(vec)[:, cs]).astype(BF)
    move.store(out_s, out_h)
    move.finish()


def layer_end(rights, rws, middle, vec, after=()):
    rows, d = middle.shape
    k = len(rights)
    shards, width = rights[0].shape[1], rights[0].shape[3]
    scratch = [VM((k, shards, rows, width), BF), VM((k, shards, width, d), BF), VM((rows, d), F32), VM(vec.shape, F32), VM((rows, d), BF)]
    args = (middle, vec, *rights, *rws)
    return call(functools.partial(layer_kernel, k), "layer_end", args, "h" * len(args),
                [("h", S((rows, d), BF))], scratch, 4 + 2 * k, 2 * rows * d * k * shards * width, 12 * MIB, None, after)[0]


def placed(ref, p, code, pieces):
    step = ref.shape[0] // pieces
    return ref[pl.ds(pl.multiple_of(jnp.bitwise_xor(p, code) * step, 16), step), :]


def load_halves(move, m0, m1, t0, t1, cols, both, me):
    half = m0.shape[0]
    return [move.load(m0.at[:, cols], both.at[me, :half]), move.load(m1.at[:, cols], both.at[me, half:]),
            move.load(t0.at[:, cols], both.at[1 - me, :half]), move.load(t1.at[:, cols], both.at[1 - me, half:])]


def finish_ffn_kernel(pieces, k, meta, m0, m1, t0, t1, *refs):
    ghw_h, grw_h, both, whole, wide, tall, sems = refs[-7:]
    move = Mover(sems)
    me, code = meta[0], meta[1]
    d, width = wide.shape
    for c in load_halves(move, m0, m1, t0, t1, slice(0, width), both, me):
        c.wait()
    step = d // pieces
    for p in range(pieces):
        wide[p * step:(p + 1) * step, :] = placed(both.at[0], p, code, pieces).astype(F32)
    move.store(wide, ghw_h.at[:, k * width:(k + 1) * width])
    for p in range(pieces):
        whole[p * step:(p + 1) * step, :] = placed(both.at[1], p, code, pieces)
    for c in range(0, width, 128):
        cs = slice(c, c + 128)
        tall[cs, :] = whole[:, cs].T.astype(F32)
    move.store(tall, grw_h.at[k * width:(k + 1) * width])
    move.finish()


def finish_ffn(meta, pieces, parts, k, shard, before, after=()):
    d, width = 2 * parts[0].shape[0], parts[0].shape[1]
    args = (meta, *parts, *before)
    return call(functools.partial(finish_ffn_kernel, pieces, k), "finish_ffn", args, "shhhh" + "h" * len(before),
                [("h", S((d, shard), F32)), ("h", S((shard, d), F32))],
                [VM((2, d, width), BF), VM((d, width), BF), VM((d, width), F32), VM((width, d), F32)], 8, 0, 4 * MIB,
                {5 + i: i for i in range(len(before))}, after)


def finish_pair_kernel(pieces, meta, m0, m1, t0, t1, *refs):
    outs, (both, wide, sems) = refs[:-3], refs[-3:]
    move = Mover(sems)
    me = meta[0]
    d = wide.shape[1]
    pairs = len(outs) // 2
    loads = [load_halves(move, m0, m1, t0, t1, slice(k * d, (k + 1) * d), both.at[k], me) for k in range(pairs)]
    step = d // pieces
    for k in range(pairs):
        for c in loads[k]:
            c.wait()
        for t in range(2):
            code = jnp.where(me == t, meta[2], meta[3])
            for p in range(pieces):
                wide[2 * k + t, p * step:(p + 1) * step, :] = placed(both.at[k, t], p, code, pieces).astype(F32)
            move.store(wide.at[2 * k + t], outs[2 * k + t])
    move.finish()


def finish_pair(meta, pieces, parts, d, after=()):
    pairs = parts[0].shape[1] // d
    return call(functools.partial(finish_pair_kernel, pieces), "finish_pair", (meta, *parts), "shhhh",
                [("h", S((d, d), F32))] * (2 * pairs), [VM((pairs, 2, d, d), BF), VM((2 * pairs, d, d), F32)], 4 + 6 * pairs, 0, 8 * MIB, None, after)


def bits_below(size):
    return [1 << i for i in range(size.bit_length() - 1)]


class Layout:
    def __init__(self, mesh):
        self.nb, self.nt = mesh.shape["batch"], mesh.shape["tp"]
        self.tp = [("tp", b) for b in reversed(bits_below(self.nt))]
        self.batch = [("batch", b) for b in bits_below(self.nb)[1:]]
        self.lanes = (self.tp + self.batch, self.batch[:1] + self.tp + self.batch[1:])

    def partner(self, device, level):
        b, t = divmod(device, self.nt)
        axis, bit = level
        return (b ^ bit) * self.nt + t if axis == "batch" else b * self.nt + (t ^ bit)

    def swap(self, value, level):
        pairs = []
        for device in range(self.nb * self.nt):
            core, to = device // self.nt % 2, device
            for one in level if isinstance(level, list) else [level]:
                to = self.partner(to, self.lanes[core][one] if isinstance(one, int) else one)
            pairs.append((device, to))
        return lax.ppermute(value, ("batch", "tp"), pairs)


CORE = ("batch", 1)


def code_of(levels, place):
    out = jnp.int32(0)
    for axis, bit in levels:
        out = out * 2 + (place[axis] // bit) % 2
    return out


def add(a, b):
    return (a.astype(F32) + b.astype(F32)).astype(BF)


def scatter_levels(levels, rows, least=48):
    n = 0
    while n < len(levels) and rows % 32 == 0 and rows // 2 >= least:
        rows //= 2
        n += 1
    return n


class Chain:
    def __init__(self, lay, steps):
        self.lay, self.steps, self.result = lay, steps, None
        self.go(next(steps))

    def go(self, requests):
        self.sent = [v for v, _ in requests]
        self.here = [self.lay.swap(v, level) for v, level in requests]

    def step(self):
        try:
            self.go(self.steps.send(self.here))
        except StopIteration as end:
            self.result, self.sent, self.here = end.value, [], []
        return self


def fence(arrays, *chains):
    chains = [c for c in chains if c.here]
    arrays, held = lax.optimization_barrier((arrays, [c.here for c in chains]))
    for chain, here in zip(chains, held):
        chain.here = here
        chain.step()
    return arrays


def sent(*chains):
    return tuple(v for c in chains for v in c.sent)


def halving(a, b, levels):
    for level in levels:
        n = a.shape[0] // 2
        kept = add(a[:n], b[:n])
        (b,) = yield [(add(a[n:], b[n:]), level)]
        a = kept
    return add(a, b)


def quartering(held, high, low):
    n = held.shape[0] // 4
    got = yield [(held[n:2 * n], [low]), (held[2 * n:3 * n], [high]), (held[3 * n:], [high, low])]
    return sum((g.astype(F32) for g in got), held[:n].astype(F32)).astype(BF)


def fourfold(held, high, low):
    got = yield [(held, [low]), (held, [high]), (held, [high, low])]
    return jnp.concatenate([held] + got, axis=0)


def doubling(held, levels):
    for level in levels:
        (got,) = yield [(held, level)]
        held = jnp.concatenate([held, got], axis=0)
    return held


def spread(held, level):
    other, mine = yield [(held, level), (held, CORE)]
    (rest,) = yield [(other, CORE)]
    return held, other, mine, rest


def single(held, levels):
    for level in levels:
        n = held.shape[0] // 2
        (got,) = yield [(held[n:], level)]
        held = add(held[:n], got)
    return held


def reduce_ffn(lay, gone, stay, keep):
    m = len(lay.lanes[0])
    n = gone.shape[0]
    (recv,) = yield [(gone, CORE)]
    b, recv = yield [(add(keep[n:], recv), 0), (stay, CORE)]
    held = yield from halving(add(keep[:n], recv), b, range(1, m - 2))
    held = yield from quartering(held, m - 2, m - 1)
    held = yield from doubling(held, reversed(lay.batch[1:]))
    return (yield from spread(held, lay.batch[0]))


def reduce_pair(lay, n, send, keep, ahead):
    (recv,) = yield [(send, CORE)]
    held = yield from halving(keep, recv, range(n - 2))
    held = yield from (single(held, (n - 2, n - 1)) if ahead else quartering(held, n - 2, n - 1))
    for level in range(n, len(lay.lanes[0])):
        (got,) = yield [(held, level)]
        held = add(held, got)
    held = yield from fourfold(held, n - 2, n - 1)
    held = yield from doubling(held, reversed(range(1, n - 2)))
    return (yield from spread(held, 0))


def reduce_small(lay, vectors, hidden):
    n, shard = vectors.shape[0], hidden[0].shape[0]
    for level in lay.tp:
        bit = level[1]
        (got,) = yield [(jnp.concatenate([vectors] + [hidden[j + bit] for j in range(bit)]), level)]
        vectors = vectors + got[:n]
        hidden = [hidden[j] + got[n + j * shard:n + (j + 1) * shard] for j in range(bit)]
    held = jnp.concatenate([vectors, hidden[0]])
    for level in [CORE] + lay.batch:
        (got,) = yield [(held, level)]
        held = held + got
    return held


def on_device(
    lay,
    inputs,
    cotangent,
    zinc_lengths,
    pubchem_lengths,
    feature_stack,
    train_step,
    redraw_interval,
    attn_gain,
    attn_shift,
    query_weight,
    query_bias,
    key_weight,
    key_bias,
    value_weight,
    value_bias,
    output_weight,
    output_bias,
    ffn_gain,
    ffn_shift,
    hidden_weight,
    hidden_bias,
    return_weight,
    return_bias,
):
    nt = lay.nt
    d, shard = hidden_weight.shape
    rows = inputs.shape[0]
    width = min(768, shard)
    chunks = shard // width
    zm, pm = zinc_lengths.shape[0], pubchem_lengths.shape[0]
    place = {"batch": lax.axis_index("batch"), "tp": lax.axis_index("tp")}
    core = place["batch"] % 2

    def shares(k):
        hw = lax.dynamic_slice(hidden_weight, (core * (d // 2), k * width), (d // 2, width))
        rw = lax.dynamic_slice(return_weight, (k * width + core * (width // 2), 0), (width // 2, d))
        return [jnp.concatenate([hw, rw], axis=0)] if width == d else [hw, rw]

    def from_tp(own):
        pool = {0: own}
        for level in lay.tp:
            for j in list(pool):
                pool[j | level[1]] = [lay.swap(v, level) for v in pool[j]]
        return [v for j in range(1, nt) for v in pool[j]]

    own = [shares(k) for k in range(chunks)]
    per = len(own[0])
    biases = from_tp([hidden_bias])
    here = {k: from_tp(own[k]) for k in range(chunks)}

    n_pair = scatter_levels(lay.lanes[0], d)
    codes = [code_of(lane[:n_pair], place) for lane in lay.lanes]
    pick = train_step[0] // redraw_interval[0] % feature_stack.shape[0]
    meta = jnp.stack([core, code_of(lay.batch, place), jnp.where(core == 0, codes[0], codes[1]), jnp.where(core == 0, codes[1], codes[0]),
                      code_of(lay.batch[:-2], place) * 4, pick]).astype(jnp.int32)
    table = rotary_const()

    out = attend_fwd(
        meta, zinc_lengths, pubchem_lengths, cotangent, inputs,
        (attn_gain, attn_shift, query_bias, key_bias, value_bias, output_bias, ffn_gain, ffn_shift),
        query_weight, key_weight, value_weight, output_weight, feature_stack, table)
    out, here[0], biases = lax.optimization_barrier((out, here[0], biases))
    qkv, f, state, trans, middle, n2, left, proj = out

    pieces, pair_pieces = 2 ** len(lay.batch), 2 ** n_pair
    chains, rights, hws, rws, hidden = [], [], [], [], []
    for k in range(chunks):
        near = [lay.swap(v, CORE) for v in here[k]]
        if chains:
            near = fence(near, chains[-1])
        parts = [[v[i] for i in range(j * per, (j + 1) * per) for v in (here[k], near)] for j in range(nt - 1)]
        out = ffn_chunk(meta, pieces, nt, n2, left, cotangent, hidden_bias, hidden_weight, return_weight, parts, biases, k, width,
                        sent(*chains))
        if k + 1 < chunks:
            out, here[k + 1] = lax.optimization_barrier((out, here[k + 1]))
        gone, stay, keep, right, bias, hw, rw = fence(out, *chains)
        chains.append(Chain(lay, reduce_ffn(lay, gone, stay, keep)))
        rights.append(right)
        hws.append(hw)
        rws.append(rw)
        hidden.append(bias)

    middle = fence(middle, chains[-1])
    out = mid(rights, hws, cotangent, middle, output_weight, ffn_gain, sent(*chains))
    gm, gb, gatt, vec1 = fence(out, *chains)
    out = value_bwd(meta, zm, pm, pair_pieces, gatt, gb, f, state, trans, sent(*chains))
    send, keep, gv, uw, gst, vec2 = fence(out, *chains)
    pair_a = Chain(lay, reduce_pair(lay, n_pair, send, keep, True))
    uw = fence(uw, pair_a)
    out = query_bwd(meta, zm, pm, pair_pieces, uw, gst, qkv, f, state, trans, proj, table, sent(pair_a, *chains))
    send, keep, gqk, vec3 = fence(out, pair_a, *chains)
    pair_b = Chain(lay, reduce_pair(lay, n_pair, send, keep, False))
    gqk = fence(gqk, pair_b)
    out = input_back(gqk, gv, query_weight, key_weight, value_weight, inputs, gm, attn_gain, sent(pair_a, pair_b, *chains))
    (input_grad, vec4), middle = fence((out, middle), pair_a, pair_b, *chains)
    layer_out = layer_end(rights, rws, middle, return_bias, sent(pair_b, pair_a, *chains))
    layer_out, vec4 = fence((layer_out, vec4), pair_b, pair_a, *chains)
    vec3 = jnp.concatenate([vec3, vec4], axis=0)
    vectors = jnp.concatenate([vec1, vec2, vec3], axis=0).reshape(-1)
    small = Chain(lay, reduce_small(lay, vectors, [jnp.concatenate([hidden[k][j] for k in range(chunks)]) for j in range(nt)]))

    every = [pair_b, pair_a, small] + chains
    ffn_out, k, first = (), 0, None
    while any(c.here for c in every):
        if k < chunks and chains[k].result is not None:
            ffn_out = finish_ffn(meta, pieces, chains[k].result, k, shard, ffn_out, sent(*every))
            k += 1
            ffn_out = fence(ffn_out, *every)
        elif first is None and pair_a.result is not None:
            first = fence(finish_pair(meta, pair_pieces, pair_a.result, d, sent(*every)), *every)
        else:
            fence((), *every)
    while k < chunks:
        ffn_out = finish_ffn(meta, pieces, chains[k].result, k, shard, ffn_out)
        k += 1
    gwo, gwv = finish_pair(meta, pair_pieces, pair_a.result, d) if first is None else first
    gwq, gwk = finish_pair(meta, pair_pieces, pair_b.result, d)
    vecs = small.result[:9 * d].reshape(9, d)
    return (layer_out, input_grad, vecs[7], vecs[8], gwq, vecs[5], gwk, vecs[6], gwv, vecs[4], gwo, vecs[2],
            vecs[0], vecs[1], ffn_out[0], small.result[9 * d:], ffn_out[1], vecs[3])


def solution(mesh):
    rows, whole, hidden = P(("batch", "tp"), None), P(), P(None, "tp")
    return jax.shard_map(
        functools.partial(on_device, Layout(mesh)),
        mesh=mesh,
        in_specs=(rows, rows, P(("batch", "tp")), P(("batch", "tp"))) + (whole,) * 15 + (hidden, P("tp"), P("tp", None), whole),
        out_specs=(rows, rows) + (whole,) * 12 + (hidden, P("tp"), P("tp", None), whole),
        check_vma=False,
    )
```

```python
import functools
import math

import jax
import jax.numpy as jnp
import numpy as np
from jax import lax
from jax.experimental import pallas as pl
from jax.experimental.pallas import tpu as pltpu
from jax.sharding import PartitionSpec as P

ZPAD = 64
PPAD = 256
F32 = jnp.float32
BF = jnp.bfloat16
VM = pltpu.VMEM
GROUP = 4
S = jax.ShapeDtypeStruct
TIMES = {"attend_fwd": 24, "ffn_chunk": 17, "layer_end": 9, "mid": 8, "value_bwd": 13, "query_bwd": 13, "input_back": 10, "finish_ffn": 5, "finish_pair": 5}
MIB = 2**20
GRANT = 60


def dot(a, b):
    return jnp.dot(a, b, preferred_element_type=F32)


def dot_t(a, b):
    return lax.dot_general(a, b, (((1,), (1,)), ((), ())), preferred_element_type=F32)


def dot_c(a, b):
    return lax.dot_general(a, b, (((0,), (0,)), ((), ())), preferred_element_type=F32)


def split(v):
    hi = v.astype(BF)
    return hi, (v - hi.astype(F32)).astype(BF)


def norm_parts(values):
    center = values - jnp.mean(values, axis=-1, keepdims=True)
    rate = lax.rsqrt(jnp.mean(center * center, axis=-1, keepdims=True) + 1e-05)
    return center * rate, rate


def row(ref):
    return ref[...].reshape(1, -1)


def block_mask(width):
    f = lax.broadcasted_iota(jnp.int32, (128, width), 0) // 32
    c = lax.broadcasted_iota(jnp.int32, (128, width), 1) % 256 // 64
    return f == c


def molecules(zm, pm):
    return [(i * ZPAD, ZPAD) for i in range(zm)] + [(zm * ZPAD + i * PPAD, PPAD) for i in range(pm)]


def members(mols, b):
    return [(i, r, n) for i, (r, n) in enumerate(mols) if b * PPAD <= r < (b + 1) * PPAD]


class Mover:
    def __init__(self, sems):
        self.sems, self.n, self.out = sems, 0, []

    def load(self, src, dst):
        copy = pltpu.make_async_copy(src, dst, self.sems.at[self.n])
        self.n += 1
        copy.start()
        return copy

    def store(self, src, dst):
        self.out.append(self.load(src, dst))

    def finish(self):
        for copy in self.out:
            copy.wait()


def call(kernel, name, args, spaces, outs, scratch, copies, flops, moved, aliases=None, after=()):
    n, extra = len(args), len(after)

    def body(*refs):
        kernel(*refs[:n], *refs[n + extra:])

    spec = {
        "v": pl.BlockSpec(memory_space=VM),
        "h": pl.BlockSpec(memory_space=pltpu.HBM),
        "s": pl.BlockSpec(memory_space=pltpu.SMEM),
    }
    return pl.pallas_call(
        body,
        out_shape=tuple(o for _, o in outs),
        in_specs=[spec[s] for s in spaces] + [spec["h"]] * extra,
        out_specs=tuple(spec[s] for s, _ in outs),
        scratch_shapes=list(scratch) + [pltpu.SemaphoreType.DMA((copies,))],
        input_output_aliases=aliases or {},
        compiler_params=pltpu.CompilerParams(vmem_limit_bytes=GRANT * MIB),
        cost_estimate=pl.CostEstimate(flops=int(TIMES[name] * 1.15e9), bytes_accessed=moved, transcendentals=0),
        name=name,
    )(*args, *after)


def place_heads(scaled):
    two = jnp.concatenate([scaled, scaled], axis=1)
    return jnp.where(block_mask(256), jnp.concatenate([two, two], axis=1), 0.0)


def attend_fwd_kernel(zm, pm, meta, zlen, plen, cot_h, x_h, gain_h, shift_h, bq_h, bk_h, bv_h, bo_h, gain2_h, shift2_h,
                      wq_h, wk_h, wv_h, wo_h, stack_h, table_h, energy_h,
                      qkv_h, f_h, state_h, trans_h, middle_h, n2_h, left_h, proj_h,
                      cot, n2_s, left, x, vec, wq, wk, wv, wo, fp, proj, table, energy, qkv, f_s, state_s, trans, middle_s, att_s, sems):
    move = Mover(sems)
    rows, d = x.shape
    first = [move.load(x_h, x), move.load(gain_h, vec.at[0]), move.load(shift_h, vec.at[1]), move.load(stack_h.at[meta[5]], fp),
             move.load(cot_h, cot)]
    later = [move.load(s, t) for s, t in ((wq_h, wq), (bq_h, vec.at[2]), (table_h, table), (energy_h, energy), (wk_h, wk),
                                          (bk_h, vec.at[3]), (wv_h, wv), (bv_h, vec.at[4]))]
    last = [move.load(s, t) for s, t in ((wo_h, wo), (bo_h, vec.at[5]), (gain2_h, vec.at[6]), (shift2_h, vec.at[7]))]
    mols = molecules(zm, pm)
    groups = d // 256
    blocks = range(rows // PPAD)
    keep = block_mask(512)
    ones = jnp.ones((PPAD, 256), BF)

    def vector(i):
        return vec[i].reshape(1, -1)

    for c in first:
        c.wait()
    for g in range(groups):
        p = fp[g * GROUP:(g + 1) * GROUP].reshape(GROUP * 32, 64) * 64 ** -0.25
        turned = jnp.concatenate([p[:, 32:], -p[:, :32]], axis=1)
        hi, lo = split(jnp.concatenate([place_heads(p), place_heads(turned)], axis=1))
        proj[0, g] = hi
        proj[1, g] = lo
    n1s = {}
    for b in blocks:
        rs = slice(b * PPAD, (b + 1) * PPAD)
        normed, _ = norm_parts(x[rs, :].astype(F32))
        n1s[b] = (normed * vector(0) + vector(1)).astype(BF)
        trans[1, :, rs] = n1s[b].T
        left[1, :, rs] = cot[rs, :].T
    for c in later:
        c.wait()
    move.store(proj.at[0], proj_h)
    move.store(trans.at[1], trans_h.at[1])
    move.store(left.at[1], left_h.at[1])
    for b in blocks:
        mem = members(mols, b)
        rs = slice(b * PPAD, (b + 1) * PPAD)
        n1 = n1s[b]
        cosb, sinb = (jnp.concatenate([table[t, :n, :] for _, _, n in mem], axis=0) for t in range(2))
        cosb = jnp.concatenate([cosb, cosb], axis=1)
        sinb = jnp.concatenate([sinb, sinb], axis=1)
        live = jnp.concatenate(
            [(lax.broadcasted_iota(jnp.int32, (n, 128), 0) < (zlen[i] if i < zm else plen[i - zm])).astype(F32) for i, r, n in mem], axis=0)
        for g in range(groups):
            cs = slice(g * 256, (g + 1) * 256)
            fs = slice(g * 128, (g + 1) * 128)

            def features(w, bias, slot):
                v = dot(n1, w[:, cs]) + vector(bias)[:, cs]
                qkv[slot, rs, cs] = v.astype(BF)
                ch, cl = split(v * cosb)
                sh, sl = split(v * sinb)
                eh, el = split(v * v)
                ph, plo = proj[0, g], proj[1, g]
                e = energy[...]
                inner = (dot_t(ch, ph[:, :256]) + dot_t(sh, ph[:, 256:]) + dot_t(cl, ph[:, :256]) + dot_t(sl, ph[:, 256:])
                         + dot_t(ch, plo[:, :256]) + dot_t(sh, plo[:, 256:]) - dot_t(eh, e) - dot_t(el, e))
                return jnp.exp(inner) * (32 ** -0.5)

            fq = features(wq, 2, 0).astype(BF)
            fk = (features(wk, 3, 1) * live).astype(BF)
            f_s[0, rs, fs] = fq
            f_s[1, rs, fs] = fk
            v = (dot(n1, wv[:, cs]) + vector(4)[:, cs]).astype(BF)
            qkv[2, rs, cs] = v
            for i, r, n in mem:
                ms = slice(r - b * PPAD, r - b * PPAD + n)
                vo = jnp.concatenate([v[ms], ones[:n]], axis=1)
                state = jnp.where(keep, dot_c(fk[ms], vo), 0.0).astype(BF)
                state_s[i, g] = state
                nd = dot(fq[ms], state)
                att_s[r:r + n, cs] = (nd[:, :256] / nd[:, 256:]).astype(BF)
    for s, t in ((qkv, qkv_h), (f_s, f_h), (state_s, state_h)):
        move.store(s, t)
    for c in last:
        c.wait()
    for b in blocks:
        rs = slice(b * PPAD, (b + 1) * PPAD)
        trans[0, :, rs] = att_s[rs, :].T
        middle = x[rs, :].astype(F32) + (dot(att_s[rs, :], wo[...]) + vector(5))
        middle_s[rs, :] = middle
        normed, _ = norm_parts(middle)
        n2 = (normed * vector(6) + vector(7)).astype(BF)
        n2_s[rs, :] = n2
        left[0, :, rs] = n2.T
    move.store(middle_s, middle_h)
    move.store(n2_s, n2_h)
    move.store(trans.at[0], trans_h.at[0])
    move.store(left.at[0], left_h.at[0])
    move.finish()


def rotary_const():
    place = np.arange(PPAD, dtype=np.float64)
    rates = np.exp(np.arange(32, dtype=np.float64) * (-2.0 * math.log(10000.0) / 64))
    ang = place[:, None] * rates[None, :]
    return np.tile(np.stack([np.cos(ang), np.sin(ang)]), (1, 1, 4)).astype(np.float32)


def head_const(scale):
    f = np.arange(128)[:, None] // 32
    c = np.arange(256)[None, :] // 64
    return ((f == c) * scale).astype(jnp.bfloat16)


def attend_fwd(meta, zlen, plen, cot, x, vectors, wq, wk, wv, wo, stack, table):
    rows, d = x.shape
    zm, pm = zlen.shape[0], plen.shape[0]
    groups = d // 256
    states = (zm + pm, groups, 128, 512)
    outs = [S((3, rows, d), BF), S((2, rows, d // 2), BF), S(states, BF), S((2, d, rows), BF),
            S((rows, d), F32), S((rows, d), BF), S((2, d, rows), BF), S((groups, 128, 512), BF)]
    args = (meta, zlen, plen, cot, x, *vectors, wq, wk, wv, wo, stack, table, head_const(1 / 16))
    scratch = ([VM((rows, d), BF)] * 2 + [VM((2, d, rows), BF), VM((rows, d), BF), VM((8, d), F32)] + [VM((d, d), BF)] * 4
               + [VM(stack.shape[1:], F32), VM((2, groups, 128, 512), BF), VM(table.shape, F32), VM((128, 256), BF)]
               + [VM((3, rows, d), BF), VM((2, rows, d // 2), BF), VM(states, BF), VM((2, d, rows), BF), VM((rows, d), F32), VM((rows, d), BF)])
    return call(
        functools.partial(attend_fwd_kernel, zm, pm), "attend_fwd", args, "sss" + "h" * (len(args) - 3),
        [("h", o) for o in outs], scratch, 32, 2 * rows * d * d * 4, 16 * MIB)


def gelu_parts(h):
    bell = jnp.exp(h * h * -0.5)
    t = 1.0 / (1.0 + (0.3275911 * math.sqrt(0.5)) * jnp.abs(h))
    poly = t * (0.127414796 + t * (-0.142248368 + t * (0.7107068705 + t * (-0.7265760135 + t * 0.5307027145))))
    tail = poly * bell
    phi = jnp.where(h >= 0, 1.0 - tail, tail)
    return h * phi, phi + h * bell * (1.0 / math.sqrt(2 * math.pi))


def place_pieces(code, src, dst):
    n, step = src.shape[0], src.shape[1]
    for p in range(n):
        off = pl.multiple_of(jnp.bitwise_xor(p, code) * step, 16)
        dst[pl.ds(off, step), :] = src[p]


def ffn_kernel(pieces, shards, k, per, meta, n2_h, left_h, cot_h, hb_h, hw_h, rw_h, *refs):
    parts = {j: refs[(j - 1) * per:j * per] for j in range(1, shards)}
    hbs = refs[(shards - 1) * per:(shards - 1) * (per + 1)]
    e_prev = refs[(shards - 1) * (per + 1)] if k else None
    (gone_h, stay_h, keep_h, act_h, bias_o, e_h, rws_h, n2, left, cot, hb, hw, rw, hw2, rw2, right, stage, e_s, sems) = refs[-19:]
    move = Mover(sems)
    d, width = hw.shape[1:]
    half_d = d // 2
    me, code = meta[0], meta[1]
    order = list(range(1, shards)) + [0]
    early, late = {}, {}
    for j in order:
        early[j] = [move.load(hbs[j - 1] if j else hb_h, hb.at[j])]
        if j == order[0]:
            early[j].append(move.load(n2_h, n2))
        late[j] = []
        if j == 0:
            early[j].append(move.load(hw_h.at[:, k * width:(k + 1) * width], hw.at[0]))
            late[j].append(move.load(rw_h.at[k * width:(k + 1) * width, :], rw.at[0]))
        elif per == 2:
            early[j] += [move.load(parts[j][p].at[:half_d], hw2.at[j - 1, p]) for p in range(2)]
            late[j] += [move.load(parts[j][p].at[half_d:], rw2.at[j - 1, p]) for p in range(2)]
        else:
            early[j] += [move.load(parts[j][p], hw2.at[j - 1, p]) for p in range(2)]
            late[j] += [move.load(parts[j][2 + p], rw2.at[j - 1, p]) for p in range(2)]
        if j == order[0]:
            late[j].append(move.load(cot_h, cot))
    last = [move.load(left_h, left)]
    if k:
        last.append(move.load(e_prev, e_s))
    step, half = d // pieces, pieces // 2
    tile = 256 if width % 256 == 0 else 128
    for j in order:
        for c in early[j] + late[j]:
            c.wait()
        if j:
            place_pieces(me, hw2.at[j - 1], hw.at[j])
            place_pieces(me, rw2.at[j - 1], rw.at[j])
        bias = hb[j].reshape(1, -1)[:, k * width:(k + 1) * width].astype(F32)
        for c in range(0, width, tile):
            cs = slice(c, c + tile)
            h = dot(n2[...], hw[j, :, cs]) + bias[:, cs]
            act, slope = gelu_parts(h)
            ga = dot_t(cot[...], rw[j, cs, :])
            gh = (ga * slope).astype(BF)
            right[0, j, :, cs] = gh
            right[1, j, :, cs] = act.astype(BF)
            bias_o[j:j + 1, cs] = jnp.sum(gh.astype(F32), axis=0, keepdims=True)
        move.store(right.at[1, j], act_h.at[j])
        move.store(rw.at[j], rws_h.at[j])
    for c in last:
        c.wait()
    for c in range(0, d, 256):
        cs = slice(c, c + 256)
        part = sum(dot_t(right[0, j], hw[j, cs, :]) for j in order)
        e_s[:, cs] = e_s[:, cs] + part if k else part
    move.store(e_s, e_h)
    for kind, slot in ((1 - me, 0), (me, 1)):
        for j in order:
            for c in range(0, width, tile):
                cs = slice(c, c + tile)
                value = dot(left[kind], right[kind, j, :, cs]).astype(BF)
                for p in range(pieces):
                    rel = jnp.bitwise_xor(p, code)
                    second = rel // half * (shards * half) + j * half + rel % half
                    off = pl.multiple_of(jnp.where(kind == 0, j * pieces + rel, second) * step, 16)
                    stage[slot, pl.ds(off, step), cs] = value[p * step:(p + 1) * step]
        if slot:
            move.store(stage.at[1], keep_h)
        else:
            cut = shards * d // 2
            move.store(stage.at[0, cut:], gone_h)
            move.store(stage.at[0, :cut], stay_h)
    move.finish()


def ffn_chunk(meta, pieces, shards, n2, left, cot, hb, hw, rw, parts, hbs, k, width, before, after=()):
    rows, d = n2.shape
    per = len(parts[0])
    part = S((shards * d // 2, width), BF)
    outs = [("h", part), ("h", part), ("h", S((shards * d, width), BF)), ("h", S((shards, rows, width), BF)), ("v", S((shards, width), F32)),
            ("h", S((rows, d), F32)), ("h", S((shards, width, d), BF))]
    scratch = [VM((rows, d), BF), VM((2, d, rows), BF), VM((rows, d), BF), VM((shards, 1) + hb.shape, BF), VM((shards, d, width), BF),
               VM((shards, width, d), BF), VM((shards - 1, 2, d // 2, width), BF), VM((shards - 1, 2, width // 2, d), BF),
               VM((2, shards, rows, width), BF), VM((2, shards * d, width), BF), VM((rows, d), F32)]
    args = (meta, n2, left, cot, hb.reshape(1, -1), hw, rw) + tuple(p for part in parts for p in part) + tuple(b.reshape(1, -1) for b in hbs) + tuple(before)
    return call(
        functools.partial(ffn_kernel, pieces, shards, k, per), "ffn_chunk", args,
        "s" + "h" * (len(args) - 1), outs, scratch, 12 + 13 * shards, 2 * rows * d * width * 5 * shards, 12 * MIB, None, after)


def products(move, pieces, codes, stage, outs):
    for slot, (left, right, out) in enumerate(outs):
        d = out.shape[0]
        step = d // pieces
        for c in range(0, d, 256):
            cs = slice(c, c + 256)
            value = dot(left[...], right[:, cs]).astype(BF)
            for p in range(pieces):
                off = pl.multiple_of(jnp.bitwise_xor(p, codes[slot]) * step, 16)
                stage[slot, pl.ds(off, step), cs] = value[p * step:(p + 1) * step]
        move.store(stage.at[slot], out)


def mid_kernel(e_h, cot_h, middle_h, wo_h, vec_h, gm_h, gb_h, gatt_h, vec_o, e_s, cot, middle, wo, vec, gm_s, gb_s, gatt, sems):
    move = Mover(sems)
    rows, d = middle.shape
    loads = [[move.load(s.at[r:r + 256], t.at[r:r + 256]) for s, t in ((middle_h, middle), (e_h, e_s), (cot_h, cot))]
             for r in range(0, rows, 256)]
    gain = move.load(vec_h, vec)
    last = move.load(wo_h, wo)
    gain.wait()
    gain2 = row(vec)
    acc_g = acc_s = acc_b = acc_c = 0.0
    for i, r in enumerate(range(0, rows, 256)):
        for c in loads[i]:
            c.wait()
        rs = slice(r, r + 256)
        e = e_s[rs, :]
        n, rate = norm_parts(middle[rs, :])
        c = cot[rs, :].astype(F32)
        acc_g += jnp.sum(e * n, axis=0, keepdims=True)
        acc_s += jnp.sum(e, axis=0, keepdims=True)
        acc_c += jnp.sum(c, axis=0, keepdims=True)
        eg = e * gain2
        gm = c + rate * (eg - jnp.mean(eg, axis=-1, keepdims=True) - n * jnp.mean(eg * n, axis=-1, keepdims=True))
        gm_s[rs, :] = gm
        gb = gm.astype(BF)
        gb_s[rs, :] = gb
        acc_b += jnp.sum(gb.astype(F32), axis=0, keepdims=True)
    for i, acc in enumerate((acc_g, acc_s, acc_b, acc_c)):
        vec_o[i:i + 1, :] = acc
    move.store(gm_s, gm_h)
    move.store(gb_s, gb_h)
    last.wait()
    for c in range(0, d, 256):
        cs = slice(c, c + 256)
        gatt[:, cs] = dot_t(gb_s[...], wo[cs, :]).astype(BF)
    move.store(gatt, gatt_h)
    move.finish()


def mid(e, cot, middle, wo, gain2, after=()):
    rows, d = middle.shape
    outs = [("h", S((rows, d), F32)), ("h", S((rows, d), BF)), ("h", S((rows, d), BF)), ("v", S((4, d), F32))]
    scratch = [VM((rows, d), F32), VM((rows, d), BF), VM((rows, d), F32), VM((d, d), BF), VM(gain2.shape, F32), VM((rows, d), F32),
               VM((rows, d), BF), VM((rows, d), BF)]
    args = (e, cot, middle, wo, gain2)
    return call(mid_kernel, "mid", args, "h" * len(args), outs, scratch, 8 + 3 * (rows // 256), 2 * rows * d * d, 8 * MIB, None, after)


def value_bwd_kernel(zm, pm, pieces, meta, gatt_h, gb_h, f_h, state_h, trans_h,
                     send_h, keep_h, gv_h, uw_h, gst_h, vec_o, gatt, uw_o, gst_o, f, state, left, right, stage, sems):
    move = Mover(sems)
    mols = molecules(zm, pm)
    rows, d = gatt.shape
    groups = d // 256
    loads = []
    for g in range(groups):
        cs, fs = slice(g * 256, (g + 1) * 256), slice(g * 128, (g + 1) * 128)
        loads.append([move.load(f_h.at[:, :, fs], f.at[:, :, fs]), move.load(state_h.at[:, g], state.at[:, g]),
                      move.load(gatt_h.at[:, cs], gatt.at[:, cs])])
    last = [move.load(trans_h, left), move.load(gb_h, right.at[0])]
    keep = block_mask(512)
    for g in range(groups):
        for c in loads[g]:
            c.wait()
        cs = slice(g * 256, (g + 1) * 256)
        fs = slice(g * 128, (g + 1) * 128)
        total = 0.0
        for i, (r, n) in enumerate(mols):
            ms = slice(r, r + n)
            st = state[i, g]
            q = f[0, ms, fs]
            nd = dot(q, st)
            rden = 1.0 / nd[:, 256:]
            u = gatt[ms, cs].astype(F32) * rden
            uw = jnp.concatenate([u, -(u * (nd[:, :256] * rden))], axis=1).astype(BF)
            uw_o[ms, slice(g * 512, (g + 1) * 512)] = uw
            gst = jnp.where(keep, dot_c(q, uw), 0.0).astype(BF)
            gst_o[i, g] = gst
            gv = dot(f[1, ms, fs], gst[:, :256]).astype(BF)
            right[1, ms, cs] = gv
            total += jnp.sum(gv.astype(F32), axis=0, keepdims=True)
        vec_o[0:1, cs] = total
    move.store(right.at[1], gv_h)
    move.store(uw_o, uw_h)
    move.store(gst_o, gst_h)
    for c in last:
        c.wait()
    me = meta[0]
    products(move, pieces, (meta[3], meta[2]), stage, ((left.at[1 - me], right.at[1 - me], send_h), (left.at[me], right.at[me], keep_h)))
    move.finish()


def value_bwd(meta, zm, pm, pieces, gatt, gb, f, state, trans, after=()):
    rows, d = gatt.shape
    outs = [("h", S((d, d), BF))] * 2 + [("h", S((rows, d), BF)), ("h", S((rows, 2 * d), BF)), ("h", S(state.shape, BF)), ("v", S((1, d), F32))]
    scratch = [VM((rows, d), BF), VM((rows, 2 * d), BF), VM(state.shape, BF), VM(f.shape, BF), VM(state.shape, BF), VM((2, d, rows), BF),
               VM((2, rows, d), BF), VM((2, d, d), BF)]
    args = (meta, gatt, gb, f, state, trans)
    return call(functools.partial(value_bwd_kernel, zm, pm, pieces), "value_bwd", args, "shhhhh", outs, scratch,
                10 + 3 * d // 256, 2 * d**3 * 3, 8 * MIB, None, after)


def query_bwd_kernel(zm, pm, pieces, meta, uw_h, gst_h, qkv_h, f_h, state_h, trans_h, proj_h, energy_h, table_h,
                     send_h, keep_h, gqk_h, vec_o, uw, gst, qkv, f, state, n1t, proj, energy, table, gqk, stage, sems):
    move = Mover(sems)
    mols = molecules(zm, pm)
    _, rows, d = qkv.shape
    loads = [[move.load(s, t) for s, t in ((proj_h, proj), (energy_h, energy), (table_h, table))]]
    for g in range(d // 256):
        cs, fs, us = slice(g * 256, (g + 1) * 256), slice(g * 128, (g + 1) * 128), slice(g * 512, (g + 1) * 512)
        if g:
            loads.append([])
        loads[g] += [move.load(uw_h.at[:, us], uw.at[:, us]), move.load(state_h.at[:, g], state.at[:, g]),
                     move.load(f_h.at[:, :, fs], f.at[:, :, fs]), move.load(gst_h.at[:, g], gst.at[:, g]),
                     move.load(qkv_h.at[:, :, cs], qkv.at[:, :, cs])]
    later = [move.load(trans_h.at[1], n1t)]
    for g in range(d // 256):
        for c in loads[g]:
            c.wait()
        cs = slice(g * 256, (g + 1) * 256)
        fs = slice(g * 128, (g + 1) * 128)
        sums = [0.0, 0.0]
        for b in range(rows // PPAD):
            mem = members(mols, b)
            rs = slice(b * PPAD, (b + 1) * PPAD)
            gfq, gfk = [], []
            for i, r, n in mem:
                ms = slice(r, r + n)
                gfq.append(dot_t(uw[ms, slice(g * 512, (g + 1) * 512)], state[i, g]))
                gfk.append(dot_t(jnp.concatenate([qkv[2, ms, cs], jnp.ones((n, 256), BF)], axis=1), gst[i, g]))
            cosb, sinb = (jnp.concatenate([table[t, :n, :] for _, _, n in mem], axis=0) for t in range(2))
            cosb = jnp.concatenate([cosb, cosb], axis=1)
            sinb = jnp.concatenate([sinb, sinb], axis=1)
            for t, gf in enumerate((gfq, gfk)):
                gp = (jnp.concatenate(gf, axis=0) * f[t, rs, fs].astype(F32)).astype(BF)
                back = dot(gp, proj[g])
                tot = dot(gp, energy[...])
                grad = (cosb * back[:, :256] + sinb * back[:, 256:] - tot * qkv[t, rs, cs].astype(F32)).astype(BF)
                gqk[t, rs, cs] = grad
                sums[t] += jnp.sum(grad.astype(F32), axis=0, keepdims=True)
        for t in range(2):
            vec_o[t:t + 1, cs] = sums[t]
    for c in later:
        c.wait()
    me = meta[0]
    products(move, pieces, (meta[3], meta[2]), stage, ((n1t, gqk.at[1 - me], send_h), (n1t, gqk.at[me], keep_h)))
    move.store(gqk, gqk_h)
    move.finish()


def query_bwd(meta, zm, pm, pieces, uw, gst, qkv, f, state, trans, proj, table, after=()):
    _, rows, d = qkv.shape
    outs = [("h", S((d, d), BF))] * 2 + [("h", S((2, rows, d), BF)), ("v", S((2, d), F32))]
    scratch = [VM(uw.shape, BF), VM(gst.shape, BF), VM(qkv.shape, BF), VM(f.shape, BF), VM(state.shape, BF), VM((d, rows), BF),
               VM(proj.shape, BF), VM((128, 256), BF), VM(table.shape, F32), VM((2, rows, d), BF), VM((2, d, d), BF)]
    args = (meta, uw, gst, qkv, f, state, trans, proj, head_const(64 ** -0.5), table)
    return call(functools.partial(query_bwd_kernel, zm, pm, pieces), "query_bwd", args, "s" + "h" * (len(args) - 1), outs, scratch,
                8 + 5 * d // 256, 2 * d**3 * 6, 12 * MIB, None, after)


def input_kernel(gqk_h, gv_h, wq_h, wk_h, wv_h, x_h, gm_h, gain_h, out_h, vec_o, gqk, gv, wq, wk, wv, x, gm, vec, e_s, out_s, sems):
    move = Mover(sems)
    rows, d = x.shape
    loads = [(move.load(gqk_h.at[0], gqk.at[0]), move.load(wq_h, wq)), (move.load(gqk_h.at[1], gqk.at[1]), move.load(wk_h, wk)),
             (move.load(gv_h, gv), move.load(wv_h, wv))]
    last = [move.load(s, t) for s, t in ((x_h, x), (gm_h, gm), (gain_h, vec))]
    for (left, right), load in zip(((gqk.at[0], wq), (gqk.at[1], wk), (gv, wv)), loads):
        for c in load:
            c.wait()
        for c in range(0, d, 256):
            cs = slice(c, c + 256)
            part = dot_t(left[...], right[cs, :])
            e_s[:, cs] = part if right is wq else e_s[:, cs] + part
    for c in last:
        c.wait()
    gain = row(vec)
    acc_g = acc_s = 0.0
    for r in range(0, rows, 256):
        rs = slice(r, r + 256)
        e = e_s[rs, :]
        n, rate = norm_parts(x[rs, :].astype(F32))
        acc_g += jnp.sum(e * n, axis=0, keepdims=True)
        acc_s += jnp.sum(e, axis=0, keepdims=True)
        eg = e * gain
        gx = rate * (eg - jnp.mean(eg, axis=-1, keepdims=True) - n * jnp.mean(eg * n, axis=-1, keepdims=True))
        out_s[rs, :] = (gm[rs, :] + gx).astype(BF)
    move.store(out_s, out_h)
    vec_o[0:1, :] = acc_g
    vec_o[1:2, :] = acc_s
    move.finish()


def input_back(gqk, gv, wq, wk, wv, x, gm, gain, after=()):
    rows, d = x.shape
    scratch = [VM(gqk.shape, BF), VM(gv.shape, BF)] + [VM((d, d), BF)] * 3 + [
        VM((rows, d), BF), VM((rows, d), F32), VM(gain.shape, F32), VM((rows, d), F32), VM((rows, d), BF)]
    args = (gqk, gv, wq, wk, wv, x, gm, gain)
    return call(input_kernel, "input_back", args, "h" * len(args), [("h", S((rows, d), BF)), ("v", S((2, d), F32))], scratch,
                16, 2 * d**3 * 3, 8 * MIB, None, after)


def layer_kernel(chunks, middle_h, vec_h, *refs):
    rights_h, rws_h = refs[:chunks], refs[chunks:2 * chunks]
    out_h, acts, rws, middle, vec, out_s, sems = refs[2 * chunks:]
    move = Mover(sems)
    base = [move.load(middle_h, middle), move.load(vec_h, vec)]
    loads = [[move.load(rights_h[k], acts.at[k]), move.load(rws_h[k], rws.at[k])] for k in range(chunks)]
    d = middle.shape[1]
    for c in base:
        c.wait()
    for k, load in enumerate(loads):
        for c in load:
            c.wait()
        for c in range(0, d, 256):
            cs = slice(c, c + 256)
            total = middle[:, cs] + sum(dot(acts[k, j], rws[k, j, :, cs]) for j in range(acts.shape[1]))
            if k + 1 < chunks:
                middle[:, cs] = total
            else:
                out_s[:, cs] = (total + row(vec)[:, cs]).astype(BF)
    move.store(out_s, out_h)
    move.finish()


def layer_end(rights, rws, middle, vec, after=()):
    rows, d = middle.shape
    k = len(rights)
    shards, _, width = rights[0].shape
    scratch = [VM((k, shards, rows, width), BF), VM((k, shards, width, d), BF), VM((rows, d), F32), VM(vec.shape, F32), VM((rows, d), BF)]
    args = (middle, vec, *rights, *rws)
    return call(functools.partial(layer_kernel, k), "layer_end", args, "h" * len(args),
                [("h", S((rows, d), BF))], scratch, 4 + 2 * k, 2 * rows * d * k * shards * width, 12 * MIB, None, after)[0]


def placed(ref, p, code, pieces):
    step = ref.shape[0] // pieces
    return ref[pl.ds(pl.multiple_of(jnp.bitwise_xor(p, code) * step, 16), step), :]


def load_halves(move, m0, m1, t0, t1, cols, both, me):
    half = m0.shape[0]
    return [move.load(m0.at[:, cols], both.at[me, :half]), move.load(m1.at[:, cols], both.at[me, half:]),
            move.load(t0.at[:, cols], both.at[1 - me, :half]), move.load(t1.at[:, cols], both.at[1 - me, half:])]


def finish_ffn_kernel(pieces, k, meta, m0, m1, t0, t1, *refs):
    ghw_h, grw_h, both, whole, wide, tall, sems = refs[-7:]
    move = Mover(sems)
    me, code = meta[0], meta[1]
    d, width = wide.shape
    for c in load_halves(move, m0, m1, t0, t1, slice(0, width), both, me):
        c.wait()
    step = d // pieces
    for p in range(pieces):
        wide[p * step:(p + 1) * step, :] = placed(both.at[0], p, code, pieces).astype(F32)
    move.store(wide, ghw_h.at[:, k * width:(k + 1) * width])
    for p in range(pieces):
        whole[p * step:(p + 1) * step, :] = placed(both.at[1], p, code, pieces)
    for c in range(0, width, 128):
        cs = slice(c, c + 128)
        tall[cs, :] = whole[:, cs].T.astype(F32)
    move.store(tall, grw_h.at[k * width:(k + 1) * width])
    move.finish()


def finish_ffn(meta, pieces, parts, k, shard, before, after=()):
    d, width = 2 * parts[0].shape[0], parts[0].shape[1]
    args = (meta, *parts, *before)
    return call(functools.partial(finish_ffn_kernel, pieces, k), "finish_ffn", args, "shhhh" + "h" * len(before),
                [("h", S((d, shard), F32)), ("h", S((shard, d), F32))],
                [VM((2, d, width), BF), VM((d, width), BF), VM((d, width), F32), VM((width, d), F32)], 8, 0, 4 * MIB,
                {5 + i: i for i in range(len(before))}, after)


def finish_pair_kernel(pieces, meta, m0, m1, t0, t1, *refs):
    outs, (both, wide, sems) = refs[:-3], refs[-3:]
    move = Mover(sems)
    me = meta[0]
    d = wide.shape[1]
    pairs = len(outs) // 2
    loads = [load_halves(move, m0, m1, t0, t1, slice(k * d, (k + 1) * d), both.at[k], me) for k in range(pairs)]
    step = d // pieces
    for k in range(pairs):
        for c in loads[k]:
            c.wait()
        for t in range(2):
            code = jnp.where(me == t, meta[2], meta[3])
            for p in range(pieces):
                wide[2 * k + t, p * step:(p + 1) * step, :] = placed(both.at[k, t], p, code, pieces).astype(F32)
            move.store(wide.at[2 * k + t], outs[2 * k + t])
    move.finish()


def finish_pair(meta, pieces, parts, d, after=()):
    pairs = parts[0].shape[1] // d
    return call(functools.partial(finish_pair_kernel, pieces), "finish_pair", (meta, *parts), "shhhh",
                [("h", S((d, d), F32))] * (2 * pairs), [VM((pairs, 2, d, d), BF), VM((2 * pairs, d, d), F32)], 4 + 6 * pairs, 0, 8 * MIB, None, after)


def bits_below(size):
    return [1 << i for i in range(size.bit_length() - 1)]


class Layout:
    def __init__(self, mesh):
        self.nb, self.nt = mesh.shape["batch"], mesh.shape["tp"]
        self.tp = [("tp", b) for b in reversed(bits_below(self.nt))]
        self.batch = [("batch", b) for b in bits_below(self.nb)[1:]]
        self.lanes = (self.tp + self.batch, self.batch[:1] + self.tp + self.batch[1:])

    def partner(self, device, level):
        b, t = divmod(device, self.nt)
        axis, bit = level
        return (b ^ bit) * self.nt + t if axis == "batch" else b * self.nt + (t ^ bit)

    def swap(self, value, level):
        pairs = []
        for device in range(self.nb * self.nt):
            core, to = device // self.nt % 2, device
            for one in level if isinstance(level, list) else [level]:
                to = self.partner(to, self.lanes[core][one] if isinstance(one, int) else one)
            pairs.append((device, to))
        return lax.ppermute(value, ("batch", "tp"), pairs)


CORE = ("batch", 1)


def code_of(levels, place):
    out = jnp.int32(0)
    for axis, bit in levels:
        out = out * 2 + (place[axis] // bit) % 2
    return out


def add(a, b):
    return (a.astype(F32) + b.astype(F32)).astype(BF)


def scatter_levels(levels, rows, least=48):
    n = 0
    while n < len(levels) and rows % 32 == 0 and rows // 2 >= least:
        rows //= 2
        n += 1
    return n


class Chain:
    def __init__(self, lay, steps):
        self.lay, self.steps, self.result = lay, steps, None
        self.go(next(steps))

    def go(self, requests):
        self.sent = [v for v, _ in requests]
        self.here = [self.lay.swap(v, level) for v, level in requests]

    def step(self):
        try:
            self.go(self.steps.send(self.here))
        except StopIteration as end:
            self.result, self.sent, self.here = end.value, [], []
        return self


def fence(arrays, *chains):
    chains = [c for c in chains if c.here]
    arrays, held = lax.optimization_barrier((arrays, [c.here for c in chains]))
    for chain, here in zip(chains, held):
        chain.here = here
        chain.step()
    return arrays


def sent(*chains):
    return tuple(v for c in chains for v in c.sent)


def halving(a, b, levels):
    for level in levels:
        n = a.shape[0] // 2
        kept = add(a[:n], b[:n])
        (b,) = yield [(add(a[n:], b[n:]), level)]
        a = kept
    return add(a, b)


def quartering(held, high, low):
    n = held.shape[0] // 4
    got = yield [(held[n:2 * n], [low]), (held[2 * n:3 * n], [high]), (held[3 * n:], [high, low])]
    return sum((g.astype(F32) for g in got), held[:n].astype(F32)).astype(BF)


def fourfold(held, high, low):
    got = yield [(held, [low]), (held, [high]), (held, [high, low])]
    return jnp.concatenate([held] + got, axis=0)


def doubling(held, levels):
    for level in levels:
        (got,) = yield [(held, level)]
        held = jnp.concatenate([held, got], axis=0)
    return held


def spread(held, level):
    other, mine = yield [(held, level), (held, CORE)]
    (rest,) = yield [(other, CORE)]
    return held, other, mine, rest


def single(held, levels):
    for level in levels:
        n = held.shape[0] // 2
        (got,) = yield [(held[n:], level)]
        held = add(held[:n], got)
    return held


def reduce_ffn(lay, gone, stay, keep):
    m = len(lay.lanes[0])
    n = gone.shape[0]
    (recv,) = yield [(gone, CORE)]
    b, recv = yield [(add(keep[n:], recv), 0), (stay, CORE)]
    held = yield from halving(add(keep[:n], recv), b, range(1, m - 2))
    held = yield from quartering(held, m - 2, m - 1)
    held = yield from doubling(held, reversed(lay.batch[1:]))
    return (yield from spread(held, lay.batch[0]))


def reduce_pair(lay, n, send, keep, ahead):
    (recv,) = yield [(send, CORE)]
    held = yield from halving(keep, recv, range(n - 2))
    held = yield from (single(held, (n - 2, n - 1)) if ahead else quartering(held, n - 2, n - 1))
    for level in range(n, len(lay.lanes[0])):
        (got,) = yield [(held, level)]
        held = add(held, got)
    return held


def gather_pairs(lay, n, held):
    held = yield from fourfold(held, n - 2, n - 1)
    held = yield from doubling(held, reversed(range(1, n - 2)))
    return (yield from spread(held, 0))


def reduce_small(lay, vectors, hidden):
    n, shard = vectors.shape[0], hidden[0].shape[0]
    for level in lay.tp:
        bit = level[1]
        (got,) = yield [(jnp.concatenate([vectors] + [hidden[j + bit] for j in range(bit)]), level)]
        vectors = vectors + got[:n]
        hidden = [hidden[j] + got[n + j * shard:n + (j + 1) * shard] for j in range(bit)]
    held = jnp.concatenate([vectors, hidden[0]])
    for level in [CORE] + lay.batch:
        (got,) = yield [(held, level)]
        held = held + got
    return held


def on_device(
    lay,
    inputs,
    cotangent,
    zinc_lengths,
    pubchem_lengths,
    feature_stack,
    train_step,
    redraw_interval,
    attn_gain,
    attn_shift,
    query_weight,
    query_bias,
    key_weight,
    key_bias,
    value_weight,
    value_bias,
    output_weight,
    output_bias,
    ffn_gain,
    ffn_shift,
    hidden_weight,
    hidden_bias,
    return_weight,
    return_bias,
):
    nt = lay.nt
    d, shard = hidden_weight.shape
    rows = inputs.shape[0]
    width = min(768, shard)
    chunks = shard // width
    zm, pm = zinc_lengths.shape[0], pubchem_lengths.shape[0]
    place = {"batch": lax.axis_index("batch"), "tp": lax.axis_index("tp")}
    core = place["batch"] % 2

    def shares(k):
        hw = lax.dynamic_slice(hidden_weight, (core * (d // 2), k * width), (d // 2, width))
        rw = lax.dynamic_slice(return_weight, (k * width + core * (width // 2), 0), (width // 2, d))
        return [jnp.concatenate([hw, rw], axis=0)] if width == d else [hw, rw]

    def from_tp(own):
        pool = {0: own}
        for level in lay.tp:
            for j in list(pool):
                pool[j | level[1]] = [lay.swap(v, level) for v in pool[j]]
        return [v for j in range(1, nt) for v in pool[j]]

    own = [shares(k) for k in range(chunks)]
    per = len(own[0])
    biases = from_tp([hidden_bias])
    here = {k: from_tp(own[k]) for k in range(chunks)}

    n_pair = scatter_levels(lay.lanes[0], d)
    codes = [code_of(lane[:n_pair], place) for lane in lay.lanes]
    pick = train_step[0] // redraw_interval[0] % feature_stack.shape[0]
    meta = jnp.stack([core, code_of(lay.batch, place), jnp.where(core == 0, codes[0], codes[1]), jnp.where(core == 0, codes[1], codes[0]),
                      code_of(lay.batch[:-2], place) * 4, pick]).astype(jnp.int32)
    table = rotary_const()

    out = attend_fwd(
        meta, zinc_lengths, pubchem_lengths, cotangent, inputs,
        (attn_gain, attn_shift, query_bias, key_bias, value_bias, output_bias, ffn_gain, ffn_shift),
        query_weight, key_weight, value_weight, output_weight, feature_stack, table)
    out, here[0], biases = lax.optimization_barrier((out, here[0], biases))
    qkv, f, state, trans, middle, n2, left, proj = out

    pieces, pair_pieces = 2 ** len(lay.batch), 2 ** n_pair
    chains, acts, rws, hidden, before = [], [], [], [], ()
    for k in range(chunks):
        near = [lay.swap(v, CORE) for v in here[k]]
        if chains:
            near = fence(near, chains[-1])
        parts = [[v[i] for i in range(j * per, (j + 1) * per) for v in (here[k], near)] for j in range(nt - 1)]
        out = ffn_chunk(meta, pieces, nt, n2, left, cotangent, hidden_bias, hidden_weight, return_weight, parts, biases, k, width,
                        before, sent(*chains))
        if k + 1 < chunks:
            out, here[k + 1] = lax.optimization_barrier((out, here[k + 1]))
        gone, stay, keep, act, bias, e, rw = fence(out, *chains)
        before = (e,)
        chains.append(Chain(lay, reduce_ffn(lay, gone, stay, keep)))
        acts.append(act)
        rws.append(rw)
        hidden.append(bias)

    middle = fence(middle, chains[-1])
    out = mid(e, cotangent, middle, output_weight, ffn_gain, sent(*chains))
    gm, gb, gatt, vec1 = fence(out, *chains[:-1])
    out = value_bwd(meta, zm, pm, pair_pieces, gatt, gb, f, state, trans, sent(*chains))
    send, keep, gv, uw, gst, vec2 = fence(out, *chains)
    pair_a = Chain(lay, reduce_pair(lay, n_pair, send, keep, True))
    uw = fence(uw, pair_a)
    out = query_bwd(meta, zm, pm, pair_pieces, uw, gst, qkv, f, state, trans, proj, table, sent(pair_a, *chains))
    send, keep, gqk, vec3 = fence(out, pair_a, *chains)
    pair_b = Chain(lay, reduce_pair(lay, n_pair, send, keep, False))
    gqk = fence(gqk, pair_b)
    out = input_back(gqk, gv, query_weight, key_weight, value_weight, inputs, gm, attn_gain, sent(pair_a, pair_b, *chains))
    (input_grad, vec4), middle = fence((out, middle), pair_a, pair_b, *chains)
    layer_out = layer_end(acts, rws, middle, return_bias, sent(pair_b, pair_a, *chains))
    layer_out, vec4 = fence((layer_out, vec4), pair_b, pair_a, *chains)
    vec3 = jnp.concatenate([vec3, vec4], axis=0)
    vectors = jnp.concatenate([vec1, vec2, vec3], axis=0).reshape(-1)
    small = Chain(lay, reduce_small(lay, vectors, [jnp.concatenate([hidden[k][j] for k in range(chunks)]) for j in range(nt)]))

    ffn_out, k, turn, pairs = (), 0, 0, None
    while pairs is None or pairs.here or any(c.here for c in chains):
        every = [pairs] if pairs else [pair_b, pair_a]
        every += chains + ([small] if turn else [])
        turn += 1
        if k < chunks and chains[k].result is not None:
            ffn_out = finish_ffn(meta, pieces, chains[k].result, k, shard, ffn_out, sent(*every))
            k += 1
            ffn_out = fence(ffn_out, *every)
        else:
            fence((), *every)
        if pairs is None and pair_a.result is not None and pair_b.result is not None:
            pairs = Chain(lay, gather_pairs(lay, n_pair, jnp.concatenate([pair_a.result, pair_b.result], axis=1)))
    while k < chunks:
        ffn_out = finish_ffn(meta, pieces, chains[k].result, k, shard, ffn_out, sent(small))
        k += 1
    gwo, gwv, gwq, gwk = finish_pair(meta, pair_pieces, pairs.result, d, sent(small))
    while small.here:
        small.step()
    vecs = small.result[:9 * d].reshape(9, d)
    return (layer_out, input_grad, vecs[7], vecs[8], gwq, vecs[5], gwk, vecs[6], gwv, vecs[4], gwo, vecs[2],
            vecs[0], vecs[1], ffn_out[0], small.result[9 * d:], ffn_out[1], vecs[3])


def solution(mesh):
    rows, whole, hidden = P(("batch", "tp"), None), P(), P(None, "tp")
    return jax.shard_map(
        functools.partial(on_device, Layout(mesh)),
        mesh=mesh,
        in_specs=(rows, rows, P(("batch", "tp")), P(("batch", "tp"))) + (whole,) * 15 + (hidden, P("tp"), P("tp", None), whole),
        out_specs=(rows, rows) + (whole,) * 12 + (hidden, P("tp"), P("tp", None), whole),
        check_vma=False,
    )
```

```python
import functools
import math

import jax
import jax.numpy as jnp
import numpy as np
from jax import lax
from jax.experimental import pallas as pl
from jax.experimental.pallas import tpu as pltpu
from jax.sharding import PartitionSpec as P

ZPAD = 64
PPAD = 256
F32 = jnp.float32
BF = jnp.bfloat16
VM = pltpu.VMEM
GROUP = 4
S = jax.ShapeDtypeStruct
TIMES = {"attend_fwd": 24, "ffn_chunk": 17, "layer_end": 9, "mid": 8, "value_bwd": 13, "query_bwd": 13, "input_back": 10, "finish_ffn": 5, "finish_pair": 5}
MIB = 2**20
GRANT = 60


def dot(a, b):
    return jnp.dot(a, b, preferred_element_type=F32)


def dot_t(a, b):
    return lax.dot_general(a, b, (((1,), (1,)), ((), ())), preferred_element_type=F32)


def dot_c(a, b):
    return lax.dot_general(a, b, (((0,), (0,)), ((), ())), preferred_element_type=F32)


def split(v):
    hi = v.astype(BF)
    return hi, (v - hi.astype(F32)).astype(BF)


def norm_parts(values):
    center = values - jnp.mean(values, axis=-1, keepdims=True)
    rate = lax.rsqrt(jnp.mean(center * center, axis=-1, keepdims=True) + 1e-05)
    return center * rate, rate


def row(ref):
    return ref[...].reshape(1, -1)


def block_mask(width):
    f = lax.broadcasted_iota(jnp.int32, (128, width), 0) // 32
    c = lax.broadcasted_iota(jnp.int32, (128, width), 1) % 256 // 64
    return f == c


def molecules(zm, pm):
    return [(i * ZPAD, ZPAD) for i in range(zm)] + [(zm * ZPAD + i * PPAD, PPAD) for i in range(pm)]


def members(mols, b):
    return [(i, r, n) for i, (r, n) in enumerate(mols) if b * PPAD <= r < (b + 1) * PPAD]


class Mover:
    def __init__(self, sems):
        self.sems, self.n, self.out = sems, 0, []

    def load(self, src, dst):
        copy = pltpu.make_async_copy(src, dst, self.sems.at[self.n])
        self.n += 1
        copy.start()
        return copy

    def store(self, src, dst):
        self.out.append(self.load(src, dst))

    def finish(self):
        for copy in self.out:
            copy.wait()


def call(kernel, name, args, spaces, outs, scratch, copies, flops, moved, aliases=None, after=()):
    n, extra = len(args), len(after)

    def body(*refs):
        kernel(*refs[:n], *refs[n + extra:])

    spec = {
        "v": pl.BlockSpec(memory_space=VM),
        "h": pl.BlockSpec(memory_space=pltpu.HBM),
        "s": pl.BlockSpec(memory_space=pltpu.SMEM),
    }
    return pl.pallas_call(
        body,
        out_shape=tuple(o for _, o in outs),
        in_specs=[spec[s] for s in spaces] + [spec["h"]] * extra,
        out_specs=tuple(spec[s] for s, _ in outs),
        scratch_shapes=list(scratch) + [pltpu.SemaphoreType.DMA((copies,))],
        input_output_aliases=aliases or {},
        compiler_params=pltpu.CompilerParams(vmem_limit_bytes=GRANT * MIB),
        cost_estimate=pl.CostEstimate(flops=int(TIMES[name] * 1.15e9), bytes_accessed=moved, transcendentals=0),
        name=name,
    )(*args, *after)


def place_heads(scaled):
    two = jnp.concatenate([scaled, scaled], axis=1)
    return jnp.where(block_mask(256), jnp.concatenate([two, two], axis=1), 0.0)


def attend_fwd_kernel(zm, pm, meta, zlen, plen, cot_h, x_h, gain_h, shift_h, bq_h, bk_h, bv_h, bo_h, gain2_h, shift2_h,
                      wq_h, wk_h, wv_h, wo_h, stack_h, table_h, energy_h,
                      qkv_h, f_h, state_h, trans_h, middle_h, n2_h, left_h, proj_h,
                      cot, n2_s, left, x, vec, wq, wk, wv, wo, fp, proj, table, energy, qkv, f_s, state_s, trans, middle_s, att_s, sems):
    move = Mover(sems)
    rows, d = x.shape
    first = [move.load(x_h, x), move.load(gain_h, vec.at[0]), move.load(shift_h, vec.at[1]), move.load(stack_h.at[meta[5]], fp),
             move.load(cot_h, cot)]
    later = [move.load(s, t) for s, t in ((wq_h, wq), (bq_h, vec.at[2]), (table_h, table), (energy_h, energy), (wk_h, wk),
                                          (bk_h, vec.at[3]), (wv_h, wv), (bv_h, vec.at[4]))]
    last = [move.load(s, t) for s, t in ((wo_h, wo), (bo_h, vec.at[5]), (gain2_h, vec.at[6]), (shift2_h, vec.at[7]))]
    mols = molecules(zm, pm)
    groups = d // 256
    blocks = range(rows // PPAD)
    keep = block_mask(512)
    ones = jnp.ones((PPAD, 256), BF)

    def vector(i):
        return vec[i].reshape(1, -1)

    for c in first:
        c.wait()
    for g in range(groups):
        p = fp[g * GROUP:(g + 1) * GROUP].reshape(GROUP * 32, 64) * 64 ** -0.25
        turned = jnp.concatenate([p[:, 32:], -p[:, :32]], axis=1)
        hi, lo = split(jnp.concatenate([place_heads(p), place_heads(turned)], axis=1))
        proj[0, g] = hi
        proj[1, g] = lo
    n1s = {}
    for b in blocks:
        rs = slice(b * PPAD, (b + 1) * PPAD)
        normed, _ = norm_parts(x[rs, :].astype(F32))
        n1s[b] = (normed * vector(0) + vector(1)).astype(BF)
        trans[1, :, rs] = n1s[b].T
        left[1, :, rs] = cot[rs, :].T
    for c in later:
        c.wait()
    move.store(proj.at[0], proj_h)
    move.store(trans.at[1], trans_h.at[1])
    move.store(left.at[1], left_h.at[1])
    for b in blocks:
        mem = members(mols, b)
        rs = slice(b * PPAD, (b + 1) * PPAD)
        n1 = n1s[b]
        cosb, sinb = (jnp.concatenate([table[t, :n, :] for _, _, n in mem], axis=0) for t in range(2))
        cosb = jnp.concatenate([cosb, cosb], axis=1)
        sinb = jnp.concatenate([sinb, sinb], axis=1)
        live = jnp.concatenate(
            [(lax.broadcasted_iota(jnp.int32, (n, 128), 0) < (zlen[i] if i < zm else plen[i - zm])).astype(F32) for i, r, n in mem], axis=0)
        for g in range(groups):
            cs = slice(g * 256, (g + 1) * 256)
            fs = slice(g * 128, (g + 1) * 128)

            def features(w, bias, slot):
                v = dot(n1, w[:, cs]) + vector(bias)[:, cs]
                qkv[slot, rs, cs] = v.astype(BF)
                ch, cl = split(v * cosb)
                sh, sl = split(v * sinb)
                eh, el = split(v * v)
                ph, plo = proj[0, g], proj[1, g]
                e = energy[...]
                inner = (dot_t(ch, ph[:, :256]) + dot_t(sh, ph[:, 256:]) + dot_t(cl, ph[:, :256]) + dot_t(sl, ph[:, 256:])
                         + dot_t(ch, plo[:, :256]) + dot_t(sh, plo[:, 256:]) - dot_t(eh, e) - dot_t(el, e))
                return jnp.exp(inner) * (32 ** -0.5)

            fq = features(wq, 2, 0).astype(BF)
            fk = (features(wk, 3, 1) * live).astype(BF)
            f_s[0, rs, fs] = fq
            f_s[1, rs, fs] = fk
            v = (dot(n1, wv[:, cs]) + vector(4)[:, cs]).astype(BF)
            qkv[2, rs, cs] = v
            for i, r, n in mem:
                ms = slice(r - b * PPAD, r - b * PPAD + n)
                vo = jnp.concatenate([v[ms], ones[:n]], axis=1)
                state = jnp.where(keep, dot_c(fk[ms], vo), 0.0).astype(BF)
                state_s[i, g] = state
                nd = dot(fq[ms], state)
                att_s[r:r + n, cs] = (nd[:, :256] / nd[:, 256:]).astype(BF)
    for s, t in ((qkv, qkv_h), (f_s, f_h), (state_s, state_h)):
        move.store(s, t)
    for c in last:
        c.wait()
    for b in blocks:
        rs = slice(b * PPAD, (b + 1) * PPAD)
        trans[0, :, rs] = att_s[rs, :].T
        middle = x[rs, :].astype(F32) + (dot(att_s[rs, :], wo[...]) + vector(5))
        middle_s[rs, :] = middle
        normed, _ = norm_parts(middle)
        n2 = (normed * vector(6) + vector(7)).astype(BF)
        n2_s[rs, :] = n2
        left[0, :, rs] = n2.T
    move.store(middle_s, middle_h)
    move.store(n2_s, n2_h)
    move.store(trans.at[0], trans_h.at[0])
    move.store(left.at[0], left_h.at[0])
    move.finish()


def rotary_const():
    place = np.arange(PPAD, dtype=np.float64)
    rates = np.exp(np.arange(32, dtype=np.float64) * (-2.0 * math.log(10000.0) / 64))
    ang = place[:, None] * rates[None, :]
    return np.tile(np.stack([np.cos(ang), np.sin(ang)]), (1, 1, 4)).astype(np.float32)


def head_const(scale):
    f = np.arange(128)[:, None] // 32
    c = np.arange(256)[None, :] // 64
    return ((f == c) * scale).astype(jnp.bfloat16)


def attend_fwd(meta, zlen, plen, cot, x, vectors, wq, wk, wv, wo, stack, table):
    rows, d = x.shape
    zm, pm = zlen.shape[0], plen.shape[0]
    groups = d // 256
    states = (zm + pm, groups, 128, 512)
    outs = [S((3, rows, d), BF), S((2, rows, d // 2), BF), S(states, BF), S((2, d, rows), BF),
            S((rows, d), F32), S((rows, d), BF), S((2, d, rows), BF), S((groups, 128, 512), BF)]
    args = (meta, zlen, plen, cot, x, *vectors, wq, wk, wv, wo, stack, table, head_const(1 / 16))
    scratch = ([VM((rows, d), BF)] * 2 + [VM((2, d, rows), BF), VM((rows, d), BF), VM((8, d), F32)] + [VM((d, d), BF)] * 4
               + [VM(stack.shape[1:], F32), VM((2, groups, 128, 512), BF), VM(table.shape, F32), VM((128, 256), BF)]
               + [VM((3, rows, d), BF), VM((2, rows, d // 2), BF), VM(states, BF), VM((2, d, rows), BF), VM((rows, d), F32), VM((rows, d), BF)])
    return call(
        functools.partial(attend_fwd_kernel, zm, pm), "attend_fwd", args, "sss" + "h" * (len(args) - 3),
        [("h", o) for o in outs], scratch, 32, 2 * rows * d * d * 4, 16 * MIB)


def gelu_parts(h):
    bell = jnp.exp(h * h * -0.5)
    t = 1.0 / (1.0 + (0.3275911 * math.sqrt(0.5)) * jnp.abs(h))
    poly = t * (0.127414796 + t * (-0.142248368 + t * (0.7107068705 + t * (-0.7265760135 + t * 0.5307027145))))
    tail = poly * bell
    phi = jnp.where(h >= 0, 1.0 - tail, tail)
    return h * phi, phi + h * bell * (1.0 / math.sqrt(2 * math.pi))


def place_pieces(code, src, dst):
    n, step = src.shape[0], src.shape[1]
    for p in range(n):
        off = pl.multiple_of(jnp.bitwise_xor(p, code) * step, 16)
        dst[pl.ds(off, step), :] = src[p]


def ffn_kernel(pieces, shards, k, per, meta, n2_h, left_h, cot_h, hb_h, hw_h, rw_h, *refs):
    parts = {j: refs[(j - 1) * per:j * per] for j in range(1, shards)}
    hbs = refs[(shards - 1) * per:(shards - 1) * (per + 1)]
    e_prev = refs[(shards - 1) * (per + 1)] if k else None
    (gone_h, stay_h, keep_h, act_h, bias_o, e_h, rws_h, n2, left, cot, hb, hw, rw, hw2, rw2, right, stage, e_s, sems) = refs[-19:]
    move = Mover(sems)
    d, width = hw.shape[1:]
    half_d = d // 2
    me, code = meta[0], meta[1]
    order = list(range(1, shards)) + [0]
    early, late = {}, {}
    for j in order:
        early[j] = [move.load(hbs[j - 1] if j else hb_h, hb.at[j])]
        if j == order[0]:
            early[j].append(move.load(n2_h, n2))
        late[j] = []
        if j == 0:
            early[j].append(move.load(hw_h.at[:, k * width:(k + 1) * width], hw.at[0]))
            late[j].append(move.load(rw_h.at[k * width:(k + 1) * width, :], rw.at[0]))
        elif per == 2:
            early[j] += [move.load(parts[j][p].at[:half_d], hw2.at[j - 1, p]) for p in range(2)]
            late[j] += [move.load(parts[j][p].at[half_d:], rw2.at[j - 1, p]) for p in range(2)]
        else:
            early[j] += [move.load(parts[j][p], hw2.at[j - 1, p]) for p in range(2)]
            late[j] += [move.load(parts[j][2 + p], rw2.at[j - 1, p]) for p in range(2)]
        if j == order[0]:
            late[j].append(move.load(cot_h, cot))
    last = [move.load(left_h, left)]
    if k:
        last.append(move.load(e_prev, e_s))
    step, half = d // pieces, pieces // 2
    tile = width
    for j in order:
        for c in early[j] + late[j]:
            c.wait()
        if j:
            place_pieces(me, hw2.at[j - 1], hw.at[j])
            place_pieces(me, rw2.at[j - 1], rw.at[j])
        bias = hb[j].reshape(1, -1)[:, k * width:(k + 1) * width].astype(F32)
        for c in range(0, width, tile):
            cs = slice(c, c + tile)
            h = dot(n2[...], hw[j, :, cs]) + bias[:, cs]
            act, slope = gelu_parts(h)
            ga = dot_t(cot[...], rw[j, cs, :])
            gh = (ga * slope).astype(BF)
            right[0, j, :, cs] = gh
            right[1, j, :, cs] = act.astype(BF)
            bias_o[j:j + 1, cs] = jnp.sum(gh.astype(F32), axis=0, keepdims=True)
        move.store(right.at[1, j], act_h.at[j])
        move.store(rw.at[j], rws_h.at[j])
    for c in last:
        c.wait()
    for c in range(0, d, 768):
        cs = slice(c, c + 768)
        part = sum(dot_t(right[0, j], hw[j, cs, :]) for j in order)
        e_s[:, cs] = e_s[:, cs] + part if k else part
    move.store(e_s, e_h)
    for kind, slot in ((1 - me, 0), (me, 1)):
        for j in order:
            for c in range(0, width, tile):
                cs = slice(c, c + tile)
                value = dot(left[kind], right[kind, j, :, cs]).astype(BF)
                for p in range(pieces):
                    rel = jnp.bitwise_xor(p, code)
                    second = rel // half * (shards * half) + j * half + rel % half
                    off = pl.multiple_of(jnp.where(kind == 0, j * pieces + rel, second) * step, 16)
                    stage[slot, pl.ds(off, step), cs] = value[p * step:(p + 1) * step]
        if slot:
            move.store(stage.at[1], keep_h)
        else:
            cut = shards * d // 2
            move.store(stage.at[0, cut:], gone_h)
            move.store(stage.at[0, :cut], stay_h)
    move.finish()


def ffn_chunk(meta, pieces, shards, n2, left, cot, hb, hw, rw, parts, hbs, k, width, before, after=()):
    rows, d = n2.shape
    per = len(parts[0])
    part = S((shards * d // 2, width), BF)
    outs = [("h", part), ("h", part), ("h", S((shards * d, width), BF)), ("h", S((shards, rows, width), BF)), ("v", S((shards, width), F32)),
            ("h", S((rows, d), F32)), ("h", S((shards, width, d), BF))]
    scratch = [VM((rows, d), BF), VM((2, d, rows), BF), VM((rows, d), BF), VM((shards, 1) + hb.shape, BF), VM((shards, d, width), BF),
               VM((shards, width, d), BF), VM((shards - 1, 2, d // 2, width), BF), VM((shards - 1, 2, width // 2, d), BF),
               VM((2, shards, rows, width), BF), VM((2, shards * d, width), BF), VM((rows, d), F32)]
    args = (meta, n2, left, cot, hb.reshape(1, -1), hw, rw) + tuple(p for part in parts for p in part) + tuple(b.reshape(1, -1) for b in hbs) + tuple(before)
    return call(
        functools.partial(ffn_kernel, pieces, shards, k, per), "ffn_chunk", args,
        "s" + "h" * (len(args) - 1), outs, scratch, 12 + 13 * shards, 2 * rows * d * width * 5 * shards, 12 * MIB, None, after)


def products(move, pieces, codes, stage, outs):
    for slot, (left, right, out) in enumerate(outs):
        d = out.shape[0]
        step = d // pieces
        for c in range(0, d, 768):
            cs = slice(c, c + 768)
            value = dot(left[...], right[:, cs]).astype(BF)
            for p in range(pieces):
                off = pl.multiple_of(jnp.bitwise_xor(p, codes[slot]) * step, 16)
                stage[slot, pl.ds(off, step), cs] = value[p * step:(p + 1) * step]
        move.store(stage.at[slot], out)


def mid_kernel(e_h, cot_h, middle_h, wo_h, vec_h, gm_h, gb_h, gatt_h, vec_o, e_s, cot, middle, wo, vec, gm_s, gb_s, gatt, sems):
    move = Mover(sems)
    rows, d = middle.shape
    loads = [[move.load(s.at[r:r + 256], t.at[r:r + 256]) for s, t in ((middle_h, middle), (e_h, e_s), (cot_h, cot))]
             for r in range(0, rows, 256)]
    gain = move.load(vec_h, vec)
    last = move.load(wo_h, wo)
    gain.wait()
    gain2 = row(vec)
    acc_g = acc_s = acc_b = acc_c = 0.0
    for i, r in enumerate(range(0, rows, 256)):
        for c in loads[i]:
            c.wait()
        rs = slice(r, r + 256)
        e = e_s[rs, :]
        n, rate = norm_parts(middle[rs, :])
        c = cot[rs, :].astype(F32)
        acc_g += jnp.sum(e * n, axis=0, keepdims=True)
        acc_s += jnp.sum(e, axis=0, keepdims=True)
        acc_c += jnp.sum(c, axis=0, keepdims=True)
        eg = e * gain2
        gm = c + rate * (eg - jnp.mean(eg, axis=-1, keepdims=True) - n * jnp.mean(eg * n, axis=-1, keepdims=True))
        gm_s[rs, :] = gm
        gb = gm.astype(BF)
        gb_s[rs, :] = gb
        acc_b += jnp.sum(gb.astype(F32), axis=0, keepdims=True)
    for i, acc in enumerate((acc_g, acc_s, acc_b, acc_c)):
        vec_o[i:i + 1, :] = acc
    move.store(gm_s, gm_h)
    move.store(gb_s, gb_h)
    last.wait()
    for c in range(0, d, 768):
        cs = slice(c, c + 768)
        gatt[:, cs] = dot_t(gb_s[...], wo[cs, :]).astype(BF)
    move.store(gatt, gatt_h)
    move.finish()


def mid(e, cot, middle, wo, gain2, after=()):
    rows, d = middle.shape
    outs = [("h", S((rows, d), F32)), ("h", S((rows, d), BF)), ("h", S((rows, d), BF)), ("v", S((4, d), F32))]
    scratch = [VM((rows, d), F32), VM((rows, d), BF), VM((rows, d), F32), VM((d, d), BF), VM(gain2.shape, F32), VM((rows, d), F32),
               VM((rows, d), BF), VM((rows, d), BF)]
    args = (e, cot, middle, wo, gain2)
    return call(mid_kernel, "mid", args, "h" * len(args), outs, scratch, 8 + 3 * (rows // 256), 2 * rows * d * d, 8 * MIB, None, after)


def value_bwd_kernel(zm, pm, pieces, meta, gatt_h, gb_h, f_h, state_h, trans_h,
                     send_h, keep_h, gv_h, uw_h, gst_h, vec_o, gatt, uw_o, gst_o, f, state, left, right, stage, sems):
    move = Mover(sems)
    mols = molecules(zm, pm)
    rows, d = gatt.shape
    groups = d // 256
    loads = []
    for g in range(groups):
        cs, fs = slice(g * 256, (g + 1) * 256), slice(g * 128, (g + 1) * 128)
        loads.append([move.load(f_h.at[:, :, fs], f.at[:, :, fs]), move.load(state_h.at[:, g], state.at[:, g]),
                      move.load(gatt_h.at[:, cs], gatt.at[:, cs])])
    last = [move.load(trans_h, left), move.load(gb_h, right.at[0])]
    keep = block_mask(512)
    for g in range(groups):
        for c in loads[g]:
            c.wait()
        cs = slice(g * 256, (g + 1) * 256)
        fs = slice(g * 128, (g + 1) * 128)
        total = 0.0
        for i, (r, n) in enumerate(mols):
            ms = slice(r, r + n)
            st = state[i, g]
            q = f[0, ms, fs]
            nd = dot(q, st)
            rden = 1.0 / nd[:, 256:]
            u = gatt[ms, cs].astype(F32) * rden
            uw = jnp.concatenate([u, -(u * (nd[:, :256] * rden))], axis=1).astype(BF)
            uw_o[ms, slice(g * 512, (g + 1) * 512)] = uw
            gst = jnp.where(keep, dot_c(q, uw), 0.0).astype(BF)
            gst_o[i, g] = gst
            gv = dot(f[1, ms, fs], gst[:, :256]).astype(BF)
            right[1, ms, cs] = gv
            total += jnp.sum(gv.astype(F32), axis=0, keepdims=True)
        vec_o[0:1, cs] = total
    move.store(right.at[1], gv_h)
    move.store(uw_o, uw_h)
    move.store(gst_o, gst_h)
    for c in last:
        c.wait()
    me = meta[0]
    products(move, pieces, (meta[3], meta[2]), stage, ((left.at[1 - me], right.at[1 - me], send_h), (left.at[me], right.at[me], keep_h)))
    move.finish()


def value_bwd(meta, zm, pm, pieces, gatt, gb, f, state, trans, after=()):
    rows, d = gatt.shape
    outs = [("h", S((d, d), BF))] * 2 + [("h", S((rows, d), BF)), ("h", S((rows, 2 * d), BF)), ("h", S(state.shape, BF)), ("v", S((1, d), F32))]
    scratch = [VM((rows, d), BF), VM((rows, 2 * d), BF), VM(state.shape, BF), VM(f.shape, BF), VM(state.shape, BF), VM((2, d, rows), BF),
               VM((2, rows, d), BF), VM((2, d, d), BF)]
    args = (meta, gatt, gb, f, state, trans)
    return call(functools.partial(value_bwd_kernel, zm, pm, pieces), "value_bwd", args, "shhhhh", outs, scratch,
                10 + 3 * d // 256, 2 * d**3 * 3, 8 * MIB, None, after)


def query_bwd_kernel(zm, pm, pieces, meta, uw_h, gst_h, qkv_h, f_h, state_h, trans_h, proj_h, energy_h, table_h,
                     send_h, keep_h, gqk_h, vec_o, uw, gst, qkv, f, state, n1t, proj, energy, table, gqk, stage, sems):
    move = Mover(sems)
    mols = molecules(zm, pm)
    _, rows, d = qkv.shape
    loads = [[move.load(s, t) for s, t in ((proj_h, proj), (energy_h, energy), (table_h, table))]]
    for g in range(d // 256):
        cs, fs, us = slice(g * 256, (g + 1) * 256), slice(g * 128, (g + 1) * 128), slice(g * 512, (g + 1) * 512)
        if g:
            loads.append([])
        loads[g] += [move.load(uw_h.at[:, us], uw.at[:, us]), move.load(state_h.at[:, g], state.at[:, g]),
                     move.load(f_h.at[:, :, fs], f.at[:, :, fs]), move.load(gst_h.at[:, g], gst.at[:, g]),
                     move.load(qkv_h.at[:, :, cs], qkv.at[:, :, cs])]
    later = [move.load(trans_h.at[1], n1t)]
    for g in range(d // 256):
        for c in loads[g]:
            c.wait()
        cs = slice(g * 256, (g + 1) * 256)
        fs = slice(g * 128, (g + 1) * 128)
        sums = [0.0, 0.0]
        for b in range(rows // PPAD):
            mem = members(mols, b)
            rs = slice(b * PPAD, (b + 1) * PPAD)
            gfq, gfk = [], []
            for i, r, n in mem:
                ms = slice(r, r + n)
                gfq.append(dot_t(uw[ms, slice(g * 512, (g + 1) * 512)], state[i, g]))
                gfk.append(dot_t(jnp.concatenate([qkv[2, ms, cs], jnp.ones((n, 256), BF)], axis=1), gst[i, g]))
            cosb, sinb = (jnp.concatenate([table[t, :n, :] for _, _, n in mem], axis=0) for t in range(2))
            cosb = jnp.concatenate([cosb, cosb], axis=1)
            sinb = jnp.concatenate([sinb, sinb], axis=1)
            for t, gf in enumerate((gfq, gfk)):
                gp = (jnp.concatenate(gf, axis=0) * f[t, rs, fs].astype(F32)).astype(BF)
                back = dot(gp, proj[g])
                tot = dot(gp, energy[...])
                grad = (cosb * back[:, :256] + sinb * back[:, 256:] - tot * qkv[t, rs, cs].astype(F32)).astype(BF)
                gqk[t, rs, cs] = grad
                sums[t] += jnp.sum(grad.astype(F32), axis=0, keepdims=True)
        for t in range(2):
            vec_o[t:t + 1, cs] = sums[t]
    for c in later:
        c.wait()
    me = meta[0]
    products(move, pieces, (meta[3], meta[2]), stage, ((n1t, gqk.at[1 - me], send_h), (n1t, gqk.at[me], keep_h)))
    move.store(gqk, gqk_h)
    move.finish()


def query_bwd(meta, zm, pm, pieces, uw, gst, qkv, f, state, trans, proj, table, after=()):
    _, rows, d = qkv.shape
    outs = [("h", S((d, d), BF))] * 2 + [("h", S((2, rows, d), BF)), ("v", S((2, d), F32))]
    scratch = [VM(uw.shape, BF), VM(gst.shape, BF), VM(qkv.shape, BF), VM(f.shape, BF), VM(state.shape, BF), VM((d, rows), BF),
               VM(proj.shape, BF), VM((128, 256), BF), VM(table.shape, F32), VM((2, rows, d), BF), VM((2, d, d), BF)]
    args = (meta, uw, gst, qkv, f, state, trans, proj, head_const(64 ** -0.5), table)
    return call(functools.partial(query_bwd_kernel, zm, pm, pieces), "query_bwd", args, "s" + "h" * (len(args) - 1), outs, scratch,
                8 + 5 * d // 256, 2 * d**3 * 6, 12 * MIB, None, after)


def input_kernel(gqk_h, gv_h, wq_h, wk_h, wv_h, x_h, gm_h, gain_h, out_h, vec_o, gqk, gv, wq, wk, wv, x, gm, vec, e_s, out_s, sems):
    move = Mover(sems)
    rows, d = x.shape
    loads = [(move.load(gqk_h.at[0], gqk.at[0]), move.load(wq_h, wq)), (move.load(gqk_h.at[1], gqk.at[1]), move.load(wk_h, wk)),
             (move.load(gv_h, gv), move.load(wv_h, wv))]
    last = [move.load(s, t) for s, t in ((x_h, x), (gm_h, gm), (gain_h, vec))]
    for (left, right), load in zip(((gqk.at[0], wq), (gqk.at[1], wk), (gv, wv)), loads):
        for c in load:
            c.wait()
        for c in range(0, d, 768):
            cs = slice(c, c + 768)
            part = dot_t(left[...], right[cs, :])
            e_s[:, cs] = part if right is wq else e_s[:, cs] + part
    for c in last:
        c.wait()
    gain = row(vec)
    acc_g = acc_s = 0.0
    for r in range(0, rows, 256):
        rs = slice(r, r + 256)
        e = e_s[rs, :]
        n, rate = norm_parts(x[rs, :].astype(F32))
        acc_g += jnp.sum(e * n, axis=0, keepdims=True)
        acc_s += jnp.sum(e, axis=0, keepdims=True)
        eg = e * gain
        gx = rate * (eg - jnp.mean(eg, axis=-1, keepdims=True) - n * jnp.mean(eg * n, axis=-1, keepdims=True))
        out_s[rs, :] = (gm[rs, :] + gx).astype(BF)
    move.store(out_s, out_h)
    vec_o[0:1, :] = acc_g
    vec_o[1:2, :] = acc_s
    move.finish()


def input_back(gqk, gv, wq, wk, wv, x, gm, gain, after=()):
    rows, d = x.shape
    scratch = [VM(gqk.shape, BF), VM(gv.shape, BF)] + [VM((d, d), BF)] * 3 + [
        VM((rows, d), BF), VM((rows, d), F32), VM(gain.shape, F32), VM((rows, d), F32), VM((rows, d), BF)]
    args = (gqk, gv, wq, wk, wv, x, gm, gain)
    return call(input_kernel, "input_back", args, "h" * len(args), [("h", S((rows, d), BF)), ("v", S((2, d), F32))], scratch,
                16, 2 * d**3 * 3, 8 * MIB, None, after)


def layer_kernel(chunks, middle_h, vec_h, *refs):
    rights_h, rws_h = refs[:chunks], refs[chunks:2 * chunks]
    out_h, acts, rws, middle, vec, out_s, sems = refs[2 * chunks:]
    move = Mover(sems)
    base = [move.load(middle_h, middle), move.load(vec_h, vec)]
    loads = [[move.load(rights_h[k], acts.at[k]), move.load(rws_h[k], rws.at[k])] for k in range(chunks)]
    d = middle.shape[1]
    for c in base:
        c.wait()
    for k, load in enumerate(loads):
        for c in load:
            c.wait()
        for c in range(0, d, 768):
            cs = slice(c, c + 768)
            total = middle[:, cs] + sum(dot(acts[k, j], rws[k, j, :, cs]) for j in range(acts.shape[1]))
            if k + 1 < chunks:
                middle[:, cs] = total
            else:
                out_s[:, cs] = (total + row(vec)[:, cs]).astype(BF)
    move.store(out_s, out_h)
    move.finish()


def layer_end(rights, rws, middle, vec, after=()):
    rows, d = middle.shape
    k = len(rights)
    shards, _, width = rights[0].shape
    scratch = [VM((k, shards, rows, width), BF), VM((k, shards, width, d), BF), VM((rows, d), F32), VM(vec.shape, F32), VM((rows, d), BF)]
    args = (middle, vec, *rights, *rws)
    return call(functools.partial(layer_kernel, k), "layer_end", args, "h" * len(args),
                [("h", S((rows, d), BF))], scratch, 4 + 2 * k, 2 * rows * d * k * shards * width, 12 * MIB, None, after)[0]


def placed(ref, p, code, pieces):
    step = ref.shape[0] // pieces
    return ref[pl.ds(pl.multiple_of(jnp.bitwise_xor(p, code) * step, 16), step), :]


def load_halves(move, m0, m1, t0, t1, cols, both, me):
    half = m0.shape[0]
    return [move.load(m0.at[:, cols], both.at[me, :half]), move.load(m1.at[:, cols], both.at[me, half:]),
            move.load(t0.at[:, cols], both.at[1 - me, :half]), move.load(t1.at[:, cols], both.at[1 - me, half:])]


def finish_ffn_kernel(pieces, k, meta, m0, m1, t0, t1, *refs):
    ghw_h, grw_h, both, whole, wide, tall, sems = refs[-7:]
    move = Mover(sems)
    me, code = meta[0], meta[1]
    d, width = wide.shape
    for c in load_halves(move, m0, m1, t0, t1, slice(0, width), both, me):
        c.wait()
    step = d // pieces
    for p in range(pieces):
        wide[p * step:(p + 1) * step, :] = placed(both.at[0], p, code, pieces).astype(F32)
    move.store(wide, ghw_h.at[:, k * width:(k + 1) * width])
    for p in range(pieces):
        whole[p * step:(p + 1) * step, :] = placed(both.at[1], p, code, pieces)
    for c in range(0, width, 128):
        cs = slice(c, c + 128)
        tall[cs, :] = whole[:, cs].T.astype(F32)
    move.store(tall, grw_h.at[k * width:(k + 1) * width])
    move.finish()


def finish_ffn(meta, pieces, parts, k, shard, before, after=()):
    d, width = 2 * parts[0].shape[0], parts[0].shape[1]
    args = (meta, *parts, *before)
    return call(functools.partial(finish_ffn_kernel, pieces, k), "finish_ffn", args, "shhhh" + "h" * len(before),
                [("h", S((d, shard), F32)), ("h", S((shard, d), F32))],
                [VM((2, d, width), BF), VM((d, width), BF), VM((d, width), F32), VM((width, d), F32)], 8, 0, 4 * MIB,
                {5 + i: i for i in range(len(before))}, after)


def finish_pair_kernel(pieces, meta, m0, m1, t0, t1, *refs):
    outs, (both, wide, sems) = refs[:-3], refs[-3:]
    move = Mover(sems)
    me = meta[0]
    d = wide.shape[1]
    pairs = len(outs) // 2
    loads = [load_halves(move, m0, m1, t0, t1, slice(k * d, (k + 1) * d), both.at[k], me) for k in range(pairs)]
    step = d // pieces
    for k in range(pairs):
        for c in loads[k]:
            c.wait()
        for t in range(2):
            code = jnp.where(me == t, meta[2], meta[3])
            for p in range(pieces):
                wide[2 * k + t, p * step:(p + 1) * step, :] = placed(both.at[k, t], p, code, pieces).astype(F32)
            move.store(wide.at[2 * k + t], outs[2 * k + t])
    move.finish()


def finish_pair(meta, pieces, parts, d, after=()):
    pairs = parts[0].shape[1] // d
    return call(functools.partial(finish_pair_kernel, pieces), "finish_pair", (meta, *parts), "shhhh",
                [("h", S((d, d), F32))] * (2 * pairs), [VM((pairs, 2, d, d), BF), VM((2 * pairs, d, d), F32)], 4 + 6 * pairs, 0, 8 * MIB, None, after)


def bits_below(size):
    return [1 << i for i in range(size.bit_length() - 1)]


class Layout:
    def __init__(self, mesh):
        self.nb, self.nt = mesh.shape["batch"], mesh.shape["tp"]
        self.tp = [("tp", b) for b in reversed(bits_below(self.nt))]
        self.batch = [("batch", b) for b in bits_below(self.nb)[1:]]
        self.lanes = (self.tp + self.batch, self.batch[:1] + self.tp + self.batch[1:])

    def partner(self, device, level):
        b, t = divmod(device, self.nt)
        axis, bit = level
        return (b ^ bit) * self.nt + t if axis == "batch" else b * self.nt + (t ^ bit)

    def swap(self, value, level):
        pairs = []
        for device in range(self.nb * self.nt):
            core, to = device // self.nt % 2, device
            for one in level if isinstance(level, list) else [level]:
                to = self.partner(to, self.lanes[core][one] if isinstance(one, int) else one)
            pairs.append((device, to))
        return lax.ppermute(value, ("batch", "tp"), pairs)


CORE = ("batch", 1)


def code_of(levels, place):
    out = jnp.int32(0)
    for axis, bit in levels:
        out = out * 2 + (place[axis] // bit) % 2
    return out


def add(a, b):
    return (a.astype(F32) + b.astype(F32)).astype(BF)


def scatter_levels(levels, rows, least=48):
    n = 0
    while n < len(levels) and rows % 32 == 0 and rows // 2 >= least:
        rows //= 2
        n += 1
    return n


class Chain:
    def __init__(self, lay, steps):
        self.lay, self.steps, self.result = lay, steps, None
        self.go(next(steps))

    def go(self, requests):
        self.sent = [v for v, _ in requests]
        self.here = [self.lay.swap(v, level) for v, level in requests]

    def step(self):
        try:
            self.go(self.steps.send(self.here))
        except StopIteration as end:
            self.result, self.sent, self.here = end.value, [], []
        return self


def fence(arrays, *chains):
    chains = [c for c in chains if c.here]
    arrays, held = lax.optimization_barrier((arrays, [c.here for c in chains]))
    for chain, here in zip(chains, held):
        chain.here = here
        chain.step()
    return arrays


def sent(*chains):
    return tuple(v for c in chains for v in c.sent)


def halving(a, b, levels):
    for level in levels:
        n = a.shape[0] // 2
        kept = add(a[:n], b[:n])
        (b,) = yield [(add(a[n:], b[n:]), level)]
        a = kept
    return a, b


def quartering(a, b, high, low):
    n = a.shape[0] // 4
    parts = [add(a[i * n:(i + 1) * n], b[i * n:(i + 1) * n]) for i in range(4)]
    got = yield [(parts[1], [low]), (parts[2], [high]), (parts[3], [high, low])]
    return sum((g.astype(F32) for g in got), parts[0].astype(F32)).astype(BF)


def fourfold(held, high, low):
    got = yield [(held, [low]), (held, [high]), (held, [high, low])]
    return jnp.concatenate([held] + got, axis=0)


def doubling(held, levels):
    for level in levels:
        (got,) = yield [(held, level)]
        held = jnp.concatenate([held, got], axis=0)
    return held


def spread(held, level):
    other, mine = yield [(held, level), (held, CORE)]
    (rest,) = yield [(other, CORE)]
    return held, other, mine, rest


def reduce_ffn(lay, gone, stay, keep):
    m = len(lay.lanes[0])
    n = gone.shape[0]
    (recv,) = yield [(gone, CORE)]
    b, recv = yield [(add(keep[n:], recv), 0), (stay, CORE)]
    a, b = yield from halving(add(keep[:n], recv), b, range(1, m - 2))
    held = yield from quartering(a, b, m - 2, m - 1)
    held = yield from doubling(held, reversed(lay.batch[1:]))
    return (yield from spread(held, lay.batch[0]))


def reduce_pair(lay, n, send, keep, ahead):
    (recv,) = yield [(send, CORE)]
    if ahead:
        held = add(*(yield from halving(keep, recv, range(n))))
    else:
        a, b = yield from halving(keep, recv, range(n - 2))
        held = yield from quartering(a, b, n - 2, n - 1)
    for level in range(n, len(lay.lanes[0])):
        (got,) = yield [(held, level)]
        held = add(held, got)
    return held


def gather_pairs(lay, n, held):
    held = yield from fourfold(held, n - 2, n - 1)
    held = yield from doubling(held, reversed(range(1, n - 2)))
    return (yield from spread(held, 0))


def reduce_small(lay, vectors, hidden):
    n, shard = vectors.shape[0], hidden[0].shape[0]
    for level in lay.tp:
        bit = level[1]
        (got,) = yield [(jnp.concatenate([vectors] + [hidden[j + bit] for j in range(bit)]), level)]
        vectors = vectors + got[:n]
        hidden = [hidden[j] + got[n + j * shard:n + (j + 1) * shard] for j in range(bit)]
    held = jnp.concatenate([vectors, hidden[0]])
    for level in [CORE] + lay.batch[:-2]:
        (got,) = yield [(held, level)]
        held = held + got
    high, low = lay.batch[-2:]
    got = yield [(held, [low]), (held, [high]), (held, [high, low])]
    return held + got[0] + got[1] + got[2]


def on_device(
    lay,
    inputs,
    cotangent,
    zinc_lengths,
    pubchem_lengths,
    feature_stack,
    train_step,
    redraw_interval,
    attn_gain,
    attn_shift,
    query_weight,
    query_bias,
    key_weight,
    key_bias,
    value_weight,
    value_bias,
    output_weight,
    output_bias,
    ffn_gain,
    ffn_shift,
    hidden_weight,
    hidden_bias,
    return_weight,
    return_bias,
):
    nt = lay.nt
    d, shard = hidden_weight.shape
    rows = inputs.shape[0]
    width = min(768, shard)
    chunks = shard // width
    zm, pm = zinc_lengths.shape[0], pubchem_lengths.shape[0]
    place = {"batch": lax.axis_index("batch"), "tp": lax.axis_index("tp")}
    core = place["batch"] % 2

    def shares(k):
        hw = lax.dynamic_slice(hidden_weight, (core * (d // 2), k * width), (d // 2, width))
        rw = lax.dynamic_slice(return_weight, (k * width + core * (width // 2), 0), (width // 2, d))
        return [jnp.concatenate([hw, rw], axis=0)] if width == d else [hw, rw]

    def from_tp(own):
        pool = {0: own}
        for level in lay.tp:
            for j in list(pool):
                pool[j | level[1]] = [lay.swap(v, level) for v in pool[j]]
        return [v for j in range(1, nt) for v in pool[j]]

    own = [shares(k) for k in range(chunks)]
    per = len(own[0])
    biases = from_tp([hidden_bias])
    here = {k: from_tp(own[k]) for k in range(chunks)}

    n_pair = scatter_levels(lay.lanes[0], d)
    codes = [code_of(lane[:n_pair], place) for lane in lay.lanes]
    pick = train_step[0] // redraw_interval[0] % feature_stack.shape[0]
    meta = jnp.stack([core, code_of(lay.batch, place), jnp.where(core == 0, codes[0], codes[1]), jnp.where(core == 0, codes[1], codes[0]),
                      code_of(lay.batch[:-2], place) * 4, pick]).astype(jnp.int32)
    table = rotary_const()

    out = attend_fwd(
        meta, zinc_lengths, pubchem_lengths, cotangent, inputs,
        (attn_gain, attn_shift, query_bias, key_bias, value_bias, output_bias, ffn_gain, ffn_shift),
        query_weight, key_weight, value_weight, output_weight, feature_stack, table)
    out, here[0], biases = lax.optimization_barrier((out, here[0], biases))
    qkv, f, state, trans, middle, n2, left, proj = out

    pieces, pair_pieces = 2 ** len(lay.batch), 2 ** n_pair
    chains, acts, rws, hidden, before = [], [], [], [], ()
    for k in range(chunks):
        near = [lay.swap(v, CORE) for v in here[k]]
        if chains:
            near = fence(near, chains[-1])
        parts = [[v[i] for i in range(j * per, (j + 1) * per) for v in (here[k], near)] for j in range(nt - 1)]
        out = ffn_chunk(meta, pieces, nt, n2, left, cotangent, hidden_bias, hidden_weight, return_weight, parts, biases, k, width,
                        before, sent(*chains))
        if k + 1 < chunks:
            out, here[k + 1] = lax.optimization_barrier((out, here[k + 1]))
        gone, stay, keep, act, bias, e, rw = fence(out, *chains)
        before = (e,)
        chains.append(Chain(lay, reduce_ffn(lay, gone, stay, keep)))
        acts.append(act)
        rws.append(rw)
        hidden.append(bias)

    middle = fence(middle, chains[-1])
    out = mid(e, cotangent, middle, output_weight, ffn_gain, sent(*chains))
    gm, gb, gatt, vec1 = fence(out, *chains[:-1])
    out = value_bwd(meta, zm, pm, pair_pieces, gatt, gb, f, state, trans, sent(*chains))
    send, keep, gv, uw, gst, vec2 = fence(out, *chains)
    pair_a = Chain(lay, reduce_pair(lay, n_pair, send, keep, True))
    uw = fence(uw, pair_a)
    out = query_bwd(meta, zm, pm, pair_pieces, uw, gst, qkv, f, state, trans, proj, table, sent(pair_a, *chains))
    send, keep, gqk, vec3 = fence(out, pair_a, *chains)
    pair_b = Chain(lay, reduce_pair(lay, n_pair, send, keep, False))
    gqk = fence(gqk, pair_b)
    out = input_back(gqk, gv, query_weight, key_weight, value_weight, inputs, gm, attn_gain, sent(pair_a, pair_b, *chains))
    (input_grad, vec4), middle = fence((out, middle), pair_a, pair_b, *chains)
    layer_out = layer_end(acts, rws, middle, return_bias, sent(pair_b, pair_a, *chains))
    layer_out, vec4 = fence((layer_out, vec4), pair_b, pair_a, *chains)
    vec3 = jnp.concatenate([vec3, vec4], axis=0)
    vectors = jnp.concatenate([vec1, vec2, vec3], axis=0).reshape(-1)
    small = Chain(lay, reduce_small(lay, vectors, [jnp.concatenate([hidden[k][j] for k in range(chunks)]) for j in range(nt)]))

    ffn_out, k, pairs = (), 0, None
    while pairs is None or pairs.here or any(c.here for c in chains):
        every = [pairs] if pairs else [pair_b, pair_a]
        every += chains + [small]
        if k < chunks and chains[k].result is not None:
            ffn_out = finish_ffn(meta, pieces, chains[k].result, k, shard, ffn_out, sent(*every))
            k += 1
            ffn_out = fence(ffn_out, *every)
        else:
            fence((), *every)
        if pairs is None and pair_a.result is not None and pair_b.result is not None:
            pairs = Chain(lay, gather_pairs(lay, n_pair, jnp.concatenate([pair_a.result, pair_b.result], axis=1)))
    while k < chunks:
        ffn_out = finish_ffn(meta, pieces, chains[k].result, k, shard, ffn_out, sent(small))
        k += 1
    while small.here:
        small.step()
    gwo, gwv, gwq, gwk = finish_pair(meta, pair_pieces, pairs.result, d, (small.result,))
    vecs = small.result[:9 * d].reshape(9, d)
    return (layer_out, input_grad, vecs[7], vecs[8], gwq, vecs[5], gwk, vecs[6], gwv, vecs[4], gwo, vecs[2],
            vecs[0], vecs[1], ffn_out[0], small.result[9 * d:], ffn_out[1], vecs[3])


def solution(mesh):
    rows, whole, hidden = P(("batch", "tp"), None), P(), P(None, "tp")
    return jax.shard_map(
        functools.partial(on_device, Layout(mesh)),
        mesh=mesh,
        in_specs=(rows, rows, P(("batch", "tp")), P(("batch", "tp"))) + (whole,) * 15 + (hidden, P("tp"), P("tp", None), whole),
        out_specs=(rows, rows) + (whole,) * 12 + (hidden, P("tp"), P("tp", None), whole),
        check_vma=False,
    )
```

```python
import functools
import math

import jax
import jax.numpy as jnp
import numpy as np
from jax import lax
from jax.experimental import pallas as pl
from jax.experimental.pallas import tpu as pltpu
from jax.sharding import PartitionSpec as P

ZPAD = 64
PPAD = 256
F32 = jnp.float32
BF = jnp.bfloat16
VM = pltpu.VMEM
GROUP = 4
S = jax.ShapeDtypeStruct
TIMES = {"attend_fwd": 24, "ffn_chunk": 17, "layer_end": 9, "mid": 8, "value_bwd": 13, "query_bwd": 13, "input_back": 10, "finish_ffn": 5, "finish_pair": 5}
MIB = 2**20
GRANT = 60


def dot(a, b):
    return jnp.dot(a, b, preferred_element_type=F32)


def dot_t(a, b):
    return lax.dot_general(a, b, (((1,), (1,)), ((), ())), preferred_element_type=F32)


def dot_c(a, b):
    return lax.dot_general(a, b, (((0,), (0,)), ((), ())), preferred_element_type=F32)


def split(v):
    hi = v.astype(BF)
    return hi, (v - hi.astype(F32)).astype(BF)


def norm_parts(values):
    center = values - jnp.mean(values, axis=-1, keepdims=True)
    rate = lax.rsqrt(jnp.mean(center * center, axis=-1, keepdims=True) + 1e-05)
    return center * rate, rate


def row(ref):
    return ref[...].reshape(1, -1)


def block_mask(width):
    f = lax.broadcasted_iota(jnp.int32, (128, width), 0) // 32
    c = lax.broadcasted_iota(jnp.int32, (128, width), 1) % 256 // 64
    return f == c


def molecules(zm, pm):
    return [(i * ZPAD, ZPAD) for i in range(zm)] + [(zm * ZPAD + i * PPAD, PPAD) for i in range(pm)]


def members(mols, b):
    return [(i, r, n) for i, (r, n) in enumerate(mols) if b * PPAD <= r < (b + 1) * PPAD]


class Mover:
    def __init__(self, sems):
        self.sems, self.n, self.out = sems, 0, []

    def load(self, src, dst):
        copy = pltpu.make_async_copy(src, dst, self.sems.at[self.n])
        self.n += 1
        copy.start()
        return copy

    def store(self, src, dst):
        self.out.append(self.load(src, dst))

    def finish(self):
        for copy in self.out:
            copy.wait()


def call(kernel, name, args, spaces, outs, scratch, copies, flops, moved, aliases=None, after=()):
    n, extra = len(args), len(after)

    def body(*refs):
        kernel(*refs[:n], *refs[n + extra:])

    spec = {
        "v": pl.BlockSpec(memory_space=VM),
        "h": pl.BlockSpec(memory_space=pltpu.HBM),
        "s": pl.BlockSpec(memory_space=pltpu.SMEM),
    }
    return pl.pallas_call(
        body,
        out_shape=tuple(o for _, o in outs),
        in_specs=[spec[s] for s in spaces] + [spec["h"]] * extra,
        out_specs=tuple(spec[s] for s, _ in outs),
        scratch_shapes=list(scratch) + [pltpu.SemaphoreType.DMA((copies,))],
        input_output_aliases=aliases or {},
        compiler_params=pltpu.CompilerParams(vmem_limit_bytes=GRANT * MIB),
        cost_estimate=pl.CostEstimate(flops=int(TIMES[name] * 1.15e9), bytes_accessed=moved, transcendentals=0),
        name=name,
    )(*args, *after)


def place_heads(scaled):
    two = jnp.concatenate([scaled, scaled], axis=1)
    return jnp.where(block_mask(256), jnp.concatenate([two, two], axis=1), 0.0)


def attend_fwd_kernel(zm, pm, meta, zlen, plen, cot_h, x_h, gain_h, shift_h, bq_h, bk_h, bv_h, bo_h, gain2_h, shift2_h,
                      wq_h, wk_h, wv_h, wo_h, stack_h, table_h, energy_h,
                      qkv_h, f_h, state_h, trans_h, middle_h, n2_h, left_h, proj_h,
                      cot, n2_s, left, x, vec, wq, wk, wv, wo, fp, proj, table, energy, qkv, f_s, state_s, trans, middle_s, att_s, sems):
    move = Mover(sems)
    rows, d = x.shape
    first = [move.load(x_h, x), move.load(gain_h, vec.at[0]), move.load(shift_h, vec.at[1]), move.load(stack_h.at[meta[5]], fp),
             move.load(cot_h, cot)]
    later = [move.load(s, t) for s, t in ((wq_h, wq), (bq_h, vec.at[2]), (table_h, table), (energy_h, energy), (wk_h, wk),
                                          (bk_h, vec.at[3]), (wv_h, wv), (bv_h, vec.at[4]))]
    last = [move.load(s, t) for s, t in ((wo_h, wo), (bo_h, vec.at[5]), (gain2_h, vec.at[6]), (shift2_h, vec.at[7]))]
    mols = molecules(zm, pm)
    groups = d // 256
    blocks = range(rows // PPAD)
    keep = block_mask(512)
    ones = jnp.ones((PPAD, 256), BF)

    def vector(i):
        return vec[i].reshape(1, -1)

    for c in first:
        c.wait()
    for g in range(groups):
        p = fp[g * GROUP:(g + 1) * GROUP].reshape(GROUP * 32, 64) * 64 ** -0.25
        turned = jnp.concatenate([p[:, 32:], -p[:, :32]], axis=1)
        hi, lo = split(jnp.concatenate([place_heads(p), place_heads(turned)], axis=1))
        proj[0, g] = hi
        proj[1, g] = lo
    n1s = {}
    for b in blocks:
        rs = slice(b * PPAD, (b + 1) * PPAD)
        normed, _ = norm_parts(x[rs, :].astype(F32))
        n1s[b] = (normed * vector(0) + vector(1)).astype(BF)
        trans[1, :, rs] = n1s[b].T
        left[1, :, rs] = cot[rs, :].T
    for c in later:
        c.wait()
    move.store(proj.at[0], proj_h)
    move.store(trans.at[1], trans_h.at[1])
    move.store(left.at[1], left_h.at[1])
    for b in blocks:
        mem = members(mols, b)
        rs = slice(b * PPAD, (b + 1) * PPAD)
        n1 = n1s[b]
        cosb, sinb = (jnp.concatenate([table[t, :n, :] for _, _, n in mem], axis=0) for t in range(2))
        cosb = jnp.concatenate([cosb, cosb], axis=1)
        sinb = jnp.concatenate([sinb, sinb], axis=1)
        live = jnp.concatenate(
            [(lax.broadcasted_iota(jnp.int32, (n, 128), 0) < (zlen[i] if i < zm else plen[i - zm])).astype(F32) for i, r, n in mem], axis=0)
        for g in range(groups):
            cs = slice(g * 256, (g + 1) * 256)
            fs = slice(g * 128, (g + 1) * 128)

            def features(w, bias, slot):
                v = dot(n1, w[:, cs]) + vector(bias)[:, cs]
                qkv[slot, rs, cs] = v.astype(BF)
                ch, cl = split(v * cosb)
                sh, sl = split(v * sinb)
                eh, el = split(v * v)
                ph, plo = proj[0, g], proj[1, g]
                e = energy[...]
                inner = (dot_t(ch, ph[:, :256]) + dot_t(sh, ph[:, 256:]) + dot_t(cl, ph[:, :256]) + dot_t(sl, ph[:, 256:])
                         + dot_t(ch, plo[:, :256]) + dot_t(sh, plo[:, 256:]) - dot_t(eh, e) - dot_t(el, e))
                return jnp.exp(inner) * (32 ** -0.5)

            fq = features(wq, 2, 0).astype(BF)
            fk = (features(wk, 3, 1) * live).astype(BF)
            f_s[0, rs, fs] = fq
            f_s[1, rs, fs] = fk
            v = (dot(n1, wv[:, cs]) + vector(4)[:, cs]).astype(BF)
            qkv[2, rs, cs] = v
            for i, r, n in mem:
                ms = slice(r - b * PPAD, r - b * PPAD + n)
                vo = jnp.concatenate([v[ms], ones[:n]], axis=1)
                state = jnp.where(keep, dot_c(fk[ms], vo), 0.0).astype(BF)
                state_s[i, g] = state
                nd = dot(fq[ms], state)
                att_s[r:r + n, cs] = (nd[:, :256] / nd[:, 256:]).astype(BF)
    for s, t in ((qkv, qkv_h), (f_s, f_h), (state_s, state_h)):
        move.store(s, t)
    for c in last:
        c.wait()
    for b in blocks:
        rs = slice(b * PPAD, (b + 1) * PPAD)
        trans[0, :, rs] = att_s[rs, :].T
        middle = x[rs, :].astype(F32) + (dot(att_s[rs, :], wo[...]) + vector(5))
        middle_s[rs, :] = middle
        normed, _ = norm_parts(middle)
        n2 = (normed * vector(6) + vector(7)).astype(BF)
        n2_s[rs, :] = n2
        left[0, :, rs] = n2.T
    move.store(middle_s, middle_h)
    move.store(n2_s, n2_h)
    move.store(trans.at[0], trans_h.at[0])
    move.store(left.at[0], left_h.at[0])
    move.finish()


def rotary_const():
    place = np.arange(PPAD, dtype=np.float64)
    rates = np.exp(np.arange(32, dtype=np.float64) * (-2.0 * math.log(10000.0) / 64))
    ang = place[:, None] * rates[None, :]
    return np.tile(np.stack([np.cos(ang), np.sin(ang)]), (1, 1, 4)).astype(np.float32)


def head_const(scale):
    f = np.arange(128)[:, None] // 32
    c = np.arange(256)[None, :] // 64
    return ((f == c) * scale).astype(jnp.bfloat16)


def attend_fwd(meta, zlen, plen, cot, x, vectors, wq, wk, wv, wo, stack, table):
    rows, d = x.shape
    zm, pm = zlen.shape[0], plen.shape[0]
    groups = d // 256
    states = (zm + pm, groups, 128, 512)
    outs = [S((3, rows, d), BF), S((2, rows, d // 2), BF), S(states, BF), S((2, d, rows), BF),
            S((rows, d), F32), S((rows, d), BF), S((2, d, rows), BF), S((groups, 128, 512), BF)]
    args = (meta, zlen, plen, cot, x, *vectors, wq, wk, wv, wo, stack, table, head_const(1 / 16))
    scratch = ([VM((rows, d), BF)] * 2 + [VM((2, d, rows), BF), VM((rows, d), BF), VM((8, d), F32)] + [VM((d, d), BF)] * 4
               + [VM(stack.shape[1:], F32), VM((2, groups, 128, 512), BF), VM(table.shape, F32), VM((128, 256), BF)]
               + [VM((3, rows, d), BF), VM((2, rows, d // 2), BF), VM(states, BF), VM((2, d, rows), BF), VM((rows, d), F32), VM((rows, d), BF)])
    return call(
        functools.partial(attend_fwd_kernel, zm, pm), "attend_fwd", args, "sss" + "h" * (len(args) - 3),
        [("h", o) for o in outs], scratch, 32, 2 * rows * d * d * 4, 16 * MIB)


def gelu_parts(h):
    bell = jnp.exp(h * h * -0.5)
    t = 1.0 / (1.0 + (0.3275911 * math.sqrt(0.5)) * jnp.abs(h))
    poly = t * (0.127414796 + t * (-0.142248368 + t * (0.7107068705 + t * (-0.7265760135 + t * 0.5307027145))))
    tail = poly * bell
    phi = jnp.where(h >= 0, 1.0 - tail, tail)
    return h * phi, phi + h * bell * (1.0 / math.sqrt(2 * math.pi))


def place_pieces(code, src, dst):
    n, step = src.shape[0], src.shape[1]
    for p in range(n):
        off = pl.multiple_of(jnp.bitwise_xor(p, code) * step, 16)
        dst[pl.ds(off, step), :] = src[p]


def ffn_kernel(pieces, shards, k, per, meta, n2_h, left_h, cot_h, hb_h, hw_h, rw_h, *refs):
    parts = {j: refs[(j - 1) * per:j * per] for j in range(1, shards)}
    hbs = refs[(shards - 1) * per:(shards - 1) * (per + 1)]
    e_prev = refs[(shards - 1) * (per + 1)] if k else None
    (gone_h, stay_h, keep_h, act_h, bias_o, e_h, rws_h, n2, left, cot, hb, hw, rw, hw2, rw2, right, stage, e_s, sems) = refs[-19:]
    move = Mover(sems)
    d, width = hw.shape[1:]
    half_d = d // 2
    me, code = meta[0], meta[1]
    order = list(range(1, shards)) + [0]
    early, late = {}, {}
    for j in order:
        early[j] = [move.load(hbs[j - 1] if j else hb_h, hb.at[j])]
        if j == order[0]:
            early[j].append(move.load(n2_h, n2))
        late[j] = []
        if j == 0:
            early[j].append(move.load(hw_h.at[:, k * width:(k + 1) * width], hw.at[0]))
            late[j].append(move.load(rw_h.at[k * width:(k + 1) * width, :], rw.at[0]))
        elif per == 2:
            early[j] += [move.load(parts[j][p].at[:half_d], hw2.at[j - 1, p]) for p in range(2)]
            late[j] += [move.load(parts[j][p].at[half_d:], rw2.at[j - 1, p]) for p in range(2)]
        else:
            early[j] += [move.load(parts[j][p], hw2.at[j - 1, p]) for p in range(2)]
            late[j] += [move.load(parts[j][2 + p], rw2.at[j - 1, p]) for p in range(2)]
        if j == order[0]:
            late[j].append(move.load(cot_h, cot))
    last = [move.load(left_h, left)]
    if k:
        last.append(move.load(e_prev, e_s))
    step, half = d // pieces, pieces // 2
    tile = width
    for j in order:
        for c in early[j] + late[j]:
            c.wait()
        if j:
            place_pieces(me, hw2.at[j - 1], hw.at[j])
            place_pieces(me, rw2.at[j - 1], rw.at[j])
        bias = hb[j].reshape(1, -1)[:, k * width:(k + 1) * width].astype(F32)
        for c in range(0, width, tile):
            cs = slice(c, c + tile)
            h = dot(n2[...], hw[j, :, cs]) + bias[:, cs]
            act, slope = gelu_parts(h)
            ga = dot_t(cot[...], rw[j, cs, :])
            gh = (ga * slope).astype(BF)
            right[0, j, :, cs] = gh
            right[1, j, :, cs] = act.astype(BF)
            bias_o[j:j + 1, cs] = jnp.sum(gh.astype(F32), axis=0, keepdims=True)
        move.store(right.at[1, j], act_h.at[j])
        move.store(rw.at[j], rws_h.at[j])
    for c in last:
        c.wait()
    for c in range(0, d, 768):
        cs = slice(c, c + 768)
        part = sum(dot_t(right[0, j], hw[j, cs, :]) for j in order)
        e_s[:, cs] = e_s[:, cs] + part if k else part
    move.store(e_s, e_h)
    for kind, slot in ((1 - me, 0), (me, 1)):
        for j in order:
            for c in range(0, width, tile):
                cs = slice(c, c + tile)
                value = dot(left[kind], right[kind, j, :, cs]).astype(BF)
                for p in range(pieces):
                    rel = jnp.bitwise_xor(p, code)
                    second = rel // half * (shards * half) + j * half + rel % half
                    off = pl.multiple_of(jnp.where(kind == 0, j * pieces + rel, second) * step, 16)
                    stage[slot, pl.ds(off, step), cs] = value[p * step:(p + 1) * step]
        if slot:
            move.store(stage.at[1], keep_h)
        else:
            cut = shards * d // 2
            move.store(stage.at[0, cut:], gone_h)
            move.store(stage.at[0, :cut], stay_h)
    move.finish()


def ffn_chunk(meta, pieces, shards, n2, left, cot, hb, hw, rw, parts, hbs, k, width, before, after=()):
    rows, d = n2.shape
    per = len(parts[0])
    part = S((shards * d // 2, width), BF)
    outs = [("h", part), ("h", part), ("h", S((shards * d, width), BF)), ("h", S((shards, rows, width), BF)), ("v", S((shards, width), F32)),
            ("h", S((rows, d), F32)), ("h", S((shards, width, d), BF))]
    scratch = [VM((rows, d), BF), VM((2, d, rows), BF), VM((rows, d), BF), VM((shards, 1) + hb.shape, BF), VM((shards, d, width), BF),
               VM((shards, width, d), BF), VM((shards - 1, 2, d // 2, width), BF), VM((shards - 1, 2, width // 2, d), BF),
               VM((2, shards, rows, width), BF), VM((2, shards * d, width), BF), VM((rows, d), F32)]
    args = (meta, n2, left, cot, hb.reshape(1, -1), hw, rw) + tuple(p for part in parts for p in part) + tuple(b.reshape(1, -1) for b in hbs) + tuple(before)
    return call(
        functools.partial(ffn_kernel, pieces, shards, k, per), "ffn_chunk", args,
        "s" + "h" * (len(args) - 1), outs, scratch, 12 + 13 * shards, 2 * rows * d * width * 5 * shards, 12 * MIB, None, after)


def products(move, pieces, codes, stage, outs):
    for slot, (left, right, out) in enumerate(outs):
        d = out.shape[0]
        step = d // pieces
        for c in range(0, d, 768):
            cs = slice(c, c + 768)
            value = dot(left[...], right[:, cs]).astype(BF)
            for p in range(pieces):
                off = pl.multiple_of(jnp.bitwise_xor(p, codes[slot]) * step, 16)
                stage[slot, pl.ds(off, step), cs] = value[p * step:(p + 1) * step]
        move.store(stage.at[slot], out)


def mid_kernel(e_h, cot_h, middle_h, wo_h, vec_h, gm_h, gb_h, gatt_h, vec_o, e_s, cot, middle, wo, vec, gm_s, gb_s, gatt, sems):
    move = Mover(sems)
    rows, d = middle.shape
    loads = [[move.load(s.at[r:r + 256], t.at[r:r + 256]) for s, t in ((middle_h, middle), (e_h, e_s), (cot_h, cot))]
             for r in range(0, rows, 256)]
    gain = move.load(vec_h, vec)
    last = move.load(wo_h, wo)
    gain.wait()
    gain2 = row(vec)
    acc_g = acc_s = acc_b = acc_c = 0.0
    for i, r in enumerate(range(0, rows, 256)):
        for c in loads[i]:
            c.wait()
        rs = slice(r, r + 256)
        e = e_s[rs, :]
        n, rate = norm_parts(middle[rs, :])
        c = cot[rs, :].astype(F32)
        acc_g += jnp.sum(e * n, axis=0, keepdims=True)
        acc_s += jnp.sum(e, axis=0, keepdims=True)
        acc_c += jnp.sum(c, axis=0, keepdims=True)
        eg = e * gain2
        gm = c + rate * (eg - jnp.mean(eg, axis=-1, keepdims=True) - n * jnp.mean(eg * n, axis=-1, keepdims=True))
        gm_s[rs, :] = gm
        gb = gm.astype(BF)
        gb_s[rs, :] = gb
        acc_b += jnp.sum(gb.astype(F32), axis=0, keepdims=True)
    for i, acc in enumerate((acc_g, acc_s, acc_b, acc_c)):
        vec_o[i:i + 1, :] = acc
    move.store(gm_s, gm_h)
    move.store(gb_s, gb_h)
    last.wait()
    for c in range(0, d, 768):
        cs = slice(c, c + 768)
        gatt[:, cs] = dot_t(gb_s[...], wo[cs, :]).astype(BF)
    move.store(gatt, gatt_h)
    move.finish()


def mid(e, cot, middle, wo, gain2, after=()):
    rows, d = middle.shape
    outs = [("h", S((rows, d), F32)), ("h", S((rows, d), BF)), ("h", S((rows, d), BF)), ("v", S((4, d), F32))]
    scratch = [VM((rows, d), F32), VM((rows, d), BF), VM((rows, d), F32), VM((d, d), BF), VM(gain2.shape, F32), VM((rows, d), F32),
               VM((rows, d), BF), VM((rows, d), BF)]
    args = (e, cot, middle, wo, gain2)
    return call(mid_kernel, "mid", args, "h" * len(args), outs, scratch, 8 + 3 * (rows // 256), 2 * rows * d * d, 8 * MIB, None, after)


def value_bwd_kernel(zm, pm, pieces, meta, gatt_h, gb_h, f_h, state_h, trans_h,
                     send_h, keep_h, gv_h, uw_h, gst_h, vec_o, gatt, uw_o, gst_o, f, state, left, right, stage, sems):
    move = Mover(sems)
    mols = molecules(zm, pm)
    rows, d = gatt.shape
    groups = d // 256
    loads = []
    for g in range(groups):
        cs, fs = slice(g * 256, (g + 1) * 256), slice(g * 128, (g + 1) * 128)
        loads.append([move.load(f_h.at[:, :, fs], f.at[:, :, fs]), move.load(state_h.at[:, g], state.at[:, g]),
                      move.load(gatt_h.at[:, cs], gatt.at[:, cs])])
    last = [move.load(trans_h, left), move.load(gb_h, right.at[0])]
    keep = block_mask(512)
    for g in range(groups):
        for c in loads[g]:
            c.wait()
        cs = slice(g * 256, (g + 1) * 256)
        fs = slice(g * 128, (g + 1) * 128)
        total = 0.0
        for i, (r, n) in enumerate(mols):
            ms = slice(r, r + n)
            st = state[i, g]
            q = f[0, ms, fs]
            nd = dot(q, st)
            rden = 1.0 / nd[:, 256:]
            u = gatt[ms, cs].astype(F32) * rden
            uw = jnp.concatenate([u, -(u * (nd[:, :256] * rden))], axis=1).astype(BF)
            uw_o[ms, slice(g * 512, (g + 1) * 512)] = uw
            gst = jnp.where(keep, dot_c(q, uw), 0.0).astype(BF)
            gst_o[i, g] = gst
            gv = dot(f[1, ms, fs], gst[:, :256]).astype(BF)
            right[1, ms, cs] = gv
            total += jnp.sum(gv.astype(F32), axis=0, keepdims=True)
        vec_o[0:1, cs] = total
    move.store(right.at[1], gv_h)
    move.store(uw_o, uw_h)
    move.store(gst_o, gst_h)
    for c in last:
        c.wait()
    me = meta[0]
    products(move, pieces, (meta[3], meta[2]), stage, ((left.at[1 - me], right.at[1 - me], send_h), (left.at[me], right.at[me], keep_h)))
    move.finish()


def value_bwd(meta, zm, pm, pieces, gatt, gb, f, state, trans, after=()):
    rows, d = gatt.shape
    outs = [("h", S((d, d), BF))] * 2 + [("h", S((rows, d), BF)), ("h", S((rows, 2 * d), BF)), ("h", S(state.shape, BF)), ("v", S((1, d), F32))]
    scratch = [VM((rows, d), BF), VM((rows, 2 * d), BF), VM(state.shape, BF), VM(f.shape, BF), VM(state.shape, BF), VM((2, d, rows), BF),
               VM((2, rows, d), BF), VM((2, d, d), BF)]
    args = (meta, gatt, gb, f, state, trans)
    return call(functools.partial(value_bwd_kernel, zm, pm, pieces), "value_bwd", args, "shhhhh", outs, scratch,
                10 + 3 * d // 256, 2 * d**3 * 3, 8 * MIB, None, after)


def query_bwd_kernel(zm, pm, pieces, meta, uw_h, gst_h, qkv_h, f_h, state_h, trans_h, proj_h, energy_h, table_h,
                     send_h, keep_h, gqk_h, vec_o, uw, gst, qkv, f, state, n1t, proj, energy, table, gqk, stage, sems):
    move = Mover(sems)
    mols = molecules(zm, pm)
    _, rows, d = qkv.shape
    loads = [[move.load(s, t) for s, t in ((proj_h, proj), (energy_h, energy), (table_h, table))]]
    for g in range(d // 256):
        cs, fs, us = slice(g * 256, (g + 1) * 256), slice(g * 128, (g + 1) * 128), slice(g * 512, (g + 1) * 512)
        if g:
            loads.append([])
        loads[g] += [move.load(uw_h.at[:, us], uw.at[:, us]), move.load(state_h.at[:, g], state.at[:, g]),
                     move.load(f_h.at[:, :, fs], f.at[:, :, fs]), move.load(gst_h.at[:, g], gst.at[:, g]),
                     move.load(qkv_h.at[:, :, cs], qkv.at[:, :, cs])]
    later = [move.load(trans_h.at[1], n1t)]
    for g in range(d // 256):
        for c in loads[g]:
            c.wait()
        cs = slice(g * 256, (g + 1) * 256)
        fs = slice(g * 128, (g + 1) * 128)
        sums = [0.0, 0.0]
        for b in range(rows // PPAD):
            mem = members(mols, b)
            rs = slice(b * PPAD, (b + 1) * PPAD)
            gfq, gfk = [], []
            for i, r, n in mem:
                ms = slice(r, r + n)
                gfq.append(dot_t(uw[ms, slice(g * 512, (g + 1) * 512)], state[i, g]))
                gfk.append(dot_t(jnp.concatenate([qkv[2, ms, cs], jnp.ones((n, 256), BF)], axis=1), gst[i, g]))
            cosb, sinb = (jnp.concatenate([table[t, :n, :] for _, _, n in mem], axis=0) for t in range(2))
            cosb = jnp.concatenate([cosb, cosb], axis=1)
            sinb = jnp.concatenate([sinb, sinb], axis=1)
            for t, gf in enumerate((gfq, gfk)):
                gp = (jnp.concatenate(gf, axis=0) * f[t, rs, fs].astype(F32)).astype(BF)
                back = dot(gp, proj[g])
                tot = dot(gp, energy[...])
                grad = (cosb * back[:, :256] + sinb * back[:, 256:] - tot * qkv[t, rs, cs].astype(F32)).astype(BF)
                gqk[t, rs, cs] = grad
                sums[t] += jnp.sum(grad.astype(F32), axis=0, keepdims=True)
        for t in range(2):
            vec_o[t:t + 1, cs] = sums[t]
    for c in later:
        c.wait()
    me = meta[0]
    products(move, pieces, (meta[3], meta[2]), stage, ((n1t, gqk.at[1 - me], send_h), (n1t, gqk.at[me], keep_h)))
    move.store(gqk, gqk_h)
    move.finish()


def query_bwd(meta, zm, pm, pieces, uw, gst, qkv, f, state, trans, proj, table, after=()):
    _, rows, d = qkv.shape
    outs = [("h", S((d, d), BF))] * 2 + [("h", S((2, rows, d), BF)), ("v", S((2, d), F32))]
    scratch = [VM(uw.shape, BF), VM(gst.shape, BF), VM(qkv.shape, BF), VM(f.shape, BF), VM(state.shape, BF), VM((d, rows), BF),
               VM(proj.shape, BF), VM((128, 256), BF), VM(table.shape, F32), VM((2, rows, d), BF), VM((2, d, d), BF)]
    args = (meta, uw, gst, qkv, f, state, trans, proj, head_const(64 ** -0.5), table)
    return call(functools.partial(query_bwd_kernel, zm, pm, pieces), "query_bwd", args, "s" + "h" * (len(args) - 1), outs, scratch,
                8 + 5 * d // 256, 2 * d**3 * 6, 12 * MIB, None, after)


def input_kernel(gqk_h, gv_h, wq_h, wk_h, wv_h, x_h, gm_h, gain_h, out_h, vec_o, gqk, gv, wq, wk, wv, x, gm, vec, e_s, out_s, sems):
    move = Mover(sems)
    rows, d = x.shape
    loads = [(move.load(gqk_h.at[0], gqk.at[0]), move.load(wq_h, wq)), (move.load(gqk_h.at[1], gqk.at[1]), move.load(wk_h, wk)),
             (move.load(gv_h, gv), move.load(wv_h, wv))]
    last = [move.load(s, t) for s, t in ((x_h, x), (gm_h, gm), (gain_h, vec))]
    for (left, right), load in zip(((gqk.at[0], wq), (gqk.at[1], wk), (gv, wv)), loads):
        for c in load:
            c.wait()
        for c in range(0, d, 768):
            cs = slice(c, c + 768)
            part = dot_t(left[...], right[cs, :])
            e_s[:, cs] = part if right is wq else e_s[:, cs] + part
    for c in last:
        c.wait()
    gain = row(vec)
    acc_g = acc_s = 0.0
    for r in range(0, rows, 256):
        rs = slice(r, r + 256)
        e = e_s[rs, :]
        n, rate = norm_parts(x[rs, :].astype(F32))
        acc_g += jnp.sum(e * n, axis=0, keepdims=True)
        acc_s += jnp.sum(e, axis=0, keepdims=True)
        eg = e * gain
        gx = rate * (eg - jnp.mean(eg, axis=-1, keepdims=True) - n * jnp.mean(eg * n, axis=-1, keepdims=True))
        out_s[rs, :] = (gm[rs, :] + gx).astype(BF)
    move.store(out_s, out_h)
    vec_o[0:1, :] = acc_g
    vec_o[1:2, :] = acc_s
    move.finish()


def input_back(gqk, gv, wq, wk, wv, x, gm, gain, after=()):
    rows, d = x.shape
    scratch = [VM(gqk.shape, BF), VM(gv.shape, BF)] + [VM((d, d), BF)] * 3 + [
        VM((rows, d), BF), VM((rows, d), F32), VM(gain.shape, F32), VM((rows, d), F32), VM((rows, d), BF)]
    args = (gqk, gv, wq, wk, wv, x, gm, gain)
    return call(input_kernel, "input_back", args, "h" * len(args), [("h", S((rows, d), BF)), ("v", S((2, d), F32))], scratch,
                16, 2 * d**3 * 3, 8 * MIB, None, after)


def layer_kernel(chunks, middle_h, vec_h, *refs):
    rights_h, rws_h = refs[:chunks], refs[chunks:2 * chunks]
    out_h, acts, rws, middle, vec, out_s, sems = refs[2 * chunks:]
    move = Mover(sems)
    base = [move.load(middle_h, middle), move.load(vec_h, vec)]
    loads = [[move.load(rights_h[k], acts.at[k]), move.load(rws_h[k], rws.at[k])] for k in range(chunks)]
    d = middle.shape[1]
    for c in base:
        c.wait()
    for k, load in enumerate(loads):
        for c in load:
            c.wait()
        for c in range(0, d, 768):
            cs = slice(c, c + 768)
            total = middle[:, cs] + sum(dot(acts[k, j], rws[k, j, :, cs]) for j in range(acts.shape[1]))
            if k + 1 < chunks:
                middle[:, cs] = total
            else:
                out_s[:, cs] = (total + row(vec)[:, cs]).astype(BF)
    move.store(out_s, out_h)
    move.finish()


def layer_end(rights, rws, middle, vec, after=()):
    rows, d = middle.shape
    k = len(rights)
    shards, _, width = rights[0].shape
    scratch = [VM((k, shards, rows, width), BF), VM((k, shards, width, d), BF), VM((rows, d), F32), VM(vec.shape, F32), VM((rows, d), BF)]
    args = (middle, vec, *rights, *rws)
    return call(functools.partial(layer_kernel, k), "layer_end", args, "h" * len(args),
                [("h", S((rows, d), BF))], scratch, 4 + 2 * k, 2 * rows * d * k * shards * width, 12 * MIB, None, after)[0]


def placed(ref, p, code, pieces):
    step = ref.shape[0] // pieces
    return ref[pl.ds(pl.multiple_of(jnp.bitwise_xor(p, code) * step, 16), step), :]


def load_halves(move, m0, m1, t0, t1, cols, both, me):
    half = m0.shape[0]
    return [move.load(m0.at[:, cols], both.at[me, :half]), move.load(m1.at[:, cols], both.at[me, half:]),
            move.load(t0.at[:, cols], both.at[1 - me, :half]), move.load(t1.at[:, cols], both.at[1 - me, half:])]


def finish_ffn_kernel(pieces, k, meta, m0, m1, t0, t1, *refs):
    ghw_h, grw_h, both, whole, wide, tall, sems = refs[-7:]
    move = Mover(sems)
    me, code = meta[0], meta[1]
    d, width = wide.shape
    for c in load_halves(move, m0, m1, t0, t1, slice(0, width), both, me):
        c.wait()
    step = d // pieces
    for p in range(pieces):
        wide[p * step:(p + 1) * step, :] = placed(both.at[0], p, code, pieces).astype(F32)
    move.store(wide, ghw_h.at[:, k * width:(k + 1) * width])
    for p in range(pieces):
        whole[p * step:(p + 1) * step, :] = placed(both.at[1], p, code, pieces)
    for c in range(0, width, 128):
        cs = slice(c, c + 128)
        tall[cs, :] = whole[:, cs].T.astype(F32)
    move.store(tall, grw_h.at[k * width:(k + 1) * width])
    move.finish()


def finish_ffn(meta, pieces, parts, k, shard, before, after=()):
    d, width = 2 * parts[0].shape[0], parts[0].shape[1]
    args = (meta, *parts, *before)
    return call(functools.partial(finish_ffn_kernel, pieces, k), "finish_ffn", args, "shhhh" + "h" * len(before),
                [("h", S((d, shard), F32)), ("h", S((shard, d), F32))],
                [VM((2, d, width), BF), VM((d, width), BF), VM((d, width), F32), VM((width, d), F32)], 8, 0, 4 * MIB,
                {5 + i: i for i in range(len(before))}, after)


def finish_pair_kernel(pieces, meta, m0, m1, t0, t1, *refs):
    outs, (both, wide, sems) = refs[:-3], refs[-3:]
    move = Mover(sems)
    me = meta[0]
    d = wide.shape[1]
    pairs = len(outs) // 2
    loads = [load_halves(move, m0, m1, t0, t1, slice(k * d, (k + 1) * d), both.at[k], me) for k in range(pairs)]
    step = d // pieces
    for k in range(pairs):
        for c in loads[k]:
            c.wait()
        for t in range(2):
            code = jnp.where(me == t, meta[2], meta[3])
            for p in range(pieces):
                wide[2 * k + t, p * step:(p + 1) * step, :] = placed(both.at[k, t], p, code, pieces).astype(F32)
            move.store(wide.at[2 * k + t], outs[2 * k + t])
    move.finish()


def finish_pair(meta, pieces, parts, d, after=()):
    pairs = parts[0].shape[1] // d
    return call(functools.partial(finish_pair_kernel, pieces), "finish_pair", (meta, *parts), "shhhh",
                [("h", S((d, d), F32))] * (2 * pairs), [VM((pairs, 2, d, d), BF), VM((2 * pairs, d, d), F32)], 4 + 6 * pairs, 0, 8 * MIB, None, after)


def bits_below(size):
    return [1 << i for i in range(size.bit_length() - 1)]


class Layout:
    def __init__(self, mesh):
        self.nb, self.nt = mesh.shape["batch"], mesh.shape["tp"]
        self.tp = [("tp", b) for b in reversed(bits_below(self.nt))]
        self.batch = [("batch", b) for b in bits_below(self.nb)[1:]]
        self.lanes = (self.tp + self.batch, self.batch[:1] + self.tp + self.batch[1:])

    def partner(self, device, level):
        b, t = divmod(device, self.nt)
        axis, bit = level
        return (b ^ bit) * self.nt + t if axis == "batch" else b * self.nt + (t ^ bit)

    def swap(self, value, level):
        pairs = []
        for device in range(self.nb * self.nt):
            core, to = device // self.nt % 2, device
            for one in level if isinstance(level, list) else [level]:
                to = self.partner(to, self.lanes[core][one] if isinstance(one, int) else one)
            pairs.append((device, to))
        return lax.ppermute(value, ("batch", "tp"), pairs)


CORE = ("batch", 1)


def code_of(levels, place):
    out = jnp.int32(0)
    for axis, bit in levels:
        out = out * 2 + (place[axis] // bit) % 2
    return out


def add(a, b):
    return (a.astype(F32) + b.astype(F32)).astype(BF)


def scatter_levels(levels, rows, least=48):
    n = 0
    while n < len(levels) and rows % 32 == 0 and rows // 2 >= least:
        rows //= 2
        n += 1
    return n


class Chain:
    def __init__(self, lay, steps):
        self.lay, self.steps, self.result = lay, steps, None
        self.go(next(steps))

    def go(self, requests):
        self.sent = [v for v, _ in requests]
        self.here = [self.lay.swap(v, level) for v, level in requests]

    def step(self):
        try:
            self.go(self.steps.send(self.here))
        except StopIteration as end:
            self.result, self.sent, self.here = end.value, [], []
        return self


def fence(arrays, *chains):
    chains = [c for c in chains if c.here]
    arrays, held = lax.optimization_barrier((arrays, [c.here for c in chains]))
    for chain, here in zip(chains, held):
        chain.here = here
        chain.step()
    return arrays


def sent(*chains):
    return tuple(v for c in chains for v in c.sent)


def halving(a, b, levels):
    for level in levels:
        n = a.shape[0] // 2
        kept = add(a[:n], b[:n])
        (b,) = yield [(add(a[n:], b[n:]), level)]
        a = kept
    return a, b


def quartering(a, b, high, low):
    n = a.shape[0] // 4
    parts = [add(a[i * n:(i + 1) * n], b[i * n:(i + 1) * n]) for i in range(4)]
    got = yield [(parts[1], [low]), (parts[2], [high]), (parts[3], [high, low])]
    return sum((g.astype(F32) for g in got), parts[0].astype(F32)).astype(BF)


def fourfold(held, high, low):
    got = yield [(held, [low]), (held, [high]), (held, [high, low])]
    return jnp.concatenate([held] + got, axis=0)


def doubling(held, levels):
    for level in levels:
        (got,) = yield [(held, level)]
        held = jnp.concatenate([held, got], axis=0)
    return held


def spread(held, level):
    other, mine = yield [(held, level), (held, CORE)]
    (rest,) = yield [(other, CORE)]
    return held, other, mine, rest


def reduce_ffn(lay, gone, stay, keep):
    m = len(lay.lanes[0])
    n = gone.shape[0]
    (recv,) = yield [(gone, CORE)]
    b, recv = yield [(add(keep[n:], recv), 0), (stay, CORE)]
    a, b = yield from halving(add(keep[:n], recv), b, range(1, m - 2))
    held = yield from quartering(a, b, m - 2, m - 1)
    held = yield from doubling(held, reversed(lay.batch[1:]))
    return (yield from spread(held, lay.batch[0]))


def reduce_pair(lay, n, send, keep, ahead):
    (recv,) = yield [(send, CORE)]
    if ahead:
        held = add(*(yield from halving(keep, recv, range(n))))
    else:
        a, b = yield from halving(keep, recv, range(n - 2))
        held = yield from quartering(a, b, n - 2, n - 1)
    for level in range(n, len(lay.lanes[0])):
        (got,) = yield [(held, level)]
        held = add(held, got)
    return held


def gather_pairs(lay, n, held):
    held = yield from fourfold(held, n - 2, n - 1)
    held = yield from doubling(held, reversed(range(1, n - 2)))
    return (yield from spread(held, 0))


def reduce_small(lay, vectors, hidden):
    n, shard = vectors.shape[0], hidden[0].shape[0]
    for level in lay.tp:
        bit = level[1]
        (got,) = yield [(jnp.concatenate([vectors] + [hidden[j + bit] for j in range(bit)]), level)]
        vectors = vectors + got[:n]
        hidden = [hidden[j] + got[n + j * shard:n + (j + 1) * shard] for j in range(bit)]
    held = jnp.concatenate([vectors, hidden[0]])
    for level in [CORE] + lay.batch[:-2]:
        (got,) = yield [(held, level)]
        held = held + got
    high, low = lay.batch[-2:]
    got = yield [(held, [low]), (held, [high]), (held, [high, low])]
    return held + got[0] + got[1] + got[2]


def on_device(
    lay,
    inputs,
    cotangent,
    zinc_lengths,
    pubchem_lengths,
    feature_stack,
    train_step,
    redraw_interval,
    attn_gain,
    attn_shift,
    query_weight,
    query_bias,
    key_weight,
    key_bias,
    value_weight,
    value_bias,
    output_weight,
    output_bias,
    ffn_gain,
    ffn_shift,
    hidden_weight,
    hidden_bias,
    return_weight,
    return_bias,
):
    nt = lay.nt
    d, shard = hidden_weight.shape
    rows = inputs.shape[0]
    width = min(768, shard)
    chunks = shard // width
    zm, pm = zinc_lengths.shape[0], pubchem_lengths.shape[0]
    place = {"batch": lax.axis_index("batch"), "tp": lax.axis_index("tp")}
    core = place["batch"] % 2

    def shares(k):
        hw = lax.dynamic_slice(hidden_weight, (core * (d // 2), k * width), (d // 2, width))
        rw = lax.dynamic_slice(return_weight, (k * width + core * (width // 2), 0), (width // 2, d))
        return [jnp.concatenate([hw, rw], axis=0)] if width == d else [hw, rw]

    def from_tp(own):
        pool = {0: own}
        for level in lay.tp:
            for j in list(pool):
                pool[j | level[1]] = [lay.swap(v, level) for v in pool[j]]
        return [v for j in range(1, nt) for v in pool[j]]

    own = [shares(k) for k in range(chunks)]
    per = len(own[0])
    biases = from_tp([hidden_bias])
    here = {k: from_tp(own[k]) for k in range(chunks)}

    n_pair = scatter_levels(lay.lanes[0], d)
    codes = [code_of(lane[:n_pair], place) for lane in lay.lanes]
    pick = train_step[0] // redraw_interval[0] % feature_stack.shape[0]
    meta = jnp.stack([core, code_of(lay.batch, place), jnp.where(core == 0, codes[0], codes[1]), jnp.where(core == 0, codes[1], codes[0]),
                      code_of(lay.batch[:-2], place) * 4, pick]).astype(jnp.int32)
    table = rotary_const()

    out = attend_fwd(
        meta, zinc_lengths, pubchem_lengths, cotangent, inputs,
        (attn_gain, attn_shift, query_bias, key_bias, value_bias, output_bias, ffn_gain, ffn_shift),
        query_weight, key_weight, value_weight, output_weight, feature_stack, table)
    out, here[0], biases = lax.optimization_barrier((out, here[0], biases))
    qkv, f, state, trans, middle, n2, left, proj = out

    pieces, pair_pieces = 2 ** len(lay.batch), 2 ** n_pair
    chains, acts, rws, hidden, before = [], [], [], [], ()
    for k in range(chunks):
        if chains:
            here[k] = fence(here[k], chains[-1])
        near = [lay.swap(v, CORE) for v in here[k]]
        parts = [[v[i] for i in range(j * per, (j + 1) * per) for v in (here[k], near)] for j in range(nt - 1)]
        out = ffn_chunk(meta, pieces, nt, n2, left, cotangent, hidden_bias, hidden_weight, return_weight, parts, biases, k, width,
                        before, sent(*chains))
        gone, stay, keep, act, bias, e, rw = fence(out, *chains)
        before = (e,)
        chains.append(Chain(lay, reduce_ffn(lay, gone, stay, keep)))
        acts.append(act)
        rws.append(rw)
        hidden.append(bias)

    middle = fence(middle, chains[-1])
    out = mid(e, cotangent, middle, output_weight, ffn_gain, sent(*chains))
    gm, gb, gatt, vec1 = fence(out, *chains[:-1])
    out = value_bwd(meta, zm, pm, pair_pieces, gatt, gb, f, state, trans, sent(*chains))
    send, keep, gv, uw, gst, vec2 = fence(out, *chains)
    pair_a = Chain(lay, reduce_pair(lay, n_pair, send, keep, True))
    uw = fence(uw, pair_a)
    out = query_bwd(meta, zm, pm, pair_pieces, uw, gst, qkv, f, state, trans, proj, table, sent(pair_a, *chains))
    send, keep, gqk, vec3 = fence(out, pair_a, *chains)
    pair_b = Chain(lay, reduce_pair(lay, n_pair, send, keep, False))
    gqk = fence(gqk, pair_b)
    out = input_back(gqk, gv, query_weight, key_weight, value_weight, inputs, gm, attn_gain, sent(pair_a, pair_b, *chains))
    (input_grad, vec4), middle = fence((out, middle), pair_a, pair_b, *chains)
    layer_out = layer_end(acts, rws, middle, return_bias, sent(pair_b, pair_a, *chains))
    layer_out, vec4 = fence((layer_out, vec4), pair_b, pair_a, *chains)
    vec3 = jnp.concatenate([vec3, vec4], axis=0)
    vectors = jnp.concatenate([vec1, vec2, vec3], axis=0).reshape(-1)
    small = Chain(lay, reduce_small(lay, vectors, [jnp.concatenate([hidden[k][j] for k in range(chunks)]) for j in range(nt)]))

    ffn_out, k, pairs = (), 0, None
    while pairs is None or pairs.here or any(c.here for c in chains):
        every = [pairs] if pairs else [pair_b, pair_a]
        every += chains + [small]
        if k < chunks and chains[k].result is not None:
            ffn_out = finish_ffn(meta, pieces, chains[k].result, k, shard, ffn_out, sent(*every))
            k += 1
            ffn_out = fence(ffn_out, *every)
        else:
            fence((), *every)
        if pairs is None and pair_a.result is not None and pair_b.result is not None:
            pairs = Chain(lay, gather_pairs(lay, n_pair, jnp.concatenate([pair_a.result, pair_b.result], axis=1)))
    while k < chunks:
        ffn_out = finish_ffn(meta, pieces, chains[k].result, k, shard, ffn_out, sent(small))
        k += 1
    while small.here:
        small.step()
    gwo, gwv, gwq, gwk = finish_pair(meta, pair_pieces, pairs.result, d, (small.result,))
    vecs = small.result[:9 * d].reshape(9, d)
    return (layer_out, input_grad, vecs[7], vecs[8], gwq, vecs[5], gwk, vecs[6], gwv, vecs[4], gwo, vecs[2],
            vecs[0], vecs[1], ffn_out[0], small.result[9 * d:], ffn_out[1], vecs[3])


def solution(mesh):
    rows, whole, hidden = P(("batch", "tp"), None), P(), P(None, "tp")
    return jax.shard_map(
        functools.partial(on_device, Layout(mesh)),
        mesh=mesh,
        in_specs=(rows, rows, P(("batch", "tp")), P(("batch", "tp"))) + (whole,) * 15 + (hidden, P("tp"), P("tp", None), whole),
        out_specs=(rows, rows) + (whole,) * 12 + (hidden, P("tp"), P("tp", None), whole),
        check_vma=False,
    )
```

```python
import functools
import math

import jax
import jax.numpy as jnp
import numpy as np
from jax import lax
from jax.experimental import pallas as pl
from jax.experimental.pallas import tpu as pltpu
from jax.sharding import PartitionSpec as P

ZPAD = 64
PPAD = 256
F32 = jnp.float32
BF = jnp.bfloat16
VM = pltpu.VMEM
GROUP = 4
S = jax.ShapeDtypeStruct
TIMES = {"attend_fwd": 24, "ffn_chunk": 17, "layer_end": 9, "mid": 8, "value_bwd": 13, "query_bwd": 13, "input_back": 10, "finish_ffn": 5, "finish_pair": 5}
MIB = 2**20
GRANT = 52


def dot(a, b):
    return jnp.dot(a, b, preferred_element_type=F32)


def dot_t(a, b):
    return lax.dot_general(a, b, (((1,), (1,)), ((), ())), preferred_element_type=F32)


def dot_c(a, b):
    return lax.dot_general(a, b, (((0,), (0,)), ((), ())), preferred_element_type=F32)


def split(v):
    hi = v.astype(BF)
    return hi, (v - hi.astype(F32)).astype(BF)


def norm_parts(values):
    center = values - jnp.mean(values, axis=-1, keepdims=True)
    rate = lax.rsqrt(jnp.mean(center * center, axis=-1, keepdims=True) + 1e-05)
    return center * rate, rate


def row(ref):
    return ref[...].reshape(1, -1)


def block_mask(width):
    f = lax.broadcasted_iota(jnp.int32, (128, width), 0) // 32
    c = lax.broadcasted_iota(jnp.int32, (128, width), 1) % 256 // 64
    return f == c


def molecules(zm, pm):
    return [(i * ZPAD, ZPAD) for i in range(zm)] + [(zm * ZPAD + i * PPAD, PPAD) for i in range(pm)]


def members(mols, b):
    return [(i, r, n) for i, (r, n) in enumerate(mols) if b * PPAD <= r < (b + 1) * PPAD]


class Mover:
    def __init__(self, sems):
        self.sems, self.n, self.out = sems, 0, []

    def load(self, src, dst):
        copy = pltpu.make_async_copy(src, dst, self.sems.at[self.n])
        self.n += 1
        copy.start()
        return copy

    def store(self, src, dst):
        self.out.append(self.load(src, dst))

    def finish(self):
        for copy in self.out:
            copy.wait()


def call(kernel, name, args, spaces, outs, scratch, copies, flops, moved, aliases=None, after=()):
    n, extra = len(args), len(after)

    def body(*refs):
        kernel(*refs[:n], *refs[n + extra:])

    spec = {
        "v": pl.BlockSpec(memory_space=VM),
        "h": pl.BlockSpec(memory_space=pltpu.HBM),
        "s": pl.BlockSpec(memory_space=pltpu.SMEM),
    }
    return pl.pallas_call(
        body,
        out_shape=tuple(o for _, o in outs),
        in_specs=[spec[s] for s in spaces] + [spec["h"]] * extra,
        out_specs=tuple(spec[s] for s, _ in outs),
        scratch_shapes=list(scratch) + [pltpu.SemaphoreType.DMA((copies,))],
        input_output_aliases=aliases or {},
        compiler_params=pltpu.CompilerParams(vmem_limit_bytes=GRANT * MIB),
        cost_estimate=pl.CostEstimate(flops=int(TIMES[name] * 1.15e9), bytes_accessed=moved, transcendentals=0),
        name=name,
    )(*args, *after)


def place_heads(scaled):
    two = jnp.concatenate([scaled, scaled], axis=1)
    return jnp.where(block_mask(256), jnp.concatenate([two, two], axis=1), 0.0)


def attend_fwd_kernel(zm, pm, meta, zlen, plen, cot_h, x_h, gain_h, shift_h, bq_h, bk_h, bv_h, bo_h, gain2_h, shift2_h,
                      wq_h, wk_h, wv_h, wo_h, stack_h, table_h, energy_h,
                      qkv_h, f_h, state_h, trans_h, middle_h, n2_h, left_h, proj_h,
                      cot, n2_s, left, x, vec, wq, wk, wv, wo, fp, proj, table, energy, qkv, f_s, state_s, trans, middle_s, att_s, sems):
    move = Mover(sems)
    rows, d = x.shape
    first = [move.load(x_h, x), move.load(gain_h, vec.at[0]), move.load(shift_h, vec.at[1]), move.load(stack_h.at[meta[5]], fp),
             move.load(cot_h, cot)]
    later = [move.load(s, t) for s, t in ((wq_h, wq), (bq_h, vec.at[2]), (table_h, table), (energy_h, energy), (wk_h, wk),
                                          (bk_h, vec.at[3]), (wv_h, wv), (bv_h, vec.at[4]))]
    last = [move.load(s, t) for s, t in ((wo_h, wo), (bo_h, vec.at[5]), (gain2_h, vec.at[6]), (shift2_h, vec.at[7]))]
    mols = molecules(zm, pm)
    groups = d // 256
    blocks = range(rows // PPAD)
    keep = block_mask(512)
    ones = jnp.ones((PPAD, 256), BF)

    def vector(i):
        return vec[i].reshape(1, -1)

    for c in first:
        c.wait()
    for g in range(groups):
        p = fp[g * GROUP:(g + 1) * GROUP].reshape(GROUP * 32, 64) * 64 ** -0.25
        turned = jnp.concatenate([p[:, 32:], -p[:, :32]], axis=1)
        hi, lo = split(jnp.concatenate([place_heads(p), place_heads(turned)], axis=1))
        proj[0, g] = hi
        proj[1, g] = lo
    n1s = {}
    for b in blocks:
        rs = slice(b * PPAD, (b + 1) * PPAD)
        normed, _ = norm_parts(x[rs, :].astype(F32))
        n1s[b] = (normed * vector(0) + vector(1)).astype(BF)
        trans[1, :, rs] = n1s[b].T
        left[1, :, rs] = cot[rs, :].T
    for c in later:
        c.wait()
    move.store(proj.at[0], proj_h)
    move.store(trans.at[1], trans_h.at[1])
    move.store(left.at[1], left_h.at[1])
    for b in blocks:
        mem = members(mols, b)
        rs = slice(b * PPAD, (b + 1) * PPAD)
        n1 = n1s[b]
        cosb, sinb = (jnp.concatenate([table[t, :n, :] for _, _, n in mem], axis=0) for t in range(2))
        cosb = jnp.concatenate([cosb, cosb], axis=1)
        sinb = jnp.concatenate([sinb, sinb], axis=1)
        live = jnp.concatenate(
            [(lax.broadcasted_iota(jnp.int32, (n, 128), 0) < (zlen[i] if i < zm else plen[i - zm])).astype(F32) for i, r, n in mem], axis=0)
        for g in range(groups):
            cs = slice(g * 256, (g + 1) * 256)
            fs = slice(g * 128, (g + 1) * 128)

            def features(w, bias, slot):
                v = dot(n1, w[:, cs]) + vector(bias)[:, cs]
                qkv[slot, rs, cs] = v.astype(BF)
                ch, cl = split(v * cosb)
                sh, sl = split(v * sinb)
                eh, el = split(v * v)
                ph, plo = proj[0, g], proj[1, g]
                e = energy[...]
                inner = (dot_t(ch, ph[:, :256]) + dot_t(sh, ph[:, 256:]) + dot_t(cl, ph[:, :256]) + dot_t(sl, ph[:, 256:])
                         + dot_t(ch, plo[:, :256]) + dot_t(sh, plo[:, 256:]) - dot_t(eh, e) - dot_t(el, e))
                return jnp.exp(inner) * (32 ** -0.5)

            fq = features(wq, 2, 0).astype(BF)
            fk = (features(wk, 3, 1) * live).astype(BF)
            f_s[0, rs, fs] = fq
            f_s[1, rs, fs] = fk
            v = (dot(n1, wv[:, cs]) + vector(4)[:, cs]).astype(BF)
            qkv[2, rs, cs] = v
            for i, r, n in mem:
                ms = slice(r - b * PPAD, r - b * PPAD + n)
                vo = jnp.concatenate([v[ms], ones[:n]], axis=1)
                state = jnp.where(keep, dot_c(fk[ms], vo), 0.0).astype(BF)
                state_s[i, g] = state
                nd = dot(fq[ms], state)
                att_s[r:r + n, cs] = (nd[:, :256] / nd[:, 256:]).astype(BF)
    for s, t in ((qkv, qkv_h), (f_s, f_h), (state_s, state_h)):
        move.store(s, t)
    for c in last:
        c.wait()
    for b in blocks:
        rs = slice(b * PPAD, (b + 1) * PPAD)
        trans[0, :, rs] = att_s[rs, :].T
        middle = x[rs, :].astype(F32) + (dot(att_s[rs, :], wo[...]) + vector(5))
        middle_s[rs, :] = middle
        normed, _ = norm_parts(middle)
        n2 = (normed * vector(6) + vector(7)).astype(BF)
        n2_s[rs, :] = n2
        left[0, :, rs] = n2.T
    move.store(middle_s, middle_h)
    move.store(n2_s, n2_h)
    move.store(trans.at[0], trans_h.at[0])
    move.store(left.at[0], left_h.at[0])
    move.finish()


def rotary_const():
    place = np.arange(PPAD, dtype=np.float64)
    rates = np.exp(np.arange(32, dtype=np.float64) * (-2.0 * math.log(10000.0) / 64))
    ang = place[:, None] * rates[None, :]
    return np.tile(np.stack([np.cos(ang), np.sin(ang)]), (1, 1, 4)).astype(np.float32)


def head_const(scale):
    f = np.arange(128)[:, None] // 32
    c = np.arange(256)[None, :] // 64
    return ((f == c) * scale).astype(jnp.bfloat16)


def attend_fwd(meta, zlen, plen, cot, x, vectors, wq, wk, wv, wo, stack, table):
    rows, d = x.shape
    zm, pm = zlen.shape[0], plen.shape[0]
    groups = d // 256
    states = (zm + pm, groups, 128, 512)
    outs = [S((3, rows, d), BF), S((2, rows, d // 2), BF), S(states, BF), S((2, d, rows), BF),
            S((rows, d), F32), S((rows, d), BF), S((2, d, rows), BF), S((groups, 128, 512), BF)]
    args = (meta, zlen, plen, cot, x, *vectors, wq, wk, wv, wo, stack, table, head_const(1 / 16))
    scratch = ([VM((rows, d), BF)] * 2 + [VM((2, d, rows), BF), VM((rows, d), BF), VM((8, d), F32)] + [VM((d, d), BF)] * 4
               + [VM(stack.shape[1:], F32), VM((2, groups, 128, 512), BF), VM(table.shape, F32), VM((128, 256), BF)]
               + [VM((3, rows, d), BF), VM((2, rows, d // 2), BF), VM(states, BF), VM((2, d, rows), BF), VM((rows, d), F32), VM((rows, d), BF)])
    return call(
        functools.partial(attend_fwd_kernel, zm, pm), "attend_fwd", args, "sss" + "h" * (len(args) - 3),
        [("h", o) for o in outs], scratch, 32, 2 * rows * d * d * 4, 16 * MIB)


def gelu_parts(h):
    bell = jnp.exp(h * h * -0.5)
    t = 1.0 / (1.0 + (0.3275911 * math.sqrt(0.5)) * jnp.abs(h))
    poly = t * (0.127414796 + t * (-0.142248368 + t * (0.7107068705 + t * (-0.7265760135 + t * 0.5307027145))))
    tail = poly * bell
    phi = jnp.where(h >= 0, 1.0 - tail, tail)
    return h * phi, phi + h * bell * (1.0 / math.sqrt(2 * math.pi))


def place_pieces(code, src, dst):
    n, step = src.shape[0], src.shape[1]
    for p in range(n):
        off = pl.multiple_of(jnp.bitwise_xor(p, code) * step, 16)
        dst[pl.ds(off, step), :] = src[p]


def ffn_kernel(pieces, shards, k, per, meta, n2_h, left_h, cot_h, hb_h, hw_h, rw_h, *refs):
    parts = {j: refs[(j - 1) * per:j * per] for j in range(1, shards)}
    hbs = refs[(shards - 1) * per:(shards - 1) * (per + 1)]
    e_prev = refs[(shards - 1) * (per + 1)] if k else None
    (gone_h, stay_h, keep_h, act_h, bias_o, e_h, rws_h, n2, left, cot, hb, hw, rw, hw2, rw2, right, stage, e_s, sems) = refs[-19:]
    move = Mover(sems)
    d, width = hw.shape[1:]
    half_d = d // 2
    me, code = meta[0], meta[1]
    order = list(range(1, shards)) + [0]
    early, late = {}, {}
    for j in order:
        early[j] = [move.load(hbs[j - 1] if j else hb_h, hb.at[j])]
        if j == order[0]:
            early[j].append(move.load(n2_h, n2))
        late[j] = []
        if j == 0:
            early[j].append(move.load(hw_h.at[:, k * width:(k + 1) * width], hw.at[0]))
            late[j].append(move.load(rw_h.at[k * width:(k + 1) * width, :], rw.at[0]))
        elif per == 2:
            early[j] += [move.load(parts[j][p].at[:half_d], hw2.at[j - 1, p]) for p in range(2)]
            late[j] += [move.load(parts[j][p].at[half_d:], rw2.at[j - 1, p]) for p in range(2)]
        else:
            early[j] += [move.load(parts[j][p], hw2.at[j - 1, p]) for p in range(2)]
            late[j] += [move.load(parts[j][2 + p], rw2.at[j - 1, p]) for p in range(2)]
        if j == order[0]:
            late[j].append(move.load(cot_h, cot))
    last = [move.load(left_h, left)]
    if k:
        last.append(move.load(e_prev, e_s))
    step, half = d // pieces, pieces // 2
    tile = width
    for j in order:
        for c in early[j] + late[j]:
            c.wait()
        if j:
            place_pieces(me, hw2.at[j - 1], hw.at[j])
            place_pieces(me, rw2.at[j - 1], rw.at[j])
        bias = hb[j].reshape(1, -1)[:, k * width:(k + 1) * width].astype(F32)
        for c in range(0, width, tile):
            cs = slice(c, c + tile)
            h = dot(n2[...], hw[j, :, cs]) + bias[:, cs]
            act, slope = gelu_parts(h)
            ga = dot_t(cot[...], rw[j, cs, :])
            gh = (ga * slope).astype(BF)
            right[0, j, :, cs] = gh
            right[1, j, :, cs] = act.astype(BF)
            bias_o[j:j + 1, cs] = jnp.sum(gh.astype(F32), axis=0, keepdims=True)
        move.store(right.at[1, j], act_h.at[j])
        move.store(rw.at[j], rws_h.at[j])
    for c in last:
        c.wait()
    for c in range(0, d, 768):
        cs = slice(c, c + 768)
        part = sum(dot_t(right[0, j], hw[j, cs, :]) for j in order)
        e_s[:, cs] = e_s[:, cs] + part if k else part
    move.store(e_s, e_h)
    for kind, slot in ((1 - me, 0), (me, 1)):
        for j in order:
            for c in range(0, width, tile):
                cs = slice(c, c + tile)
                value = dot(left[kind], right[kind, j, :, cs]).astype(BF)
                for p in range(pieces):
                    rel = jnp.bitwise_xor(p, code)
                    second = rel // half * (shards * half) + j * half + rel % half
                    off = pl.multiple_of(jnp.where(kind == 0, j * pieces + rel, second) * step, 16)
                    stage[slot, pl.ds(off, step), cs] = value[p * step:(p + 1) * step]
        if slot:
            move.store(stage.at[1], keep_h)
        else:
            cut = shards * d // 2
            move.store(stage.at[0, cut:], gone_h)
            move.store(stage.at[0, :cut], stay_h)
    move.finish()


def ffn_chunk(meta, pieces, shards, n2, left, cot, hb, hw, rw, parts, hbs, k, width, before, after=()):
    rows, d = n2.shape
    per = len(parts[0])
    part = S((shards * d // 2, width), BF)
    outs = [("h", part), ("h", part), ("h", S((shards * d, width), BF)), ("h", S((shards, rows, width), BF)), ("v", S((shards, width), F32)),
            ("h", S((rows, d), F32)), ("h", S((shards, width, d), BF))]
    scratch = [VM((rows, d), BF), VM((2, d, rows), BF), VM((rows, d), BF), VM((shards, 1) + hb.shape, BF), VM((shards, d, width), BF),
               VM((shards, width, d), BF), VM((shards - 1, 2, d // 2, width), BF), VM((shards - 1, 2, width // 2, d), BF),
               VM((2, shards, rows, width), BF), VM((2, shards * d, width), BF), VM((rows, d), F32)]
    args = (meta, n2, left, cot, hb.reshape(1, -1), hw, rw) + tuple(p for part in parts for p in part) + tuple(b.reshape(1, -1) for b in hbs) + tuple(before)
    return call(
        functools.partial(ffn_kernel, pieces, shards, k, per), "ffn_chunk", args,
        "s" + "h" * (len(args) - 1), outs, scratch, 12 + 13 * shards, 2 * rows * d * width * 5 * shards, 12 * MIB, None, after)


def products(move, pieces, codes, stage, outs):
    for slot, (left, right, out) in enumerate(outs):
        d = out.shape[0]
        step = d // pieces
        for c in range(0, d, 768):
            cs = slice(c, c + 768)
            value = dot(left[...], right[:, cs]).astype(BF)
            for p in range(pieces):
                off = pl.multiple_of(jnp.bitwise_xor(p, codes[slot]) * step, 16)
                stage[slot, pl.ds(off, step), cs] = value[p * step:(p + 1) * step]
        move.store(stage.at[slot], out)


def mid_kernel(e_h, cot_h, middle_h, wo_h, vec_h, gm_h, gb_h, gatt_h, vec_o, e_s, cot, middle, wo, vec, gm_s, gb_s, gatt, sems):
    move = Mover(sems)
    rows, d = middle.shape
    loads = [[move.load(s.at[r:r + 256], t.at[r:r + 256]) for s, t in ((middle_h, middle), (e_h, e_s), (cot_h, cot))]
             for r in range(0, rows, 256)]
    gain = move.load(vec_h, vec)
    last = move.load(wo_h, wo)
    gain.wait()
    gain2 = row(vec)
    acc_g = acc_s = acc_b = acc_c = 0.0
    for i, r in enumerate(range(0, rows, 256)):
        for c in loads[i]:
            c.wait()
        rs = slice(r, r + 256)
        e = e_s[rs, :]
        n, rate = norm_parts(middle[rs, :])
        c = cot[rs, :].astype(F32)
        acc_g += jnp.sum(e * n, axis=0, keepdims=True)
        acc_s += jnp.sum(e, axis=0, keepdims=True)
        acc_c += jnp.sum(c, axis=0, keepdims=True)
        eg = e * gain2
        gm = c + rate * (eg - jnp.mean(eg, axis=-1, keepdims=True) - n * jnp.mean(eg * n, axis=-1, keepdims=True))
        gm_s[rs, :] = gm
        gb = gm.astype(BF)
        gb_s[rs, :] = gb
        acc_b += jnp.sum(gb.astype(F32), axis=0, keepdims=True)
    for i, acc in enumerate((acc_g, acc_s, acc_b, acc_c)):
        vec_o[i:i + 1, :] = acc
    move.store(gm_s, gm_h)
    move.store(gb_s, gb_h)
    last.wait()
    for c in range(0, d, 768):
        cs = slice(c, c + 768)
        gatt[:, cs] = dot_t(gb_s[...], wo[cs, :]).astype(BF)
    move.store(gatt, gatt_h)
    move.finish()


def mid(e, cot, middle, wo, gain2, after=()):
    rows, d = middle.shape
    outs = [("h", S((rows, d), F32)), ("h", S((rows, d), BF)), ("h", S((rows, d), BF)), ("v", S((4, d), F32))]
    scratch = [VM((rows, d), F32), VM((rows, d), BF), VM((rows, d), F32), VM((d, d), BF), VM(gain2.shape, F32), VM((rows, d), F32),
               VM((rows, d), BF), VM((rows, d), BF)]
    args = (e, cot, middle, wo, gain2)
    return call(mid_kernel, "mid", args, "h" * len(args), outs, scratch, 8 + 3 * (rows // 256), 2 * rows * d * d, 8 * MIB, None, after)


def value_bwd_kernel(zm, pm, pieces, meta, gatt_h, gb_h, f_h, state_h, trans_h,
                     send_h, keep_h, gv_h, uw_h, gst_h, vec_o, gatt, uw_o, gst_o, f, state, left, right, stage, sems):
    move = Mover(sems)
    mols = molecules(zm, pm)
    rows, d = gatt.shape
    groups = d // 256
    loads = []
    for g in range(groups):
        cs, fs = slice(g * 256, (g + 1) * 256), slice(g * 128, (g + 1) * 128)
        loads.append([move.load(f_h.at[:, :, fs], f.at[:, :, fs]), move.load(state_h.at[:, g], state.at[:, g]),
                      move.load(gatt_h.at[:, cs], gatt.at[:, cs])])
    last = [move.load(trans_h, left), move.load(gb_h, right.at[0])]
    keep = block_mask(512)
    for g in range(groups):
        for c in loads[g]:
            c.wait()
        cs = slice(g * 256, (g + 1) * 256)
        fs = slice(g * 128, (g + 1) * 128)
        total = 0.0
        for i, (r, n) in enumerate(mols):
            ms = slice(r, r + n)
            st = state[i, g]
            q = f[0, ms, fs]
            nd = dot(q, st)
            rden = 1.0 / nd[:, 256:]
            u = gatt[ms, cs].astype(F32) * rden
            uw = jnp.concatenate([u, -(u * (nd[:, :256] * rden))], axis=1).astype(BF)
            uw_o[ms, slice(g * 512, (g + 1) * 512)] = uw
            gst = jnp.where(keep, dot_c(q, uw), 0.0).astype(BF)
            gst_o[i, g] = gst
            gv = dot(f[1, ms, fs], gst[:, :256]).astype(BF)
            right[1, ms, cs] = gv
            total += jnp.sum(gv.astype(F32), axis=0, keepdims=True)
        vec_o[0:1, cs] = total
    move.store(right.at[1], gv_h)
    move.store(uw_o, uw_h)
    move.store(gst_o, gst_h)
    for c in last:
        c.wait()
    me = meta[0]
    products(move, pieces, (meta[3], meta[2]), stage, ((left.at[1 - me], right.at[1 - me], send_h), (left.at[me], right.at[me], keep_h)))
    move.finish()


def value_bwd(meta, zm, pm, pieces, gatt, gb, f, state, trans, after=()):
    rows, d = gatt.shape
    outs = [("h", S((d, d), BF))] * 2 + [("h", S((rows, d), BF)), ("h", S((rows, 2 * d), BF)), ("h", S(state.shape, BF)), ("v", S((1, d), F32))]
    scratch = [VM((rows, d), BF), VM((rows, 2 * d), BF), VM(state.shape, BF), VM(f.shape, BF), VM(state.shape, BF), VM((2, d, rows), BF),
               VM((2, rows, d), BF), VM((2, d, d), BF)]
    args = (meta, gatt, gb, f, state, trans)
    return call(functools.partial(value_bwd_kernel, zm, pm, pieces), "value_bwd", args, "shhhhh", outs, scratch,
                10 + 3 * d // 256, 2 * d**3 * 3, 8 * MIB, None, after)


def query_bwd_kernel(zm, pm, pieces, meta, uw_h, gst_h, qkv_h, f_h, state_h, trans_h, proj_h, energy_h, table_h,
                     send_h, keep_h, gqk_h, vec_o, uw, gst, qkv, f, state, n1t, proj, energy, table, gqk, stage, sems):
    move = Mover(sems)
    mols = molecules(zm, pm)
    _, rows, d = qkv.shape
    loads = [[move.load(s, t) for s, t in ((proj_h, proj), (energy_h, energy), (table_h, table))]]
    for g in range(d // 256):
        cs, fs, us = slice(g * 256, (g + 1) * 256), slice(g * 128, (g + 1) * 128), slice(g * 512, (g + 1) * 512)
        if g:
            loads.append([])
        loads[g] += [move.load(uw_h.at[:, us], uw.at[:, us]), move.load(state_h.at[:, g], state.at[:, g]),
                     move.load(f_h.at[:, :, fs], f.at[:, :, fs]), move.load(gst_h.at[:, g], gst.at[:, g]),
                     move.load(qkv_h.at[:, :, cs], qkv.at[:, :, cs])]
    later = [move.load(trans_h.at[1], n1t)]
    for g in range(d // 256):
        for c in loads[g]:
            c.wait()
        cs = slice(g * 256, (g + 1) * 256)
        fs = slice(g * 128, (g + 1) * 128)
        sums = [0.0, 0.0]
        for b in range(rows // PPAD):
            mem = members(mols, b)
            rs = slice(b * PPAD, (b + 1) * PPAD)
            gfq, gfk = [], []
            for i, r, n in mem:
                ms = slice(r, r + n)
                gfq.append(dot_t(uw[ms, slice(g * 512, (g + 1) * 512)], state[i, g]))
                gfk.append(dot_t(jnp.concatenate([qkv[2, ms, cs], jnp.ones((n, 256), BF)], axis=1), gst[i, g]))
            cosb, sinb = (jnp.concatenate([table[t, :n, :] for _, _, n in mem], axis=0) for t in range(2))
            cosb = jnp.concatenate([cosb, cosb], axis=1)
            sinb = jnp.concatenate([sinb, sinb], axis=1)
            for t, gf in enumerate((gfq, gfk)):
                gp = (jnp.concatenate(gf, axis=0) * f[t, rs, fs].astype(F32)).astype(BF)
                back = dot(gp, proj[g])
                tot = dot(gp, energy[...])
                grad = (cosb * back[:, :256] + sinb * back[:, 256:] - tot * qkv[t, rs, cs].astype(F32)).astype(BF)
                gqk[t, rs, cs] = grad
                sums[t] += jnp.sum(grad.astype(F32), axis=0, keepdims=True)
        for t in range(2):
            vec_o[t:t + 1, cs] = sums[t]
    for c in later:
        c.wait()
    me = meta[0]
    products(move, pieces, (meta[3], meta[2]), stage, ((n1t, gqk.at[1 - me], send_h), (n1t, gqk.at[me], keep_h)))
    move.store(gqk, gqk_h)
    move.finish()


def query_bwd(meta, zm, pm, pieces, uw, gst, qkv, f, state, trans, proj, table, after=()):
    _, rows, d = qkv.shape
    outs = [("h", S((d, d), BF))] * 2 + [("h", S((2, rows, d), BF)), ("v", S((2, d), F32))]
    scratch = [VM(uw.shape, BF), VM(gst.shape, BF), VM(qkv.shape, BF), VM(f.shape, BF), VM(state.shape, BF), VM((d, rows), BF),
               VM(proj.shape, BF), VM((128, 256), BF), VM(table.shape, F32), VM((2, rows, d), BF), VM((2, d, d), BF)]
    args = (meta, uw, gst, qkv, f, state, trans, proj, head_const(64 ** -0.5), table)
    return call(functools.partial(query_bwd_kernel, zm, pm, pieces), "query_bwd", args, "s" + "h" * (len(args) - 1), outs, scratch,
                8 + 5 * d // 256, 2 * d**3 * 6, 12 * MIB, None, after)


def input_kernel(gqk_h, gv_h, wq_h, wk_h, wv_h, x_h, gm_h, gain_h, out_h, vec_o, gqk, gv, wq, wk, wv, x, gm, vec, e_s, out_s, sems):
    move = Mover(sems)
    rows, d = x.shape
    loads = [(move.load(gqk_h.at[0], gqk.at[0]), move.load(wq_h, wq)), (move.load(gqk_h.at[1], gqk.at[1]), move.load(wk_h, wk)),
             (move.load(gv_h, gv), move.load(wv_h, wv))]
    last = [move.load(s, t) for s, t in ((x_h, x), (gm_h, gm), (gain_h, vec))]
    for (left, right), load in zip(((gqk.at[0], wq), (gqk.at[1], wk), (gv, wv)), loads):
        for c in load:
            c.wait()
        for c in range(0, d, 768):
            cs = slice(c, c + 768)
            part = dot_t(left[...], right[cs, :])
            e_s[:, cs] = part if right is wq else e_s[:, cs] + part
    for c in last:
        c.wait()
    gain = row(vec)
    acc_g = acc_s = 0.0
    for r in range(0, rows, 256):
        rs = slice(r, r + 256)
        e = e_s[rs, :]
        n, rate = norm_parts(x[rs, :].astype(F32))
        acc_g += jnp.sum(e * n, axis=0, keepdims=True)
        acc_s += jnp.sum(e, axis=0, keepdims=True)
        eg = e * gain
        gx = rate * (eg - jnp.mean(eg, axis=-1, keepdims=True) - n * jnp.mean(eg * n, axis=-1, keepdims=True))
        out_s[rs, :] = (gm[rs, :] + gx).astype(BF)
    move.store(out_s, out_h)
    vec_o[0:1, :] = acc_g
    vec_o[1:2, :] = acc_s
    move.finish()


def input_back(gqk, gv, wq, wk, wv, x, gm, gain, after=()):
    rows, d = x.shape
    scratch = [VM(gqk.shape, BF), VM(gv.shape, BF)] + [VM((d, d), BF)] * 3 + [
        VM((rows, d), BF), VM((rows, d), F32), VM(gain.shape, F32), VM((rows, d), F32), VM((rows, d), BF)]
    args = (gqk, gv, wq, wk, wv, x, gm, gain)
    return call(input_kernel, "input_back", args, "h" * len(args), [("h", S((rows, d), BF)), ("v", S((2, d), F32))], scratch,
                16, 2 * d**3 * 3, 8 * MIB, None, after)


def layer_kernel(chunks, middle_h, vec_h, *refs):
    rights_h, rws_h = refs[:chunks], refs[chunks:2 * chunks]
    out_h, acts, rws, middle, vec, out_s, sems = refs[2 * chunks:]
    move = Mover(sems)
    base = [move.load(middle_h, middle), move.load(vec_h, vec)]
    loads = [[move.load(rights_h[k], acts.at[k]), move.load(rws_h[k], rws.at[k])] for k in range(chunks)]
    d = middle.shape[1]
    for c in base:
        c.wait()
    for k, load in enumerate(loads):
        for c in load:
            c.wait()
        for c in range(0, d, 768):
            cs = slice(c, c + 768)
            total = middle[:, cs] + sum(dot(acts[k, j], rws[k, j, :, cs]) for j in range(acts.shape[1]))
            if k + 1 < chunks:
                middle[:, cs] = total
            else:
                out_s[:, cs] = (total + row(vec)[:, cs]).astype(BF)
    move.store(out_s, out_h)
    move.finish()


def layer_end(rights, rws, middle, vec, after=()):
    rows, d = middle.shape
    k = len(rights)
    shards, _, width = rights[0].shape
    scratch = [VM((k, shards, rows, width), BF), VM((k, shards, width, d), BF), VM((rows, d), F32), VM(vec.shape, F32), VM((rows, d), BF)]
    args = (middle, vec, *rights, *rws)
    return call(functools.partial(layer_kernel, k), "layer_end", args, "h" * len(args),
                [("h", S((rows, d), BF))], scratch, 4 + 2 * k, 2 * rows * d * k * shards * width, 12 * MIB, None, after)[0]


def placed(ref, p, code, pieces):
    step = ref.shape[0] // pieces
    return ref[pl.ds(pl.multiple_of(jnp.bitwise_xor(p, code) * step, 16), step), :]


def load_halves(move, m0, m1, t0, t1, cols, both, me):
    half = m0.shape[0]
    return [move.load(m0.at[:, cols], both.at[me, :half]), move.load(m1.at[:, cols], both.at[me, half:]),
            move.load(t0.at[:, cols], both.at[1 - me, :half]), move.load(t1.at[:, cols], both.at[1 - me, half:])]


def finish_ffn_kernel(pieces, k, meta, m0, m1, t0, t1, *refs):
    ghw_h, grw_h, both, whole, wide, tall, sems = refs[-7:]
    move = Mover(sems)
    me, code = meta[0], meta[1]
    d, width = wide.shape
    for c in load_halves(move, m0, m1, t0, t1, slice(0, width), both, me):
        c.wait()
    step = d // pieces
    for p in range(pieces):
        wide[p * step:(p + 1) * step, :] = placed(both.at[0], p, code, pieces).astype(F32)
    move.store(wide, ghw_h.at[:, k * width:(k + 1) * width])
    for p in range(pieces):
        whole[p * step:(p + 1) * step, :] = placed(both.at[1], p, code, pieces)
    for c in range(0, width, 128):
        cs = slice(c, c + 128)
        tall[cs, :] = whole[:, cs].T.astype(F32)
    move.store(tall, grw_h.at[k * width:(k + 1) * width])
    move.finish()


def finish_ffn(meta, pieces, parts, k, shard, before, after=()):
    d, width = 2 * parts[0].shape[0], parts[0].shape[1]
    args = (meta, *parts, *before)
    return call(functools.partial(finish_ffn_kernel, pieces, k), "finish_ffn", args, "shhhh" + "h" * len(before),
                [("h", S((d, shard), F32)), ("h", S((shard, d), F32))],
                [VM((2, d, width), BF), VM((d, width), BF), VM((d, width), F32), VM((width, d), F32)], 8, 0, 4 * MIB,
                {5 + i: i for i in range(len(before))}, after)


def finish_pair_kernel(pieces, meta, m0, m1, t0, t1, *refs):
    outs, (both, wide, sems) = refs[:-3], refs[-3:]
    move = Mover(sems)
    me = meta[0]
    d = wide.shape[1]
    pairs = len(outs) // 2
    loads = [load_halves(move, m0, m1, t0, t1, slice(k * d, (k + 1) * d), both.at[k], me) for k in range(pairs)]
    step = d // pieces
    for k in range(pairs):
        for c in loads[k]:
            c.wait()
        for t in range(2):
            code = jnp.where(me == t, meta[2], meta[3])
            for p in range(pieces):
                wide[2 * k + t, p * step:(p + 1) * step, :] = placed(both.at[k, t], p, code, pieces).astype(F32)
            move.store(wide.at[2 * k + t], outs[2 * k + t])
    move.finish()


def finish_pair(meta, pieces, parts, d, after=()):
    pairs = parts[0].shape[1] // d
    return call(functools.partial(finish_pair_kernel, pieces), "finish_pair", (meta, *parts), "shhhh",
                [("h", S((d, d), F32))] * (2 * pairs), [VM((pairs, 2, d, d), BF), VM((2 * pairs, d, d), F32)], 4 + 6 * pairs, 0, 8 * MIB, None, after)


def bits_below(size):
    return [1 << i for i in range(size.bit_length() - 1)]


class Layout:
    def __init__(self, mesh):
        self.nb, self.nt = mesh.shape["batch"], mesh.shape["tp"]
        self.tp = [("tp", b) for b in reversed(bits_below(self.nt))]
        self.batch = [("batch", b) for b in bits_below(self.nb)[1:]]
        self.lanes = (self.tp + self.batch, self.batch[:1] + self.tp + self.batch[1:])

    def partner(self, device, level):
        b, t = divmod(device, self.nt)
        axis, bit = level
        return (b ^ bit) * self.nt + t if axis == "batch" else b * self.nt + (t ^ bit)

    def swap(self, value, level):
        pairs = []
        for device in range(self.nb * self.nt):
            core, to = device // self.nt % 2, device
            for one in level if isinstance(level, list) else [level]:
                to = self.partner(to, self.lanes[core][one] if isinstance(one, int) else one)
            pairs.append((device, to))
        return lax.ppermute(value, ("batch", "tp"), pairs)


CORE = ("batch", 1)


def code_of(levels, place):
    out = jnp.int32(0)
    for axis, bit in levels:
        out = out * 2 + (place[axis] // bit) % 2
    return out


def add(a, b):
    return (a.astype(F32) + b.astype(F32)).astype(BF)


def scatter_levels(levels, rows, least=48):
    n = 0
    while n < len(levels) and rows % 32 == 0 and rows // 2 >= least:
        rows //= 2
        n += 1
    return n


class Chain:
    def __init__(self, lay, steps):
        self.lay, self.steps, self.result = lay, steps, None
        self.go(next(steps))

    def go(self, requests):
        self.sent = [v for v, _ in requests]
        self.here = [self.lay.swap(v, level) for v, level in requests]

    def step(self):
        try:
            self.go(self.steps.send(self.here))
        except StopIteration as end:
            self.result, self.sent, self.here = end.value, [], []
        return self


def fence(arrays, *chains):
    chains = [c for c in chains if c.here]
    arrays, held = lax.optimization_barrier((arrays, [c.here for c in chains]))
    for chain, here in zip(chains, held):
        chain.here = here
        chain.step()
    return arrays


def sent(*chains):
    return tuple(v for c in chains for v in c.sent)


def halving(a, b, levels):
    for level in levels:
        n = a.shape[0] // 2
        kept = add(a[:n], b[:n])
        (b,) = yield [(add(a[n:], b[n:]), level)]
        a = kept
    return a, b


def quartering(a, b, high, low):
    n = a.shape[0] // 4
    parts = [add(a[i * n:(i + 1) * n], b[i * n:(i + 1) * n]) for i in range(4)]
    got = yield [(parts[1], [low]), (parts[2], [high]), (parts[3], [high, low])]
    return sum((g.astype(F32) for g in got), parts[0].astype(F32)).astype(BF)


def fourfold(held, high, low):
    got = yield [(held, [low]), (held, [high]), (held, [high, low])]
    return jnp.concatenate([held] + got, axis=0)


def doubling(held, levels):
    for level in levels:
        (got,) = yield [(held, level)]
        held = jnp.concatenate([held, got], axis=0)
    return held


def spread(held, level):
    other, mine = yield [(held, level), (held, CORE)]
    (rest,) = yield [(other, CORE)]
    return held, other, mine, rest


def reduce_ffn(lay, gone, stay, keep):
    m = len(lay.lanes[0])
    n = gone.shape[0]
    (recv,) = yield [(gone, CORE)]
    b, recv = yield [(add(keep[n:], recv), 0), (stay, CORE)]
    a, b = yield from halving(add(keep[:n], recv), b, range(1, m - 2))
    held = yield from quartering(a, b, m - 2, m - 1)
    held = yield from doubling(held, reversed(lay.batch[1:]))
    return (yield from spread(held, lay.batch[0]))


def reduce_pair(lay, n, send, keep, ahead):
    (recv,) = yield [(send, CORE)]
    if ahead:
        held = add(*(yield from halving(keep, recv, range(n))))
    else:
        a, b = yield from halving(keep, recv, range(n - 2))
        held = yield from quartering(a, b, n - 2, n - 1)
    for level in range(n, len(lay.lanes[0])):
        (got,) = yield [(held, level)]
        held = add(held, got)
    return held


def gather_pairs(lay, n, held):
    held = yield from fourfold(held, n - 2, n - 1)
    held = yield from doubling(held, reversed(range(1, n - 2)))
    return (yield from spread(held, 0))


def reduce_small(lay, vectors, hidden):
    n, shard = vectors.shape[0], hidden[0].shape[0]
    for level in lay.tp:
        bit = level[1]
        (got,) = yield [(jnp.concatenate([vectors] + [hidden[j + bit] for j in range(bit)]), level)]
        vectors = vectors + got[:n]
        hidden = [hidden[j] + got[n + j * shard:n + (j + 1) * shard] for j in range(bit)]
    held = jnp.concatenate([vectors, hidden[0]])
    for level in [CORE] + lay.batch[:-2]:
        (got,) = yield [(held, level)]
        held = held + got
    high, low = lay.batch[-2:]
    got = yield [(held, [low]), (held, [high]), (held, [high, low])]
    return held + got[0] + got[1] + got[2]


def on_device(
    lay,
    inputs,
    cotangent,
    zinc_lengths,
    pubchem_lengths,
    feature_stack,
    train_step,
    redraw_interval,
    attn_gain,
    attn_shift,
    query_weight,
    query_bias,
    key_weight,
    key_bias,
    value_weight,
    value_bias,
    output_weight,
    output_bias,
    ffn_gain,
    ffn_shift,
    hidden_weight,
    hidden_bias,
    return_weight,
    return_bias,
):
    nt = lay.nt
    d, shard = hidden_weight.shape
    rows = inputs.shape[0]
    width = min(768, shard)
    chunks = shard // width
    zm, pm = zinc_lengths.shape[0], pubchem_lengths.shape[0]
    place = {"batch": lax.axis_index("batch"), "tp": lax.axis_index("tp")}
    core = place["batch"] % 2

    def shares(k):
        hw = lax.dynamic_slice(hidden_weight, (core * (d // 2), k * width), (d // 2, width))
        rw = lax.dynamic_slice(return_weight, (k * width + core * (width // 2), 0), (width // 2, d))
        return [jnp.concatenate([hw, rw], axis=0)] if width == d else [hw, rw]

    def from_tp(own):
        pool = {0: own}
        for level in lay.tp:
            for j in list(pool):
                pool[j | level[1]] = [lay.swap(v, level) for v in pool[j]]
        return [v for j in range(1, nt) for v in pool[j]]

    own = [shares(k) for k in range(chunks)]
    per = len(own[0])
    biases = from_tp([hidden_bias])
    here = {k: from_tp(own[k]) for k in range(chunks)}

    n_pair = scatter_levels(lay.lanes[0], d)
    codes = [code_of(lane[:n_pair], place) for lane in lay.lanes]
    pick = train_step[0] // redraw_interval[0] % feature_stack.shape[0]
    meta = jnp.stack([core, code_of(lay.batch, place), jnp.where(core == 0, codes[0], codes[1]), jnp.where(core == 0, codes[1], codes[0]),
                      code_of(lay.batch[:-2], place) * 4, pick]).astype(jnp.int32)
    table = rotary_const()

    out = attend_fwd(
        meta, zinc_lengths, pubchem_lengths, cotangent, inputs,
        (attn_gain, attn_shift, query_bias, key_bias, value_bias, output_bias, ffn_gain, ffn_shift),
        query_weight, key_weight, value_weight, output_weight, feature_stack, table)
    out, here[0], biases = lax.optimization_barrier((out, here[0], biases))
    qkv, f, state, trans, middle, n2, left, proj = out

    pieces, pair_pieces = 2 ** len(lay.batch), 2 ** n_pair
    chains, acts, rws, hidden, before = [], [], [], [], ()
    for k in range(chunks):
        if chains:
            here[k] = fence(here[k], chains[-1])
        near = [lay.swap(v, CORE) for v in here[k]]
        parts = [[v[i] for i in range(j * per, (j + 1) * per) for v in (here[k], near)] for j in range(nt - 1)]
        out = ffn_chunk(meta, pieces, nt, n2, left, cotangent, hidden_bias, hidden_weight, return_weight, parts, biases, k, width,
                        before, sent(*chains))
        gone, stay, keep, act, bias, e, rw = fence(out, *chains)
        before = (e,)
        chains.append(Chain(lay, reduce_ffn(lay, gone, stay, keep)))
        acts.append(act)
        rws.append(rw)
        hidden.append(bias)

    middle = fence(middle, chains[-1])
    out = mid(e, cotangent, middle, output_weight, ffn_gain, sent(*chains))
    gm, gb, gatt, vec1 = fence(out, *chains[:-1])
    out = value_bwd(meta, zm, pm, pair_pieces, gatt, gb, f, state, trans, sent(*chains))
    send, keep, gv, uw, gst, vec2 = fence(out, *chains)
    pair_a = Chain(lay, reduce_pair(lay, n_pair, send, keep, True))
    uw = fence(uw, pair_a)
    out = query_bwd(meta, zm, pm, pair_pieces, uw, gst, qkv, f, state, trans, proj, table, sent(pair_a, *chains))
    send, keep, gqk, vec3 = fence(out, pair_a, *chains)
    pair_b = Chain(lay, reduce_pair(lay, n_pair, send, keep, False))
    gqk = fence(gqk, pair_b)
    out = input_back(gqk, gv, query_weight, key_weight, value_weight, inputs, gm, attn_gain, sent(pair_a, pair_b, *chains))
    (input_grad, vec4), middle = fence((out, middle), pair_a, pair_b, *chains)
    layer_out = layer_end(acts, rws, middle, return_bias, sent(pair_b, pair_a, *chains))
    layer_out, vec4 = fence((layer_out, vec4), pair_b, pair_a, *chains)
    vec3 = jnp.concatenate([vec3, vec4], axis=0)
    vectors = jnp.concatenate([vec1, vec2, vec3], axis=0).reshape(-1)
    small = Chain(lay, reduce_small(lay, vectors, [jnp.concatenate([hidden[k][j] for k in range(chunks)]) for j in range(nt)]))

    ffn_out, k, pairs = (), 0, None
    while pairs is None or pairs.here or any(c.here for c in chains):
        every = [pairs] if pairs else [pair_b, pair_a]
        every += chains + [small]
        if k < chunks and chains[k].result is not None:
            ffn_out = finish_ffn(meta, pieces, chains[k].result, k, shard, ffn_out, sent(*every))
            k += 1
            ffn_out = fence(ffn_out, *every)
        else:
            fence((), *every)
        if pairs is None and pair_a.result is not None and pair_b.result is not None:
            pairs = Chain(lay, gather_pairs(lay, n_pair, jnp.concatenate([pair_a.result, pair_b.result], axis=1)))
    while k < chunks:
        ffn_out = finish_ffn(meta, pieces, chains[k].result, k, shard, ffn_out, sent(small))
        k += 1
    while small.here:
        small.step()
    gwo, gwv, gwq, gwk = finish_pair(meta, pair_pieces, pairs.result, d, (small.result,))
    vecs = small.result[:9 * d].reshape(9, d)
    return (layer_out, input_grad, vecs[7], vecs[8], gwq, vecs[5], gwk, vecs[6], gwv, vecs[4], gwo, vecs[2],
            vecs[0], vecs[1], ffn_out[0], small.result[9 * d:], ffn_out[1], vecs[3])


def solution(mesh):
    rows, whole, hidden = P(("batch", "tp"), None), P(), P(None, "tp")
    return jax.shard_map(
        functools.partial(on_device, Layout(mesh)),
        mesh=mesh,
        in_specs=(rows, rows, P(("batch", "tp")), P(("batch", "tp"))) + (whole,) * 15 + (hidden, P("tp"), P("tp", None), whole),
        out_specs=(rows, rows) + (whole,) * 12 + (hidden, P("tp"), P("tp", None), whole),
        check_vma=False,
    )
```

```python
import functools
import math

import jax
import jax.numpy as jnp
import numpy as np
from jax import lax
from jax.experimental import pallas as pl
from jax.experimental.pallas import tpu as pltpu
from jax.sharding import PartitionSpec as P

ZPAD = 64
PPAD = 256
F32 = jnp.float32
BF = jnp.bfloat16
VM = pltpu.VMEM
GROUP = 4
S = jax.ShapeDtypeStruct
TIMES = {"attend_fwd": 24, "ffn_chunk": 17, "layer_end": 9, "mid": 8, "value_bwd": 13, "query_bwd": 13, "input_back": 10, "finish_ffn": 5, "finish_pair": 5}
MIB = 2**20
GRANT = 48


def dot(a, b):
    return jnp.dot(a, b, preferred_element_type=F32)


def dot_t(a, b):
    return lax.dot_general(a, b, (((1,), (1,)), ((), ())), preferred_element_type=F32)


def dot_c(a, b):
    return lax.dot_general(a, b, (((0,), (0,)), ((), ())), preferred_element_type=F32)


def split(v):
    hi = v.astype(BF)
    return hi, (v - hi.astype(F32)).astype(BF)


def norm_parts(values):
    center = values - jnp.mean(values, axis=-1, keepdims=True)
    rate = lax.rsqrt(jnp.mean(center * center, axis=-1, keepdims=True) + 1e-05)
    return center * rate, rate


def row(ref):
    return ref[...].reshape(1, -1)


def block_mask(width):
    f = lax.broadcasted_iota(jnp.int32, (128, width), 0) // 32
    c = lax.broadcasted_iota(jnp.int32, (128, width), 1) % 256 // 64
    return f == c


def molecules(zm, pm):
    return [(i * ZPAD, ZPAD) for i in range(zm)] + [(zm * ZPAD + i * PPAD, PPAD) for i in range(pm)]


def members(mols, b):
    return [(i, r, n) for i, (r, n) in enumerate(mols) if b * PPAD <= r < (b + 1) * PPAD]


class Mover:
    def __init__(self, sems):
        self.sems, self.n, self.out = sems, 0, []

    def load(self, src, dst):
        copy = pltpu.make_async_copy(src, dst, self.sems.at[self.n])
        self.n += 1
        copy.start()
        return copy

    def store(self, src, dst):
        self.out.append(self.load(src, dst))

    def finish(self):
        for copy in self.out:
            copy.wait()


def call(kernel, name, args, spaces, outs, scratch, copies, flops, moved, aliases=None, after=()):
    n, extra = len(args), len(after)

    def body(*refs):
        kernel(*refs[:n], *refs[n + extra:])

    spec = {
        "v": pl.BlockSpec(memory_space=VM),
        "h": pl.BlockSpec(memory_space=pltpu.HBM),
        "s": pl.BlockSpec(memory_space=pltpu.SMEM),
    }
    return pl.pallas_call(
        body,
        out_shape=tuple(o for _, o in outs),
        in_specs=[spec[s] for s in spaces] + [spec["h"]] * extra,
        out_specs=tuple(spec[s] for s, _ in outs),
        scratch_shapes=list(scratch) + [pltpu.SemaphoreType.DMA((copies,))],
        input_output_aliases=aliases or {},
        compiler_params=pltpu.CompilerParams(vmem_limit_bytes=GRANT * MIB),
        cost_estimate=pl.CostEstimate(flops=int(TIMES[name] * 1.15e9), bytes_accessed=moved, transcendentals=0),
        name=name,
    )(*args, *after)


def place_heads(scaled):
    two = jnp.concatenate([scaled, scaled], axis=1)
    return jnp.where(block_mask(256), jnp.concatenate([two, two], axis=1), 0.0)


def attend_fwd_kernel(zm, pm, meta, zlen, plen, cot_h, x_h, gain_h, shift_h, bq_h, bk_h, bv_h, bo_h, gain2_h, shift2_h,
                      wq_h, wk_h, wv_h, wo_h, stack_h, table_h, energy_h,
                      qkv_h, f_h, state_h, trans_h, middle_h, n2_h, left_h, proj_h,
                      cot, n2_s, left, x, vec, wq, wk, wv, wo, fp, proj, table, energy, qkv, f_s, state_s, trans, middle_s, att_s, sems):
    move = Mover(sems)
    rows, d = x.shape
    first = [move.load(x_h, x), move.load(gain_h, vec.at[0]), move.load(shift_h, vec.at[1]), move.load(stack_h.at[meta[5]], fp),
             move.load(cot_h, cot)]
    later = [move.load(s, t) for s, t in ((wq_h, wq), (bq_h, vec.at[2]), (table_h, table), (energy_h, energy), (wk_h, wk),
                                          (bk_h, vec.at[3]), (wv_h, wv), (bv_h, vec.at[4]))]
    last = [move.load(s, t) for s, t in ((wo_h, wo), (bo_h, vec.at[5]), (gain2_h, vec.at[6]), (shift2_h, vec.at[7]))]
    mols = molecules(zm, pm)
    groups = d // 256
    blocks = range(rows // PPAD)
    keep = block_mask(512)
    ones = jnp.ones((PPAD, 256), BF)

    def vector(i):
        return vec[i].reshape(1, -1)

    for c in first:
        c.wait()
    for g in range(groups):
        p = fp[g * GROUP:(g + 1) * GROUP].reshape(GROUP * 32, 64) * 64 ** -0.25
        turned = jnp.concatenate([p[:, 32:], -p[:, :32]], axis=1)
        hi, lo = split(jnp.concatenate([place_heads(p), place_heads(turned)], axis=1))
        proj[0, g] = hi
        proj[1, g] = lo
    n1s = {}
    for b in blocks:
        rs = slice(b * PPAD, (b + 1) * PPAD)
        normed, _ = norm_parts(x[rs, :].astype(F32))
        n1s[b] = (normed * vector(0) + vector(1)).astype(BF)
        trans[1, :, rs] = n1s[b].T
        left[1, :, rs] = cot[rs, :].T
    for c in later:
        c.wait()
    move.store(proj.at[0], proj_h)
    move.store(trans.at[1], trans_h.at[1])
    move.store(left.at[1], left_h.at[1])
    for b in blocks:
        mem = members(mols, b)
        rs = slice(b * PPAD, (b + 1) * PPAD)
        n1 = n1s[b]
        cosb, sinb = (jnp.concatenate([table[t, :n, :] for _, _, n in mem], axis=0) for t in range(2))
        cosb = jnp.concatenate([cosb, cosb], axis=1)
        sinb = jnp.concatenate([sinb, sinb], axis=1)
        live = jnp.concatenate(
            [(lax.broadcasted_iota(jnp.int32, (n, 128), 0) < (zlen[i] if i < zm else plen[i - zm])).astype(F32) for i, r, n in mem], axis=0)
        for g in range(groups):
            cs = slice(g * 256, (g + 1) * 256)
            fs = slice(g * 128, (g + 1) * 128)

            def features(w, bias, slot):
                v = dot(n1, w[:, cs]) + vector(bias)[:, cs]
                qkv[slot, rs, cs] = v.astype(BF)
                ch, cl = split(v * cosb)
                sh, sl = split(v * sinb)
                eh, el = split(v * v)
                ph, plo = proj[0, g], proj[1, g]
                e = energy[...]
                inner = (dot_t(ch, ph[:, :256]) + dot_t(sh, ph[:, 256:]) + dot_t(cl, ph[:, :256]) + dot_t(sl, ph[:, 256:])
                         + dot_t(ch, plo[:, :256]) + dot_t(sh, plo[:, 256:]) - dot_t(eh, e) - dot_t(el, e))
                return jnp.exp(inner) * (32 ** -0.5)

            fq = features(wq, 2, 0).astype(BF)
            fk = (features(wk, 3, 1) * live).astype(BF)
            f_s[0, rs, fs] = fq
            f_s[1, rs, fs] = fk
            v = (dot(n1, wv[:, cs]) + vector(4)[:, cs]).astype(BF)
            qkv[2, rs, cs] = v
            for i, r, n in mem:
                ms = slice(r - b * PPAD, r - b * PPAD + n)
                vo = jnp.concatenate([v[ms], ones[:n]], axis=1)
                state = jnp.where(keep, dot_c(fk[ms], vo), 0.0).astype(BF)
                state_s[i, g] = state
                nd = dot(fq[ms], state)
                att_s[r:r + n, cs] = (nd[:, :256] / nd[:, 256:]).astype(BF)
    for s, t in ((qkv, qkv_h), (f_s, f_h), (state_s, state_h)):
        move.store(s, t)
    for c in last:
        c.wait()
    for b in blocks:
        rs = slice(b * PPAD, (b + 1) * PPAD)
        trans[0, :, rs] = att_s[rs, :].T
        middle = x[rs, :].astype(F32) + (dot(att_s[rs, :], wo[...]) + vector(5))
        middle_s[rs, :] = middle
        normed, _ = norm_parts(middle)
        n2 = (normed * vector(6) + vector(7)).astype(BF)
        n2_s[rs, :] = n2
        left[0, :, rs] = n2.T
    move.store(middle_s, middle_h)
    move.store(n2_s, n2_h)
    move.store(trans.at[0], trans_h.at[0])
    move.store(left.at[0], left_h.at[0])
    move.finish()


def rotary_const():
    place = np.arange(PPAD, dtype=np.float64)
    rates = np.exp(np.arange(32, dtype=np.float64) * (-2.0 * math.log(10000.0) / 64))
    ang = place[:, None] * rates[None, :]
    return np.tile(np.stack([np.cos(ang), np.sin(ang)]), (1, 1, 4)).astype(np.float32)


def head_const(scale):
    f = np.arange(128)[:, None] // 32
    c = np.arange(256)[None, :] // 64
    return ((f == c) * scale).astype(jnp.bfloat16)


def attend_fwd(meta, zlen, plen, cot, x, vectors, wq, wk, wv, wo, stack, table):
    rows, d = x.shape
    zm, pm = zlen.shape[0], plen.shape[0]
    groups = d // 256
    states = (zm + pm, groups, 128, 512)
    outs = [S((3, rows, d), BF), S((2, rows, d // 2), BF), S(states, BF), S((2, d, rows), BF),
            S((rows, d), F32), S((rows, d), BF), S((2, d, rows), BF), S((groups, 128, 512), BF)]
    args = (meta, zlen, plen, cot, x, *vectors, wq, wk, wv, wo, stack, table, head_const(1 / 16))
    scratch = ([VM((rows, d), BF)] * 2 + [VM((2, d, rows), BF), VM((rows, d), BF), VM((8, d), F32)] + [VM((d, d), BF)] * 4
               + [VM(stack.shape[1:], F32), VM((2, groups, 128, 512), BF), VM(table.shape, F32), VM((128, 256), BF)]
               + [VM((3, rows, d), BF), VM((2, rows, d // 2), BF), VM(states, BF), VM((2, d, rows), BF), VM((rows, d), F32), VM((rows, d), BF)])
    return call(
        functools.partial(attend_fwd_kernel, zm, pm), "attend_fwd", args, "sss" + "h" * (len(args) - 3),
        [("h", o) for o in outs], scratch, 32, 2 * rows * d * d * 4, 16 * MIB)


def gelu_parts(h):
    bell = jnp.exp(h * h * -0.5)
    t = 1.0 / (1.0 + (0.3275911 * math.sqrt(0.5)) * jnp.abs(h))
    poly = t * (0.127414796 + t * (-0.142248368 + t * (0.7107068705 + t * (-0.7265760135 + t * 0.5307027145))))
    tail = poly * bell
    phi = jnp.where(h >= 0, 1.0 - tail, tail)
    return h * phi, phi + h * bell * (1.0 / math.sqrt(2 * math.pi))


def place_pieces(code, src, dst):
    n, step = src.shape[0], src.shape[1]
    for p in range(n):
        off = pl.multiple_of(jnp.bitwise_xor(p, code) * step, 16)
        dst[pl.ds(off, step), :] = src[p]


def ffn_kernel(pieces, shards, k, per, meta, n2_h, left_h, cot_h, hb_h, hw_h, rw_h, *refs):
    parts = {j: refs[(j - 1) * per:j * per] for j in range(1, shards)}
    hbs = refs[(shards - 1) * per:(shards - 1) * (per + 1)]
    e_prev = refs[(shards - 1) * (per + 1)] if k else None
    (gone_h, stay_h, keep_h, act_h, bias_o, e_h, rws_h, n2, left, cot, hb, hw, rw, hw2, rw2, right, stage, e_s, sems) = refs[-19:]
    move = Mover(sems)
    d, width = hw.shape[1:]
    half_d = d // 2
    me, code = meta[0], meta[1]
    order = list(range(1, shards)) + [0]
    early, late = {}, {}
    for j in order:
        early[j] = [move.load(hbs[j - 1] if j else hb_h, hb.at[j])]
        if j == order[0]:
            early[j].append(move.load(n2_h, n2))
        late[j] = []
        if j == 0:
            early[j].append(move.load(hw_h.at[:, k * width:(k + 1) * width], hw.at[0]))
            late[j].append(move.load(rw_h.at[k * width:(k + 1) * width, :], rw.at[0]))
        elif per == 2:
            early[j] += [move.load(parts[j][p].at[:half_d], hw2.at[j - 1, p]) for p in range(2)]
            late[j] += [move.load(parts[j][p].at[half_d:], rw2.at[j - 1, p]) for p in range(2)]
        else:
            early[j] += [move.load(parts[j][p], hw2.at[j - 1, p]) for p in range(2)]
            late[j] += [move.load(parts[j][2 + p], rw2.at[j - 1, p]) for p in range(2)]
        if j == order[0]:
            late[j].append(move.load(cot_h, cot))
    last = [move.load(left_h, left)]
    if k:
        last.append(move.load(e_prev, e_s))
    step, half = d // pieces, pieces // 2
    tile = width
    for j in order:
        for c in early[j] + late[j]:
            c.wait()
        if j:
            place_pieces(me, hw2.at[j - 1], hw.at[j])
            place_pieces(me, rw2.at[j - 1], rw.at[j])
        bias = hb[j].reshape(1, -1)[:, k * width:(k + 1) * width].astype(F32)
        for c in range(0, width, tile):
            cs = slice(c, c + tile)
            h = dot(n2[...], hw[j, :, cs]) + bias[:, cs]
            act, slope = gelu_parts(h)
            ga = dot_t(cot[...], rw[j, cs, :])
            gh = (ga * slope).astype(BF)
            right[0, j, :, cs] = gh
            right[1, j, :, cs] = act.astype(BF)
            bias_o[j:j + 1, cs] = jnp.sum(gh.astype(F32), axis=0, keepdims=True)
        move.store(right.at[1, j], act_h.at[j])
        move.store(rw.at[j], rws_h.at[j])
    for c in last:
        c.wait()
    for c in range(0, d, 768):
        cs = slice(c, c + 768)
        part = sum(dot_t(right[0, j], hw[j, cs, :]) for j in order)
        e_s[:, cs] = e_s[:, cs] + part if k else part
    move.store(e_s, e_h)
    for kind, slot in ((1 - me, 0), (me, 1)):
        for j in order:
            for c in range(0, width, tile):
                cs = slice(c, c + tile)
                value = dot(left[kind], right[kind, j, :, cs]).astype(BF)
                for p in range(pieces):
                    rel = jnp.bitwise_xor(p, code)
                    second = rel // half * (shards * half) + j * half + rel % half
                    off = pl.multiple_of(jnp.where(kind == 0, j * pieces + rel, second) * step, 16)
                    stage[slot, pl.ds(off, step), cs] = value[p * step:(p + 1) * step]
        if slot:
            move.store(stage.at[1], keep_h)
        else:
            cut = shards * d // 2
            move.store(stage.at[0, cut:], gone_h)
            move.store(stage.at[0, :cut], stay_h)
    move.finish()


def ffn_chunk(meta, pieces, shards, n2, left, cot, hb, hw, rw, parts, hbs, k, width, before, after=()):
    rows, d = n2.shape
    per = len(parts[0])
    part = S((shards * d // 2, width), BF)
    outs = [("h", part), ("h", part), ("h", S((shards * d, width), BF)), ("h", S((shards, rows, width), BF)), ("v", S((shards, width), F32)),
            ("h", S((rows, d), F32)), ("h", S((shards, width, d), BF))]
    scratch = [VM((rows, d), BF), VM((2, d, rows), BF), VM((rows, d), BF), VM((shards, 1) + hb.shape, BF), VM((shards, d, width), BF),
               VM((shards, width, d), BF), VM((shards - 1, 2, d // 2, width), BF), VM((shards - 1, 2, width // 2, d), BF),
               VM((2, shards, rows, width), BF), VM((2, shards * d, width), BF), VM((rows, d), F32)]
    args = (meta, n2, left, cot, hb.reshape(1, -1), hw, rw) + tuple(p for part in parts for p in part) + tuple(b.reshape(1, -1) for b in hbs) + tuple(before)
    return call(
        functools.partial(ffn_kernel, pieces, shards, k, per), "ffn_chunk", args,
        "s" + "h" * (len(args) - 1), outs, scratch, 12 + 13 * shards, 2 * rows * d * width * 5 * shards, 12 * MIB, None, after)


def products(move, pieces, codes, stage, outs):
    for slot, (left, right, out) in enumerate(outs):
        d = out.shape[0]
        step = d // pieces
        for c in range(0, d, 768):
            cs = slice(c, c + 768)
            value = dot(left[...], right[:, cs]).astype(BF)
            for p in range(pieces):
                off = pl.multiple_of(jnp.bitwise_xor(p, codes[slot]) * step, 16)
                stage[slot, pl.ds(off, step), cs] = value[p * step:(p + 1) * step]
        move.store(stage.at[slot], out)


def mid_kernel(e_h, cot_h, middle_h, wo_h, vec_h, gm_h, gb_h, gatt_h, vec_o, e_s, cot, middle, wo, vec, gm_s, gb_s, gatt, sems):
    move = Mover(sems)
    rows, d = middle.shape
    loads = [[move.load(s.at[r:r + 256], t.at[r:r + 256]) for s, t in ((middle_h, middle), (e_h, e_s), (cot_h, cot))]
             for r in range(0, rows, 256)]
    gain = move.load(vec_h, vec)
    last = move.load(wo_h, wo)
    gain.wait()
    gain2 = row(vec)
    acc_g = acc_s = acc_b = acc_c = 0.0
    for i, r in enumerate(range(0, rows, 256)):
        for c in loads[i]:
            c.wait()
        rs = slice(r, r + 256)
        e = e_s[rs, :]
        n, rate = norm_parts(middle[rs, :])
        c = cot[rs, :].astype(F32)
        acc_g += jnp.sum(e * n, axis=0, keepdims=True)
        acc_s += jnp.sum(e, axis=0, keepdims=True)
        acc_c += jnp.sum(c, axis=0, keepdims=True)
        eg = e * gain2
        gm = c + rate * (eg - jnp.mean(eg, axis=-1, keepdims=True) - n * jnp.mean(eg * n, axis=-1, keepdims=True))
        gm_s[rs, :] = gm
        gb = gm.astype(BF)
        gb_s[rs, :] = gb
        acc_b += jnp.sum(gb.astype(F32), axis=0, keepdims=True)
    for i, acc in enumerate((acc_g, acc_s, acc_b, acc_c)):
        vec_o[i:i + 1, :] = acc
    move.store(gm_s, gm_h)
    move.store(gb_s, gb_h)
    last.wait()
    for c in range(0, d, 768):
        cs = slice(c, c + 768)
        gatt[:, cs] = dot_t(gb_s[...], wo[cs, :]).astype(BF)
    move.store(gatt, gatt_h)
    move.finish()


def mid(e, cot, middle, wo, gain2, after=()):
    rows, d = middle.shape
    outs = [("h", S((rows, d), F32)), ("h", S((rows, d), BF)), ("h", S((rows, d), BF)), ("v", S((4, d), F32))]
    scratch = [VM((rows, d), F32), VM((rows, d), BF), VM((rows, d), F32), VM((d, d), BF), VM(gain2.shape, F32), VM((rows, d), F32),
               VM((rows, d), BF), VM((rows, d), BF)]
    args = (e, cot, middle, wo, gain2)
    return call(mid_kernel, "mid", args, "h" * len(args), outs, scratch, 8 + 3 * (rows // 256), 2 * rows * d * d, 8 * MIB, None, after)


def value_bwd_kernel(zm, pm, pieces, meta, gatt_h, gb_h, f_h, state_h, trans_h,
                     send_h, keep_h, gv_h, uw_h, gst_h, vec_o, gatt, uw_o, gst_o, f, state, left, right, stage, sems):
    move = Mover(sems)
    mols = molecules(zm, pm)
    rows, d = gatt.shape
    groups = d // 256
    loads = []
    for g in range(groups):
        cs, fs = slice(g * 256, (g + 1) * 256), slice(g * 128, (g + 1) * 128)
        loads.append([move.load(f_h.at[:, :, fs], f.at[:, :, fs]), move.load(state_h.at[:, g], state.at[:, g]),
                      move.load(gatt_h.at[:, cs], gatt.at[:, cs])])
    last = [move.load(trans_h, left), move.load(gb_h, right.at[0])]
    keep = block_mask(512)
    for g in range(groups):
        for c in loads[g]:
            c.wait()
        cs = slice(g * 256, (g + 1) * 256)
        fs = slice(g * 128, (g + 1) * 128)
        total = 0.0
        for i, (r, n) in enumerate(mols):
            ms = slice(r, r + n)
            st = state[i, g]
            q = f[0, ms, fs]
            nd = dot(q, st)
            rden = 1.0 / nd[:, 256:]
            u = gatt[ms, cs].astype(F32) * rden
            uw = jnp.concatenate([u, -(u * (nd[:, :256] * rden))], axis=1).astype(BF)
            uw_o[ms, slice(g * 512, (g + 1) * 512)] = uw
            gst = jnp.where(keep, dot_c(q, uw), 0.0).astype(BF)
            gst_o[i, g] = gst
            gv = dot(f[1, ms, fs], gst[:, :256]).astype(BF)
            right[1, ms, cs] = gv
            total += jnp.sum(gv.astype(F32), axis=0, keepdims=True)
        vec_o[0:1, cs] = total
    move.store(right.at[1], gv_h)
    move.store(uw_o, uw_h)
    move.store(gst_o, gst_h)
    for c in last:
        c.wait()
    me = meta[0]
    products(move, pieces, (meta[3], meta[2]), stage, ((left.at[1 - me], right.at[1 - me], send_h), (left.at[me], right.at[me], keep_h)))
    move.finish()


def value_bwd(meta, zm, pm, pieces, gatt, gb, f, state, trans, after=()):
    rows, d = gatt.shape
    outs = [("h", S((d, d), BF))] * 2 + [("h", S((rows, d), BF)), ("h", S((rows, 2 * d), BF)), ("h", S(state.shape, BF)), ("v", S((1, d), F32))]
    scratch = [VM((rows, d), BF), VM((rows, 2 * d), BF), VM(state.shape, BF), VM(f.shape, BF), VM(state.shape, BF), VM((2, d, rows), BF),
               VM((2, rows, d), BF), VM((2, d, d), BF)]
    args = (meta, gatt, gb, f, state, trans)
    return call(functools.partial(value_bwd_kernel, zm, pm, pieces), "value_bwd", args, "shhhhh", outs, scratch,
                10 + 3 * d // 256, 2 * d**3 * 3, 8 * MIB, None, after)


def query_bwd_kernel(zm, pm, pieces, meta, uw_h, gst_h, qkv_h, f_h, state_h, trans_h, proj_h, energy_h, table_h,
                     send_h, keep_h, gqk_h, vec_o, uw, gst, qkv, f, state, n1t, proj, energy, table, gqk, stage, sems):
    move = Mover(sems)
    mols = molecules(zm, pm)
    _, rows, d = qkv.shape
    loads = [[move.load(s, t) for s, t in ((proj_h, proj), (energy_h, energy), (table_h, table))]]
    for g in range(d // 256):
        cs, fs, us = slice(g * 256, (g + 1) * 256), slice(g * 128, (g + 1) * 128), slice(g * 512, (g + 1) * 512)
        if g:
            loads.append([])
        loads[g] += [move.load(uw_h.at[:, us], uw.at[:, us]), move.load(state_h.at[:, g], state.at[:, g]),
                     move.load(f_h.at[:, :, fs], f.at[:, :, fs]), move.load(gst_h.at[:, g], gst.at[:, g]),
                     move.load(qkv_h.at[:, :, cs], qkv.at[:, :, cs])]
    later = [move.load(trans_h.at[1], n1t)]
    for g in range(d // 256):
        for c in loads[g]:
            c.wait()
        cs = slice(g * 256, (g + 1) * 256)
        fs = slice(g * 128, (g + 1) * 128)
        sums = [0.0, 0.0]
        for b in range(rows // PPAD):
            mem = members(mols, b)
            rs = slice(b * PPAD, (b + 1) * PPAD)
            gfq, gfk = [], []
            for i, r, n in mem:
                ms = slice(r, r + n)
                gfq.append(dot_t(uw[ms, slice(g * 512, (g + 1) * 512)], state[i, g]))
                gfk.append(dot_t(jnp.concatenate([qkv[2, ms, cs], jnp.ones((n, 256), BF)], axis=1), gst[i, g]))
            cosb, sinb = (jnp.concatenate([table[t, :n, :] for _, _, n in mem], axis=0) for t in range(2))
            cosb = jnp.concatenate([cosb, cosb], axis=1)
            sinb = jnp.concatenate([sinb, sinb], axis=1)
            for t, gf in enumerate((gfq, gfk)):
                gp = (jnp.concatenate(gf, axis=0) * f[t, rs, fs].astype(F32)).astype(BF)
                back = dot(gp, proj[g])
                tot = dot(gp, energy[...])
                grad = (cosb * back[:, :256] + sinb * back[:, 256:] - tot * qkv[t, rs, cs].astype(F32)).astype(BF)
                gqk[t, rs, cs] = grad
                sums[t] += jnp.sum(grad.astype(F32), axis=0, keepdims=True)
        for t in range(2):
            vec_o[t:t + 1, cs] = sums[t]
    for c in later:
        c.wait()
    me = meta[0]
    products(move, pieces, (meta[3], meta[2]), stage, ((n1t, gqk.at[1 - me], send_h), (n1t, gqk.at[me], keep_h)))
    move.store(gqk, gqk_h)
    move.finish()


def query_bwd(meta, zm, pm, pieces, uw, gst, qkv, f, state, trans, proj, table, after=()):
    _, rows, d = qkv.shape
    outs = [("h", S((d, d), BF))] * 2 + [("h", S((2, rows, d), BF)), ("v", S((2, d), F32))]
    scratch = [VM(uw.shape, BF), VM(gst.shape, BF), VM(qkv.shape, BF), VM(f.shape, BF), VM(state.shape, BF), VM((d, rows), BF),
               VM(proj.shape, BF), VM((128, 256), BF), VM(table.shape, F32), VM((2, rows, d), BF), VM((2, d, d), BF)]
    args = (meta, uw, gst, qkv, f, state, trans, proj, head_const(64 ** -0.5), table)
    return call(functools.partial(query_bwd_kernel, zm, pm, pieces), "query_bwd", args, "s" + "h" * (len(args) - 1), outs, scratch,
                8 + 5 * d // 256, 2 * d**3 * 6, 12 * MIB, None, after)


def input_kernel(gqk_h, gv_h, wq_h, wk_h, wv_h, x_h, gm_h, gain_h, out_h, vec_o, gqk, gv, wq, wk, wv, x, gm, vec, e_s, out_s, sems):
    move = Mover(sems)
    rows, d = x.shape
    loads = [(move.load(gqk_h.at[0], gqk.at[0]), move.load(wq_h, wq)), (move.load(gqk_h.at[1], gqk.at[1]), move.load(wk_h, wk)),
             (move.load(gv_h, gv), move.load(wv_h, wv))]
    last = [move.load(s, t) for s, t in ((x_h, x), (gm_h, gm), (gain_h, vec))]
    for (left, right), load in zip(((gqk.at[0], wq), (gqk.at[1], wk), (gv, wv)), loads):
        for c in load:
            c.wait()
        for c in range(0, d, 768):
            cs = slice(c, c + 768)
            part = dot_t(left[...], right[cs, :])
            e_s[:, cs] = part if right is wq else e_s[:, cs] + part
    for c in last:
        c.wait()
    gain = row(vec)
    acc_g = acc_s = 0.0
    for r in range(0, rows, 256):
        rs = slice(r, r + 256)
        e = e_s[rs, :]
        n, rate = norm_parts(x[rs, :].astype(F32))
        acc_g += jnp.sum(e * n, axis=0, keepdims=True)
        acc_s += jnp.sum(e, axis=0, keepdims=True)
        eg = e * gain
        gx = rate * (eg - jnp.mean(eg, axis=-1, keepdims=True) - n * jnp.mean(eg * n, axis=-1, keepdims=True))
        out_s[rs, :] = (gm[rs, :] + gx).astype(BF)
    move.store(out_s, out_h)
    vec_o[0:1, :] = acc_g
    vec_o[1:2, :] = acc_s
    move.finish()


def input_back(gqk, gv, wq, wk, wv, x, gm, gain, after=()):
    rows, d = x.shape
    scratch = [VM(gqk.shape, BF), VM(gv.shape, BF)] + [VM((d, d), BF)] * 3 + [
        VM((rows, d), BF), VM((rows, d), F32), VM(gain.shape, F32), VM((rows, d), F32), VM((rows, d), BF)]
    args = (gqk, gv, wq, wk, wv, x, gm, gain)
    return call(input_kernel, "input_back", args, "h" * len(args), [("h", S((rows, d), BF)), ("v", S((2, d), F32))], scratch,
                16, 2 * d**3 * 3, 8 * MIB, None, after)


def layer_kernel(chunks, middle_h, vec_h, *refs):
    rights_h, rws_h = refs[:chunks], refs[chunks:2 * chunks]
    out_h, acts, rws, middle, vec, out_s, sems = refs[2 * chunks:]
    move = Mover(sems)
    base = [move.load(middle_h, middle), move.load(vec_h, vec)]
    loads = [[move.load(rights_h[k], acts.at[k]), move.load(rws_h[k], rws.at[k])] for k in range(chunks)]
    d = middle.shape[1]
    for c in base:
        c.wait()
    for k, load in enumerate(loads):
        for c in load:
            c.wait()
        for c in range(0, d, 768):
            cs = slice(c, c + 768)
            total = middle[:, cs] + sum(dot(acts[k, j], rws[k, j, :, cs]) for j in range(acts.shape[1]))
            if k + 1 < chunks:
                middle[:, cs] = total
            else:
                out_s[:, cs] = (total + row(vec)[:, cs]).astype(BF)
    move.store(out_s, out_h)
    move.finish()


def layer_end(rights, rws, middle, vec, after=()):
    rows, d = middle.shape
    k = len(rights)
    shards, _, width = rights[0].shape
    scratch = [VM((k, shards, rows, width), BF), VM((k, shards, width, d), BF), VM((rows, d), F32), VM(vec.shape, F32), VM((rows, d), BF)]
    args = (middle, vec, *rights, *rws)
    return call(functools.partial(layer_kernel, k), "layer_end", args, "h" * len(args),
                [("h", S((rows, d), BF))], scratch, 4 + 2 * k, 2 * rows * d * k * shards * width, 12 * MIB, None, after)[0]


def placed(ref, p, code, pieces):
    step = ref.shape[0] // pieces
    return ref[pl.ds(pl.multiple_of(jnp.bitwise_xor(p, code) * step, 16), step), :]


def load_halves(move, m0, m1, t0, t1, cols, both, me):
    half = m0.shape[0]
    return [move.load(m0.at[:, cols], both.at[me, :half]), move.load(m1.at[:, cols], both.at[me, half:]),
            move.load(t0.at[:, cols], both.at[1 - me, :half]), move.load(t1.at[:, cols], both.at[1 - me, half:])]


def finish_ffn_kernel(pieces, k, meta, m0, m1, t0, t1, *refs):
    ghw_h, grw_h, both, whole, wide, tall, sems = refs[-7:]
    move = Mover(sems)
    me, code = meta[0], meta[1]
    d, width = wide.shape
    for c in load_halves(move, m0, m1, t0, t1, slice(0, width), both, me):
        c.wait()
    step = d // pieces
    for p in range(pieces):
        wide[p * step:(p + 1) * step, :] = placed(both.at[0], p, code, pieces).astype(F32)
    move.store(wide, ghw_h.at[:, k * width:(k + 1) * width])
    for p in range(pieces):
        whole[p * step:(p + 1) * step, :] = placed(both.at[1], p, code, pieces)
    for c in range(0, width, 128):
        cs = slice(c, c + 128)
        tall[cs, :] = whole[:, cs].T.astype(F32)
    move.store(tall, grw_h.at[k * width:(k + 1) * width])
    move.finish()


def finish_ffn(meta, pieces, parts, k, shard, before, after=()):
    d, width = 2 * parts[0].shape[0], parts[0].shape[1]
    args = (meta, *parts, *before)
    return call(functools.partial(finish_ffn_kernel, pieces, k), "finish_ffn", args, "shhhh" + "h" * len(before),
                [("h", S((d, shard), F32)), ("h", S((shard, d), F32))],
                [VM((2, d, width), BF), VM((d, width), BF), VM((d, width), F32), VM((width, d), F32)], 8, 0, 4 * MIB,
                {5 + i: i for i in range(len(before))}, after)


def finish_pair_kernel(pieces, meta, m0, m1, t0, t1, *refs):
    outs, (both, wide, sems) = refs[:-3], refs[-3:]
    move = Mover(sems)
    me = meta[0]
    d = wide.shape[1]
    pairs = len(outs) // 2
    loads = [load_halves(move, m0, m1, t0, t1, slice(k * d, (k + 1) * d), both.at[k], me) for k in range(pairs)]
    step = d // pieces
    for k in range(pairs):
        for c in loads[k]:
            c.wait()
        for t in range(2):
            code = jnp.where(me == t, meta[2], meta[3])
            for p in range(pieces):
                wide[2 * k + t, p * step:(p + 1) * step, :] = placed(both.at[k, t], p, code, pieces).astype(F32)
            move.store(wide.at[2 * k + t], outs[2 * k + t])
    move.finish()


def finish_pair(meta, pieces, parts, d, after=()):
    pairs = parts[0].shape[1] // d
    return call(functools.partial(finish_pair_kernel, pieces), "finish_pair", (meta, *parts), "shhhh",
                [("h", S((d, d), F32))] * (2 * pairs), [VM((pairs, 2, d, d), BF), VM((2 * pairs, d, d), F32)], 4 + 6 * pairs, 0, 8 * MIB, None, after)


def bits_below(size):
    return [1 << i for i in range(size.bit_length() - 1)]


class Layout:
    def __init__(self, mesh):
        self.nb, self.nt = mesh.shape["batch"], mesh.shape["tp"]
        self.tp = [("tp", b) for b in reversed(bits_below(self.nt))]
        self.batch = [("batch", b) for b in bits_below(self.nb)[1:]]
        self.lanes = (self.tp + self.batch, self.batch[:1] + self.tp + self.batch[1:])

    def partner(self, device, level):
        b, t = divmod(device, self.nt)
        axis, bit = level
        return (b ^ bit) * self.nt + t if axis == "batch" else b * self.nt + (t ^ bit)

    def swap(self, value, level):
        pairs = []
        for device in range(self.nb * self.nt):
            core, to = device // self.nt % 2, device
            for one in level if isinstance(level, list) else [level]:
                to = self.partner(to, self.lanes[core][one] if isinstance(one, int) else one)
            pairs.append((device, to))
        return lax.ppermute(value, ("batch", "tp"), pairs)


CORE = ("batch", 1)


def code_of(levels, place):
    out = jnp.int32(0)
    for axis, bit in levels:
        out = out * 2 + (place[axis] // bit) % 2
    return out


def add(a, b):
    return (a.astype(F32) + b.astype(F32)).astype(BF)


def scatter_levels(levels, rows, least=48):
    n = 0
    while n < len(levels) and rows % 32 == 0 and rows // 2 >= least:
        rows //= 2
        n += 1
    return n


class Chain:
    def __init__(self, lay, steps):
        self.lay, self.steps, self.result = lay, steps, None
        self.go(next(steps))

    def go(self, requests):
        self.sent = [v for v, _ in requests]
        self.here = [self.lay.swap(v, level) for v, level in requests]

    def step(self):
        try:
            self.go(self.steps.send(self.here))
        except StopIteration as end:
            self.result, self.sent, self.here = end.value, [], []
        return self


def fence(arrays, *chains):
    chains = [c for c in chains if c.here]
    arrays, held = lax.optimization_barrier((arrays, [c.here for c in chains]))
    for chain, here in zip(chains, held):
        chain.here = here
        chain.step()
    return arrays


def sent(*chains):
    return tuple(v for c in chains for v in c.sent)


def halving(a, b, levels):
    for level in levels:
        n = a.shape[0] // 2
        kept = add(a[:n], b[:n])
        (b,) = yield [(add(a[n:], b[n:]), level)]
        a = kept
    return a, b


def quartering(a, b, high, low):
    n = a.shape[0] // 4
    parts = [add(a[i * n:(i + 1) * n], b[i * n:(i + 1) * n]) for i in range(4)]
    got = yield [(parts[1], [low]), (parts[2], [high]), (parts[3], [high, low])]
    return sum((g.astype(F32) for g in got), parts[0].astype(F32)).astype(BF)


def fourfold(held, high, low):
    got = yield [(held, [low]), (held, [high]), (held, [high, low])]
    return jnp.concatenate([held] + got, axis=0)


def doubling(held, levels):
    for level in levels:
        (got,) = yield [(held, level)]
        held = jnp.concatenate([held, got], axis=0)
    return held


def spread(held, level):
    other, mine = yield [(held, level), (held, CORE)]
    (rest,) = yield [(other, CORE)]
    return held, other, mine, rest


def reduce_ffn(lay, gone, stay, keep):
    m = len(lay.lanes[0])
    n = gone.shape[0]
    (recv,) = yield [(gone, CORE)]
    b, recv = yield [(add(keep[n:], recv), 0), (stay, CORE)]
    a, b = yield from halving(add(keep[:n], recv), b, range(1, m - 2))
    held = yield from quartering(a, b, m - 2, m - 1)
    held = yield from doubling(held, reversed(lay.batch[1:]))
    return (yield from spread(held, lay.batch[0]))


def reduce_pair(lay, n, send, keep, ahead):
    (recv,) = yield [(send, CORE)]
    if ahead:
        held = add(*(yield from halving(keep, recv, range(n))))
    else:
        a, b = yield from halving(keep, recv, range(n - 2))
        held = yield from quartering(a, b, n - 2, n - 1)
    for level in range(n, len(lay.lanes[0])):
        (got,) = yield [(held, level)]
        held = add(held, got)
    return held


def gather_pairs(lay, n, held):
    held = yield from fourfold(held, n - 2, n - 1)
    held = yield from doubling(held, reversed(range(1, n - 2)))
    return (yield from spread(held, 0))


def reduce_small(lay, vectors, hidden):
    n, shard = vectors.shape[0], hidden[0].shape[0]
    for level in lay.tp:
        bit = level[1]
        (got,) = yield [(jnp.concatenate([vectors] + [hidden[j + bit] for j in range(bit)]), level)]
        vectors = vectors + got[:n]
        hidden = [hidden[j] + got[n + j * shard:n + (j + 1) * shard] for j in range(bit)]
    held = jnp.concatenate([vectors, hidden[0]])
    for level in [CORE] + lay.batch[:-2]:
        (got,) = yield [(held, level)]
        held = held + got
    high, low = lay.batch[-2:]
    got = yield [(held, [low]), (held, [high]), (held, [high, low])]
    return held + got[0] + got[1] + got[2]


def on_device(
    lay,
    inputs,
    cotangent,
    zinc_lengths,
    pubchem_lengths,
    feature_stack,
    train_step,
    redraw_interval,
    attn_gain,
    attn_shift,
    query_weight,
    query_bias,
    key_weight,
    key_bias,
    value_weight,
    value_bias,
    output_weight,
    output_bias,
    ffn_gain,
    ffn_shift,
    hidden_weight,
    hidden_bias,
    return_weight,
    return_bias,
):
    nt = lay.nt
    d, shard = hidden_weight.shape
    rows = inputs.shape[0]
    width = min(768, shard)
    chunks = shard // width
    zm, pm = zinc_lengths.shape[0], pubchem_lengths.shape[0]
    place = {"batch": lax.axis_index("batch"), "tp": lax.axis_index("tp")}
    core = place["batch"] % 2

    def shares(k):
        hw = lax.dynamic_slice(hidden_weight, (core * (d // 2), k * width), (d // 2, width))
        rw = lax.dynamic_slice(return_weight, (k * width + core * (width // 2), 0), (width // 2, d))
        return [jnp.concatenate([hw, rw], axis=0)] if width == d else [hw, rw]

    def from_tp(own):
        pool = {0: own}
        for level in lay.tp:
            for j in list(pool):
                pool[j | level[1]] = [lay.swap(v, level) for v in pool[j]]
        return [v for j in range(1, nt) for v in pool[j]]

    own = [shares(k) for k in range(chunks)]
    per = len(own[0])
    biases = from_tp([hidden_bias])
    here = {k: from_tp(own[k]) for k in range(chunks)}

    n_pair = scatter_levels(lay.lanes[0], d)
    codes = [code_of(lane[:n_pair], place) for lane in lay.lanes]
    pick = train_step[0] // redraw_interval[0] % feature_stack.shape[0]
    meta = jnp.stack([core, code_of(lay.batch, place), jnp.where(core == 0, codes[0], codes[1]), jnp.where(core == 0, codes[1], codes[0]),
                      code_of(lay.batch[:-2], place) * 4, pick]).astype(jnp.int32)
    table = rotary_const()

    out = attend_fwd(
        meta, zinc_lengths, pubchem_lengths, cotangent, inputs,
        (attn_gain, attn_shift, query_bias, key_bias, value_bias, output_bias, ffn_gain, ffn_shift),
        query_weight, key_weight, value_weight, output_weight, feature_stack, table)
    out, here[0], biases = lax.optimization_barrier((out, here[0], biases))
    qkv, f, state, trans, middle, n2, left, proj = out

    pieces, pair_pieces = 2 ** len(lay.batch), 2 ** n_pair
    chains, acts, rws, hidden, before = [], [], [], [], ()
    for k in range(chunks):
        if chains:
            here[k] = fence(here[k], chains[-1])
        near = [lay.swap(v, CORE) for v in here[k]]
        parts = [[v[i] for i in range(j * per, (j + 1) * per) for v in (here[k], near)] for j in range(nt - 1)]
        out = ffn_chunk(meta, pieces, nt, n2, left, cotangent, hidden_bias, hidden_weight, return_weight, parts, biases, k, width,
                        before, sent(*chains))
        gone, stay, keep, act, bias, e, rw = fence(out, *chains)
        before = (e,)
        chains.append(Chain(lay, reduce_ffn(lay, gone, stay, keep)))
        acts.append(act)
        rws.append(rw)
        hidden.append(bias)

    middle = fence(middle, chains[-1])
    out = mid(e, cotangent, middle, output_weight, ffn_gain, sent(*chains))
    gm, gb, gatt, vec1 = fence(out, *chains[:-1])
    out = value_bwd(meta, zm, pm, pair_pieces, gatt, gb, f, state, trans, sent(*chains))
    send, keep, gv, uw, gst, vec2 = fence(out, *chains)
    pair_a = Chain(lay, reduce_pair(lay, n_pair, send, keep, True))
    uw = fence(uw, pair_a)
    out = query_bwd(meta, zm, pm, pair_pieces, uw, gst, qkv, f, state, trans, proj, table, sent(pair_a, *chains))
    send, keep, gqk, vec3 = fence(out, pair_a, *chains)
    pair_b = Chain(lay, reduce_pair(lay, n_pair, send, keep, False))
    gqk = fence(gqk, pair_b)
    out = input_back(gqk, gv, query_weight, key_weight, value_weight, inputs, gm, attn_gain, sent(pair_a, pair_b, *chains))
    (input_grad, vec4), middle = fence((out, middle), pair_a, pair_b, *chains)
    layer_out = layer_end(acts, rws, middle, return_bias, sent(pair_b, pair_a, *chains))
    layer_out, vec4 = fence((layer_out, vec4), pair_b, pair_a, *chains)
    vec3 = jnp.concatenate([vec3, vec4], axis=0)
    vectors = jnp.concatenate([vec1, vec2, vec3], axis=0).reshape(-1)
    small = Chain(lay, reduce_small(lay, vectors, [jnp.concatenate([hidden[k][j] for k in range(chunks)]) for j in range(nt)]))

    ffn_out, k, pairs = (), 0, None
    while pairs is None or pairs.here or any(c.here for c in chains):
        every = [pairs] if pairs else [pair_b, pair_a]
        every += chains + [small]
        if k < chunks and chains[k].result is not None:
            ffn_out = finish_ffn(meta, pieces, chains[k].result, k, shard, ffn_out, sent(*every))
            k += 1
            ffn_out = fence(ffn_out, *every)
        else:
            fence((), *every)
        if pairs is None and pair_a.result is not None and pair_b.result is not None:
            pairs = Chain(lay, gather_pairs(lay, n_pair, jnp.concatenate([pair_a.result, pair_b.result], axis=1)))
    while k < chunks:
        ffn_out = finish_ffn(meta, pieces, chains[k].result, k, shard, ffn_out, sent(small))
        k += 1
    while small.here:
        small.step()
    gwo, gwv, gwq, gwk = finish_pair(meta, pair_pieces, pairs.result, d, (small.result,))
    vecs = small.result[:9 * d].reshape(9, d)
    return (layer_out, input_grad, vecs[7], vecs[8], gwq, vecs[5], gwk, vecs[6], gwv, vecs[4], gwo, vecs[2],
            vecs[0], vecs[1], ffn_out[0], small.result[9 * d:], ffn_out[1], vecs[3])


def solution(mesh):
    rows, whole, hidden = P(("batch", "tp"), None), P(), P(None, "tp")
    return jax.shard_map(
        functools.partial(on_device, Layout(mesh)),
        mesh=mesh,
        in_specs=(rows, rows, P(("batch", "tp")), P(("batch", "tp"))) + (whole,) * 15 + (hidden, P("tp"), P("tp", None), whole),
        out_specs=(rows, rows) + (whole,) * 12 + (hidden, P("tp"), P("tp", None), whole),
        check_vma=False,
    )
```
